256 devices in a mesh: dp: 128 (over z, y, x), ctx: 2 (over core).
Axes of the slice: x: 4, y: 4, z: 8, core: 2. Of those that a mesh axis runs over, the one named last changes fastest.
Arguments:
- queries: bfloat16 [128, 512, 2048], P('dp', 'ctx'), may hold values from -24 to 24
- keys: bfloat16 [128, 512, 2048], P('dp', 'ctx'), may hold values from -24 to 24
- values: bfloat16 [128, 512, 2048], P('dp', 'ctx'), may hold values from -6 to 6
- residual: bfloat16 [128, 512, 2048], P('dp', 'ctx'), may hold values from -6 to 6
- grad_out: bfloat16 [128, 512, 2048], P('dp', 'ctx'), may hold values from -6 to 6
- latents: bfloat16 [128, 2, 32, 128], P('dp', 'ctx'), may hold values from -6 to 6
- image_starts: int32 [128, 2], P('dp'), may hold values from 0 to 384, as said below
- w_first: bfloat16 [32, 512], replicated, may hold values from -1 to 1
- w_second: bfloat16 [512, 2048], replicated, may hold values from -0.25 to 0.25
Outputs:
- layer_out: bfloat16 [128, 512, 2048], P('dp', 'ctx')
- grad_queries: bfloat16 [128, 512, 2048], P('dp', 'ctx')
- grad_keys: bfloat16 [128, 512, 2048], P('dp', 'ctx')
- grad_values: bfloat16 [128, 512, 2048], P('dp', 'ctx')
- grad_w_first: float32 [32, 512], replicated
- grad_w_second: float32 [512, 2048], P(None, 'ctx')
The draws below stay inside these ranges and needn't reach their ends.
Inputs may be any that keep to these rules, and one draw needn't show every extreme that they name: `image_starts`: within a document the spans of 128 positions that start at these offsets never intersect; one span starts at 0 and one ends at 512; entry i belongs to the image held as latents[:, i].
All inputs are finite; a program needn't handle non-finite values.
Results may differ from the reference program's by a relative error of at most 0.011.
Values may be sent and summed in bfloat16 or wider, within the bound.
No kernel may reach another device: no remote copies, remote signals or barrier semaphores. Data moves between devices by JAX's collectives and lax.ppermute only.
A program may use at most 128 MiB of HBM per device.

```python
import jax
import jax.numpy as jnp
from jax import lax

HEADS = 16
HEAD_DIM = 128
PATCH_DIM = 32
UNET_CH = 512
IMG_TOK = 128
WIDTH = 2048
SEQ = 512
IMAGES = 2
DOCS = 128


def draw_queries(key, part):
    key = jax.random.fold_in(key, 11)
    result = jnp.clip(jax.random.normal(key, (DOCS, SEQ, HEADS * HEAD_DIM), jnp.float32), -4.0, 4.0)
    return result.astype(jnp.bfloat16)


def draw_keys(key, part):
    key = jax.random.fold_in(key, 12)
    result = jnp.clip(jax.random.normal(key, (DOCS, SEQ, HEADS * HEAD_DIM), jnp.float32), -4.0, 4.0)
    return result.astype(jnp.bfloat16)


def pick_order(order_seed):
    return jax.random.permutation(order_seed, IMAGES)


def draw_image_starts(key, part):
    key = jax.random.fold_in(key, 5)
    cut_key, order_key = jax.random.split(key)
    text_len = SEQ - IMAGES * IMG_TOK
    cuts = jax.random.randint(cut_key, (DOCS, IMAGES), 0, text_len + 1)
    cuts = cuts.at[:, 0].set(0).at[:, IMAGES - 1].set(text_len)
    cuts = jnp.sort(cuts, axis=1)
    ordered = cuts + jnp.arange(IMAGES, dtype=jnp.int32)[None, :] * IMG_TOK
    order = jax.vmap(pick_order)(jax.random.split(order_key, DOCS))
    return jnp.take_along_axis(ordered, order, axis=1).astype(jnp.int32)


def block_scale(key, shape, shards, smallest, top_value):
    def one(position, shards_of):
        heights = jax.random.uniform(jax.random.fold_in(jax.random.fold_in(key, 6), position), (shards_of,), jnp.float32, smallest / len(shards), top_value / len(shards))
        return jnp.repeat(jnp.exp(heights), shape[position] // shards_of).reshape((-1,) + (1,) * (len(shape) - position - 1))

    gain = one(*shards[0])
    for cut in shards[1:]:
        gain = gain * one(*cut)
    return gain


def centred(rng, shape, deviation, bound, cuts=(), kind=jnp.bfloat16):
    values = jax.random.normal(rng, shape, jnp.float32) * deviation
    if len(cuts) > 0:
        values = block_scale(rng, shape, cuts, -0.22, 0.18) * values
    return jnp.clip(values, min=-bound, max=bound).astype(kind)


def setup_inputs(seed: int = 0) -> dict:
    key_of = jax.random.split(jax.random.key(seed), 10)
    queries = draw_queries(jax.random.fold_in(key_of[9], 71), 0)
    keys = draw_keys(jax.random.fold_in(key_of[9], 71), 0)
    values = centred(key_of[2], (DOCS, SEQ, WIDTH), 1.0, 6.0, ((0, 128), (1, 2)))
    residual = centred(key_of[3], (DOCS, SEQ, WIDTH), 1.0, 6.0, ((0, 128), (1, 2)))
    grad_out = centred(key_of[4], (DOCS, SEQ, WIDTH), 1.0, 6.0, ((0, 128), (1, 2)))
    latents = centred(key_of[5], (DOCS, IMAGES, PATCH_DIM, IMG_TOK), 1.0, 6.0, ((0, 128), (1, 2)))
    image_starts = draw_image_starts(jax.random.fold_in(key_of[9], 71), 0)
    w_first = centred(key_of[7], (PATCH_DIM, UNET_CH), PATCH_DIM ** -0.5, 1.0)
    w_second = centred(key_of[8], (UNET_CH, WIDTH), UNET_CH ** -0.5, 0.25)
    return {"queries": queries, "keys": keys, "values": values, "residual": residual, "grad_out": grad_out, "latents": latents, "image_starts": image_starts, "w_first": w_first, "w_second": w_second}


def locate(positions, span_starts, span_len):
    inside = (positions[:, None] >= span_starts[None, :]) & (positions[:, None] < span_starts[None, :] + span_len)
    hit_table = inside.astype(jnp.int32)
    is_image = jnp.sum(hit_table, axis=1) > 0
    slot_ids = jnp.arange(span_starts.shape[0], dtype=jnp.int32)
    image_id = jnp.where(is_image, jnp.sum(hit_table * slot_ids[None, :], axis=1), -1).astype(jnp.int32)
    offset = positions - jnp.sum(hit_table * span_starts[None, :], axis=1)
    slot_index = jnp.where(is_image, image_id * span_len + offset, 0).astype(jnp.int32)
    return image_id, is_image, slot_index


def allowed(query_pos, query_img, key_pos, key_img):
    causal = key_pos[None, :] <= query_pos[:, None]
    same_image = (query_img[:, None] == key_img[None, :]) & (query_img[:, None] >= 0)
    return causal | same_image


def encode(patch_rows, w_first, w_second):
    pre_act = jnp.dot(patch_rows, w_first, preferred_element_type=jnp.float32)
    hidden = jax.nn.silu(pre_act).astype(jnp.bfloat16)
    embedding = jnp.dot(hidden, w_second, preferred_element_type=jnp.float32).astype(jnp.bfloat16)
    return pre_act, hidden, embedding


def encode_grads(patch_rows, pre_act, hidden, grad_embed, w_second):
    back_hidden = lax.dot_general(grad_embed, w_second, (((1,), (1,)), ((), ())), preferred_element_type=jnp.float32)
    gate_sig = jax.nn.sigmoid(pre_act)
    grad_pre = (back_hidden * gate_sig * (1.0 + pre_act * (1.0 - gate_sig))).astype(jnp.bfloat16)
    grad_second = lax.dot_general(hidden, grad_embed, (((0,), (0,)), ((), ())), preferred_element_type=jnp.float32)
    grad_first = lax.dot_general(patch_rows, grad_pre, (((0,), (0,)), ((), ())), preferred_element_type=jnp.float32)
    return grad_first, grad_second


def rounded(array):
    return lax.optimization_barrier(array.astype(jnp.bfloat16)).astype(jnp.float32)


def reference(queries, keys, values, residual, grad_out, latents, image_starts, w_first, w_second):
    seq_len = queries.shape[1]
    model_width = queries.shape[2]
    score_scale = HEAD_DIM ** -0.5
    every_pos = jnp.arange(seq_len, dtype=jnp.int32)
    offsets = jnp.arange(IMG_TOK, dtype=jnp.int32)

    def one_doc(doc_item):
        query_doc, key_doc, value_doc, resid_doc, grad_doc, latent_doc, span_starts = doc_item
        image_id, is_image, slot_index = locate(every_pos, span_starts, IMG_TOK)
        patch_table = jnp.transpose(latent_doc, (0, 2, 1)).reshape(IMAGES * IMG_TOK, PATCH_DIM)
        pre_act, hidden, embedding = encode(patch_table, w_first, w_second)
        mixed = jnp.where(is_image[:, None], embedding[slot_index], resid_doc)
        visible = allowed(every_pos, image_id, every_pos, image_id)[None]
        query_heads = query_doc.reshape(seq_len, HEADS, HEAD_DIM).astype(jnp.float32)
        key_heads = key_doc.reshape(seq_len, HEADS, HEAD_DIM).astype(jnp.float32)
        value_heads = value_doc.reshape(seq_len, HEADS, HEAD_DIM).astype(jnp.float32)
        grad_heads = grad_doc.reshape(seq_len, HEADS, HEAD_DIM).astype(jnp.float32)
        scores = jnp.einsum("thd,shd->hts", query_heads, key_heads) * score_scale
        scores = jnp.where(visible, scores, -1e30)
        row_max = jnp.max(scores, axis=2, keepdims=True)
        weights = jnp.where(visible, jnp.exp(scores - row_max), 0.0)
        totals = jnp.sum(weights, axis=2, keepdims=True)
        probs = rounded(weights / totals)
        attended = jnp.einsum("hts,shd->thd", probs, value_heads)
        layer_doc = (mixed.astype(jnp.float32) + attended.reshape(seq_len, model_width)).astype(jnp.bfloat16)
        log_total = row_max + jnp.log(totals)
        out_dot = jnp.sum(grad_heads * attended, axis=2)
        back_probs = jnp.where(visible, jnp.exp(scores - log_total), 0.0)
        grad_probs = jnp.einsum("thd,shd->hts", grad_heads, value_heads)
        grad_scores = rounded(back_probs * (grad_probs - jnp.transpose(out_dot)[:, :, None]))
        grad_q = (jnp.einsum("hts,shd->thd", grad_scores, key_heads) * score_scale).astype(jnp.bfloat16)
        grad_k = (jnp.einsum("hts,thd->shd", grad_scores, query_heads) * score_scale).astype(jnp.bfloat16)
        grad_v = jnp.einsum("hts,thd->shd", rounded(back_probs), grad_heads).astype(jnp.bfloat16)
        span_pos = (span_starts[:, None] + offsets[None, :]).reshape(-1)
        grad_embed = grad_doc[span_pos]
        grad_first, grad_second = encode_grads(patch_table, pre_act, hidden, grad_embed, w_second)
        return (layer_doc, grad_q.reshape(seq_len, model_width), grad_k.reshape(seq_len, model_width),
                grad_v.reshape(seq_len, model_width), grad_first, grad_second)

    results = lax.map(one_doc, (queries, keys, values, residual, grad_out, latents, image_starts))
    doc_count = queries.shape[0]
    return (results[0], results[1], results[2], results[3],
            jnp.sum(results[4], axis=0) / doc_count, jnp.sum(results[5], axis=0) / doc_count)
```

```python
import math

import jax
import jax.numpy as jnp
from jax import lax
from jax.experimental import pallas as pl
from jax.experimental.pallas import tpu as pltpu
from jax.sharding import Mesh
from jax.sharding import PartitionSpec as P

HEAD = 128
SPAN = 128
ROWS = 256
HALF = 1024
WIDTH = 2048
SEQ = 512
CH = 512
HEADS = 8
GROUP = 2
SHARDS = 128
VMEM = 56 * 1024 * 1024

F32 = jnp.float32
BF16 = jnp.bfloat16


def dot(a, b, ca, cb):
    return lax.dot_general(a, b, (((ca,), (cb,)), ((), ())), preferred_element_type=F32)


def whole(shape):
    return pl.BlockSpec(shape, lambda *_: (0,) * len(shape))


def call(body, meta, args, in_specs, out_specs, out_shape, grid=(1,), scratch=(), aliases=None):
    return pl.pallas_call(
        body,
        grid_spec=pltpu.PrefetchScalarGridSpec(
            num_scalar_prefetch=1,
            grid=grid,
            in_specs=in_specs,
            out_specs=out_specs,
            scratch_shapes=scratch,
        ),
        out_shape=out_shape,
        input_output_aliases=aliases or {},
        compiler_params=pltpu.CompilerParams(vmem_limit_bytes=VMEM),
    )(meta, *args)


def sigmoid(v):
    return 1.0 / (1.0 + jnp.exp(-v))


def eye(n):
    rows = lax.broadcasted_iota(jnp.int32, (n, n), 0)
    cols = lax.broadcasted_iota(jnp.int32, (n, n), 1)
    return (rows == cols).astype(F32).astype(BF16)


def weight_body(meta, lat, w1, w2, g_own, g_oth, out, hid_t, first):
    step = pl.program_id(0)

    @pl.when(step == 0)
    def _():
        patches = jnp.concatenate([lat[0], lat[1]], axis=1)
        pre = dot(w1[...], patches, 0, 0)
        sig = sigmoid(pre)
        hid_t[...] = (pre * sig).astype(BF16)
        grads = jnp.concatenate([g_own[...], g_oth[...]], axis=0)
        back = dot(w2[...], grads, 1, 1)
        grad_pre = (back * sig * (1.0 + pre * (1.0 - sig))).astype(BF16)
        first[...] = dot(patches, grad_pre, 1, 1)

    half = pl.ds(pl.multiple_of(meta[0] * HALF, HALF), HALF)
    grads = jnp.concatenate([g_own[:, half], g_oth[:, half]], axis=0)
    strip = dot(hid_t[pl.ds(pl.multiple_of(step * 128, 128), 128), :], grads, 1, 0)
    rows = first[pl.ds(pl.multiple_of(step * 8, 8), 8), :]
    for i in range(8):
        for m in range(4):
            line = strip[16 * i : 16 * i + 16]
            out[4 * i + m, 0:16] = line[:, 256 * m : 256 * m + 128]
            out[4 * i + m, 16:32] = line[:, 256 * m + 128 : 256 * m + 256]
            out[4 * i + m, 32:40] = rows[:, 128 * m : 128 * m + 128]


def finish_body(meta, got, second, first):
    for i in range(8):
        for m in range(4):
            j = 4 * i + m
            second[16 * i : 16 * i + 16, 256 * m : 256 * m + 128] = got[j, 0:16].astype(F32) * (1.0 / 128.0)
            second[16 * i : 16 * i + 16, 256 * m + 128 : 256 * m + 256] = got[j, 16:32].astype(F32) * (1.0 / 128.0)
    for m in range(4):
        first[:, 128 * m : 128 * m + 128] = got[m, 32:48].astype(F32)[0:8] * (1.0 / 128.0)


def one_head(q, k, v, g, unit, unit_wide):
    scale = HEAD ** -0.5
    power = scale * math.log2(math.e)
    k_t = dot(unit, k, 1, 1).astype(BF16)
    v_t = dot(unit, v, 1, 1).astype(BF16)
    att, dq, dk, dv = [], [], [], []
    for b in range(2):
        seen = ROWS * (b + 1)
        qb = q[ROWS * b : ROWS * b + ROWS]
        gb = g[ROWS * b : ROWS * b + ROWS]
        scores = dot(k[0:seen], qb, 1, 1)
        key_pos = lax.broadcasted_iota(jnp.int32, (ROWS, ROWS), 0)
        query_pos = lax.broadcasted_iota(jnp.int32, (ROWS, ROWS), 1)
        if b == 0:
            limit = jnp.where(query_pos < SPAN, SPAN - 1, query_pos)
        else:
            limit = jnp.where(query_pos < SPAN, query_pos, ROWS - 1)
        last = jnp.where(key_pos <= limit, scores[seen - ROWS : seen], -1e30)
        scores = last if b == 0 else jnp.concatenate([scores[0:ROWS], last], axis=0)
        top = jnp.max(scores, axis=0, keepdims=True)
        e = jnp.exp2((scores - top) * power)
        p = e * (1.0 / jnp.sum(e, axis=0, keepdims=True))
        pb = p.astype(BF16)
        att_t = dot(v_t[:, 0:seen], pb, 1, 0).astype(BF16)
        att.append(dot(unit_wide, att_t, 1, 1))
        u = p * dot(v[0:seen], gb, 1, 1)
        ds = (u - p * jnp.sum(u, axis=0, keepdims=True)).astype(BF16)
        dq_t = (dot(k_t[:, 0:seen], ds, 1, 0) * scale).astype(BF16)
        dq.append(dot(unit_wide, dq_t, 1, 1).astype(BF16))
        dk.append(dot(ds, qb, 1, 0))
        dv.append(dot(pb, gb, 1, 0))
    dk = [((dk[0] + dk[1][0:ROWS]) * scale).astype(BF16), (dk[1][ROWS:SEQ] * scale).astype(BF16)]
    dv = [(dv[0] + dv[1][0:ROWS]).astype(BF16), dv[1][ROWS:SEQ].astype(BF16)]
    return att, dq, dk, dv


def hidden_of(lat, w1):
    pre = dot(lat, w1, 0, 0)
    return (pre * sigmoid(pre)).astype(BF16)


def attention_body(meta, q_own, q_oth, k_own, k_oth, v_own, v_oth, g_own, g_img, g_txt, text, lat, w1, w2,
                   lay_out, dq_out, dk_out, dv_out, att_send, dq_send, dk_send, dv_send,
                   q, k, v, g, att, dq, dk, dv, hid):
    ctx = meta[0]
    own = pl.multiple_of(ctx * ROWS, ROWS)
    oth = pl.multiple_of(ROWS - ctx * ROWS, ROWS)

    @pl.when(pl.program_id(0) == 0)
    def _():
        hid[...] = hidden_of(lat[0], w1[...])

    for full, a, b in ((q, q_own, q_oth), (k, k_own, k_oth), (v, v_own, v_oth)):
        full[pl.ds(own, ROWS), :] = a[...]
        full[pl.ds(oth, ROWS), :] = b[...]
    g[pl.ds(own, ROWS), :] = g_own[...]
    g[pl.ds(pl.multiple_of(oth + SPAN - ctx * SPAN, SPAN), SPAN), :] = g_img[...]
    g[pl.ds(pl.multiple_of(oth + ctx * SPAN, SPAN), SPAN), :] = g_txt[...]
    unit = eye(HEAD)
    unit_wide = eye(ROWS)
    for h in range(GROUP):
        cols = slice(HEAD * h, HEAD * h + HEAD)
        parts = one_head(q[:, cols], k[:, cols], v[:, cols], g[:, cols], unit, unit_wide)
        for full, halves in zip((att, dq, dk, dv), parts):
            full[0:ROWS, cols] = halves[0].astype(BF16)
            full[ROWS:SEQ, cols] = halves[1].astype(BF16)
    mine = pl.ds(own, ROWS)
    theirs = pl.ds(oth, ROWS)
    for full, keep, send in ((dq, dq_out, dq_send), (dk, dk_out, dk_send), (dv, dv_out, dv_send)):
        keep[...] = full[mine, :]
        send[...] = full[theirs, :]
    att_send[...] = att[theirs, :]
    add_residual(ctx, lay_out, att[mine, :], hid[...], w2[...], text[...])


def add_residual(ctx, lay_out, att, hid, w2, text):
    lay_out[...] = att
    image_rows = pl.ds(pl.multiple_of(ctx * SPAN, SPAN), SPAN)
    text_rows = pl.ds(pl.multiple_of(SPAN - ctx * SPAN, SPAN), SPAN)
    embedding = dot(hid, w2, 1, 0).astype(BF16).astype(F32)
    lay_out[image_rows, :] = (embedding + lay_out[image_rows, :].astype(F32)).astype(BF16)
    lay_out[text_rows, :] = (text.astype(F32) + lay_out[text_rows, :].astype(F32)).astype(BF16)


def merge_body(meta, text, lat, w1, w2, att, dq, dk, dv, lay_in, dq_in, dk_in, dv_in, lay_out, dq_out, dk_out, dv_out):
    add_residual(meta[0], lay_out, att[...], hidden_of(lat[0], w1[...]), w2[...], text[...])
    dq_out[...] = dq[...]
    dk_out[...] = dk[...]
    dv_out[...] = dv[...]


def local(queries, keys, values, residual, grad_out, latents, image_starts, w_first, w_second):
    ctx = lax.axis_index("ctx").astype(jnp.int32)
    meta = ctx[None]
    swap = [(0, 1), (1, 0)]

    def swapped(value):
        return lax.ppermute(value, "ctx", swap)

    def their_half(value):
        return lax.dynamic_slice_in_dim(value[0], (1 - ctx) * HALF, HALF, 1)

    q_rows, k_rows, v_rows, g_rows, r_rows = queries[0], keys[0], values[0], grad_out[0], residual[0]
    lat_own = latents[0, 0]
    lat_oth = swapped(lat_own)
    g_img = swapped(lax.dynamic_slice_in_dim(g_rows, ctx * SPAN, SPAN, 0))
    g_txt = swapped(lax.dynamic_slice(g_rows, ((1 - ctx) * SPAN, (1 - ctx) * HALF), (SPAN, HALF)))
    k_oth = swapped(their_half(keys))
    q_oth = swapped(their_half(queries))
    v_oth = swapped(their_half(values))
    in_order = image_starts[0, 0] == 0
    lat = jnp.where(in_order, jnp.stack([lat_own, lat_oth]), jnp.stack([lat_oth, lat_own]))

    struct = jax.ShapeDtypeStruct
    image_spec = pl.BlockSpec((SPAN, WIDTH), lambda i, m: (m[0], 0))
    payload = call(
        weight_body, meta, (lat, w_first, w_second, g_rows, g_img),
        [whole((2, 32, SPAN)), whole((32, CH)), whole((CH, WIDTH)), image_spec, whole((SPAN, WIDTH))],
        pl.BlockSpec((32, 40, 128), lambda i, m: (i, 0, 0)), struct((SHARDS, 40, 128), F32), grid=(4,),
        scratch=[pltpu.VMEM((CH, 2 * SPAN), BF16), pltpu.VMEM((32, CH), F32)],
    )
    dp = ("z", "y", "x")
    shard = lax.psum_scatter(payload, dp, scatter_dimension=0, tiled=False)

    cols = GROUP * HEAD
    steps = HEADS // GROUP
    own_spec = pl.BlockSpec((ROWS, cols), lambda i, m: (0, m[0] * steps + i))
    oth_spec = pl.BlockSpec((ROWS, cols), lambda i, m: (0, i))
    big = struct((ROWS, WIDTH), BF16)
    small = struct((ROWS, HALF), BF16)
    result = call(
        attention_body, meta,
        (q_rows, q_oth, k_rows, k_oth, v_rows, v_oth, g_rows, g_img, g_txt, r_rows, lat, w_first, w_second),
        [own_spec, oth_spec] * 3
        + [own_spec, pl.BlockSpec((SPAN, cols), lambda i, m: (0, m[0] * steps + i)),
           pl.BlockSpec((SPAN, cols), lambda i, m: (0, i)),
           pl.BlockSpec((SPAN, cols), lambda i, m: (1 - m[0], m[0] * steps + i)),
           whole((2, 32, SPAN)), whole((32, CH)), pl.BlockSpec((CH, cols), lambda i, m: (0, m[0] * steps + i))],
        [own_spec] * 4 + [oth_spec] * 4,
        [big] * 4 + [small] * 4,
        grid=(steps,),
        scratch=[pltpu.VMEM((SEQ, cols), BF16)] * 8 + [pltpu.VMEM((SPAN, CH), BF16)],
    )
    shard, *result = lax.optimization_barrier((shard, *result))
    shard = jnp.pad(shard, ((0, 8), (0, 0))).astype(BF16)
    got = lax.all_gather(shard, dp)
    sum_second, sum_first = call(
        finish_body, meta, (got,), [pl.BlockSpec((32, 48, 128), lambda i, m: (i, 0, 0))],
        [pl.BlockSpec((128, HALF), lambda i, m: (i, 0)), pl.BlockSpec((8, CH), lambda i, m: (i, 0))],
        [struct((CH, HALF), F32), struct((32, CH), F32)], grid=(4,),
    )

    sent = [swapped(value) for value in result[4:]]
    half_spec = pl.BlockSpec((ROWS, HALF), lambda i, m: (0, 1 - m[0]))
    outs = call(
        merge_body, meta, (r_rows, lat, w_first, w_second, *sent, *result[:4]),
        [pl.BlockSpec((SPAN, HALF), lambda i, m: (1 - m[0], 1 - m[0])), whole((2, 32, SPAN)), whole((32, CH)),
         pl.BlockSpec((CH, HALF), lambda i, m: (0, 1 - m[0]))]
        + [whole((ROWS, HALF))] * 4 + [pl.BlockSpec(memory_space=pl.ANY)] * 4,
        [half_spec] * 4, [big] * 4, aliases={9 + i: i for i in range(4)},
    )
    return (*[value[None] for value in outs], sum_first, sum_second)


def solution(mesh):
    axes = Mesh(mesh.devices.reshape(8, 4, 4, 2), ("z", "y", "x", "ctx"))
    dp = ("z", "y", "x")
    rows = P(dp, "ctx", None)
    return jax.shard_map(
        local,
        mesh=axes,
        in_specs=(rows, rows, rows, rows, rows, P(dp, "ctx", None, None), P(dp, None), P(), P()),
        out_specs=(rows, rows, rows, rows, P(), P(None, "ctx")),
        check_vma=False,
    )
```

```python
import math

import jax
import jax.numpy as jnp
from jax import lax
from jax.experimental import pallas as pl
from jax.experimental.pallas import tpu as pltpu
from jax.sharding import Mesh
from jax.sharding import PartitionSpec as P

HEAD = 128
SPAN = 128
ROWS = 256
HALF = 1024
WIDTH = 2048
SEQ = 512
CH = 512
HEADS = 8
GROUP = 4
VMEM = 56 * 1024 * 1024

F32 = jnp.float32
BF16 = jnp.bfloat16


def dot(a, b, ca, cb):
    return lax.dot_general(a, b, (((ca,), (cb,)), ((), ())), preferred_element_type=F32)


def whole(shape):
    return pl.BlockSpec(shape, lambda *_: (0,) * len(shape))


def call(body, scalars, args, in_specs, out_specs, out_shape, grid=(1,), scratch=(), aliases=None):
    return pl.pallas_call(
        body,
        grid_spec=pltpu.PrefetchScalarGridSpec(
            num_scalar_prefetch=len(scalars),
            grid=grid,
            in_specs=in_specs,
            out_specs=out_specs,
            scratch_shapes=scratch,
        ),
        out_shape=out_shape,
        input_output_aliases=aliases or {},
        compiler_params=pltpu.CompilerParams(vmem_limit_bytes=VMEM),
    )(*scalars, *args)


def sigmoid(v):
    return 1.0 / (1.0 + jnp.exp(-v))


def eye(n):
    rows = lax.broadcasted_iota(jnp.int32, (n, n), 0)
    cols = lax.broadcasted_iota(jnp.int32, (n, n), 1)
    return (rows == cols).astype(F32).astype(BF16)


def pick(starts, lat_own, lat_oth):
    in_order = starts[0] == 0
    one, two = lat_own[...].astype(F32), lat_oth[...].astype(F32)
    return jnp.where(in_order, one, two).astype(BF16), jnp.where(in_order, two, one).astype(BF16)


def weight_body(ctx_ref, starts, lat_own, lat_oth, w1, w2_hbm, g_own, g_oth, out, w2, grads, sems):
    ctx = ctx_ref[0]
    own_rows = pl.ds(pl.multiple_of(ctx * SPAN, SPAN), SPAN)
    oth_rows = pl.ds(pl.multiple_of(SPAN - ctx * SPAN, SPAN), SPAN)
    copies = [
        pltpu.make_async_copy(g_own.at[own_rows, :], grads.at[0:SPAN, :], sems.at[0]),
        pltpu.make_async_copy(g_oth.at[oth_rows, :], grads.at[SPAN:ROWS, :], sems.at[1]),
        pltpu.make_async_copy(w2_hbm, w2, sems.at[2]),
    ]
    for copy in copies:
        copy.start()
    patches = jnp.concatenate(pick(starts, lat_own, lat_oth), axis=1)
    pre = dot(w1[...], patches, 0, 0)
    sig = sigmoid(pre)
    hid_t = (pre * sig).astype(BF16)
    copies[0].wait()
    copies[1].wait()
    half = grads[:, pl.ds(pl.multiple_of(ctx * HALF, HALF), HALF)]
    for j in range(16):
        strip = dot(hid_t[32 * j : 32 * j + 32], half, 1, 0).astype(BF16)
        for t in range(16):
            out[j, t] = strip[16 * (t // 8) : 16 * (t // 8) + 16, 128 * (t % 8) : 128 * (t % 8) + 128]
    copies[2].wait()
    back = dot(w2[...], grads[...], 1, 1)
    grad_pre = (back * sig * (1.0 + pre * (1.0 - sig))).astype(BF16)
    first = dot(patches, grad_pre, 1, 1)
    zeros = jnp.zeros((8, 128), F32)
    for j in range(16):
        tile = first[8 * (j // 4) : 8 * (j // 4) + 8, 128 * (j % 4) : 128 * (j % 4) + 128]
        out[j, 16] = jnp.concatenate([tile, zeros], axis=0).astype(BF16)


def depth_sum_body(got, low, high):
    total = got[0].astype(F32)
    for z in range(1, 8):
        total = total + got[z].astype(F32)
    low[...] = total[0:8].astype(BF16)
    high[...] = total[8:17].astype(BF16)


def finish_body(low, high, second, first):
    for j in range(4):
        for t in range(8):
            cols = slice(128 * t, 128 * t + 128)
            second[32 * j : 32 * j + 16, cols] = low[j, t].astype(F32) * (1.0 / 128.0)
            second[32 * j + 16 : 32 * j + 32, cols] = high[j, t].astype(F32) * (1.0 / 128.0)
        first[:, 128 * j : 128 * j + 128] = high[j, 8].astype(F32)[0:8] * (1.0 / 128.0)


def chain(q, k, v, g, att, dq, dk, dv, cols, b, unit, shared):
    scale = HEAD ** -0.5
    power = scale * math.log2(math.e)
    seen = ROWS * (b + 1)
    rows = slice(ROWS * b, ROWS * b + ROWS)
    qb = q[rows, cols]
    gb = g[rows, cols]
    scores = dot(k[0:seen, cols], qb, 1, 1)
    dp = dot(v[0:seen, cols], gb, 1, 1)
    if b == 1:
        shared["k_t"] = dot(unit, k[:, cols], 1, 1).astype(BF16)
        shared["v_t"] = dot(unit, v[:, cols], 1, 1).astype(BF16)
    yield
    key_pos = lax.broadcasted_iota(jnp.int32, (ROWS, ROWS), 0)
    query_pos = lax.broadcasted_iota(jnp.int32, (ROWS, ROWS), 1)
    if b == 0:
        limit = jnp.where(query_pos < SPAN, SPAN - 1, query_pos)
    else:
        limit = jnp.where(query_pos < SPAN, query_pos, ROWS - 1)
    last = jnp.where(key_pos <= limit, scores[seen - ROWS : seen], -1e30)
    scores = last if b == 0 else jnp.concatenate([scores[0:ROWS], last], axis=0)
    top = jnp.max(scores, axis=0, keepdims=True)
    yield
    e = jnp.exp2((scores - top) * power)
    total = jnp.sum(e, axis=0, keepdims=True)
    yield
    p = e * (1.0 / total)
    pb = p.astype(BF16)
    u = p * dp
    out_dot = jnp.sum(u, axis=0, keepdims=True)
    yield
    ds = (u - p * out_dot).astype(BF16)
    att_t = dot(shared["v_t"][:, 0:seen], pb, 1, 0)
    new_v = dot(pb, gb, 1, 0)
    yield
    dq_t = dot(shared["k_t"][:, 0:seen], ds, 1, 0) * scale
    new_k = dot(ds, qb, 1, 0)
    att[rows, cols] = jnp.transpose(att_t).astype(BF16)
    yield
    dq[rows, cols] = jnp.transpose(dq_t).astype(BF16)
    if b == 1:
        shared["dk"] = new_k[0:ROWS]
        shared["dv"] = new_v[0:ROWS]
    else:
        new_k = new_k + shared["dk"]
        new_v = new_v + shared["dv"]
    dk[rows, cols] = (new_k[seen - ROWS : seen] * scale).astype(BF16)
    dv[rows, cols] = new_v[seen - ROWS : seen].astype(BF16)


def hidden_of(lat, w1):
    pre = dot(lat, w1, 0, 0)
    return (pre * sigmoid(pre)).astype(BF16)


def attention_body(ctx_ref, starts, q_own, q_oth, k_own, k_oth, v_own, v_oth, g_own, g_oth, text, lat_own, lat_oth, w1, w2,
                   lay_out, dq_out, dk_out, dv_out, att_send, dq_send, dk_send, dv_send,
                   q, k, v, g, att, dq, dk, dv, hid):
    ctx = ctx_ref[0]
    own = pl.multiple_of(ctx * ROWS, ROWS)
    oth = pl.multiple_of(ROWS - ctx * ROWS, ROWS)

    @pl.when(pl.program_id(0) == 0)
    def _():
        hid[...] = hidden_of(pick(starts, lat_own, lat_oth)[0], w1[...])

    for full, a, b in ((q, q_own, q_oth), (k, k_own, k_oth), (v, v_own, v_oth), (g, g_own, g_oth)):
        full[pl.ds(own, ROWS), :] = a[...]
        full[pl.ds(oth, ROWS), :] = b[...]
    unit = eye(HEAD)
    waiting = []
    for h in range(GROUP):
        cols = slice(HEAD * h, HEAD * h + HEAD)
        shared = {}
        for b in (1, 0):
            waiting.append(chain(q, k, v, g, att, dq, dk, dv, cols, b, unit, shared))
    running = []
    while waiting or running:
        if waiting:
            running.append(waiting.pop(0))
        running = [item for item in running if next(item, "end") != "end"]
    mine = pl.ds(own, ROWS)
    theirs = pl.ds(oth, ROWS)
    for full, keep, send in ((dq, dq_out, dq_send), (dk, dk_out, dk_send), (dv, dv_out, dv_send)):
        keep[...] = full[mine, :]
        send[...] = full[theirs, :]
    att_send[...] = att[theirs, :]
    add_residual(ctx, lay_out, att[mine, :], hid[...], w2[...], text[...])


def add_residual(ctx, lay_out, att, hid, w2, text):
    lay_out[...] = att
    image_rows = pl.ds(pl.multiple_of(ctx * SPAN, SPAN), SPAN)
    text_rows = pl.ds(pl.multiple_of(SPAN - ctx * SPAN, SPAN), SPAN)
    embedding = dot(hid, w2, 1, 0).astype(BF16).astype(F32)
    lay_out[image_rows, :] = (embedding + lay_out[image_rows, :].astype(F32)).astype(BF16)
    lay_out[text_rows, :] = (text.astype(F32) + lay_out[text_rows, :].astype(F32)).astype(BF16)


def merge_body(ctx_ref, starts, text, lat_own, lat_oth, w1, w2, att, dq, dk, dv, lay_in, dq_in, dk_in, dv_in,
               lay_out, dq_out, dk_out, dv_out, hid):
    @pl.when(pl.program_id(0) == 0)
    def _():
        hid[...] = hidden_of(pick(starts, lat_own, lat_oth)[0], w1[...])

    add_residual(ctx_ref[0], lay_out, att[...], hid[...], w2[...], text[...])
    dq_out[...] = dq[...]
    dk_out[...] = dk[...]
    dv_out[...] = dv[...]


def local(queries, keys, values, residual, grad_out, latents, image_starts, w_first, w_second):
    ctx = lax.axis_index("ctx").astype(jnp.int32)
    scalars = (ctx[None], image_starts.reshape(2))
    swap = [(0, 1), (1, 0)]

    def swapped(value):
        return lax.ppermute(value, "ctx", swap)

    q_rows, k_rows, v_rows, g_rows, r_rows = queries[0], keys[0], values[0], grad_out[0], residual[0]
    lat_own = latents[0, 0]
    lat_oth = swapped(lat_own)
    g_oth, q_oth, k_oth, v_oth = [swapped(value) for value in (g_rows, q_rows, k_rows, v_rows)]

    struct = jax.ShapeDtypeStruct
    anywhere = pl.BlockSpec(memory_space=pl.ANY)
    lat_spec = whole((32, SPAN))
    payload = call(
        weight_body, scalars, (lat_own, lat_oth, w_first, w_second, g_rows, g_oth),
        [lat_spec, lat_spec, whole((32, CH)), anywhere, anywhere, anywhere],
        whole((16, 17, 16, 128)), struct((16, 17, 16, 128), BF16),
        scratch=[pltpu.VMEM((CH, WIDTH), BF16), pltpu.VMEM((ROWS, WIDTH), BF16), pltpu.SemaphoreType.DMA((3,))],
    )
    plane = ("y", "x")
    got = lax.all_to_all(payload, plane, 0, 0, tiled=False)

    cols = GROUP * HEAD
    steps = HEADS // GROUP
    own_spec = pl.BlockSpec((ROWS, cols), lambda i, c, s: (0, c[0] * steps + i))
    send_spec = pl.BlockSpec((ROWS, cols), lambda i, c, s: (0, i))
    big = struct((ROWS, WIDTH), BF16)
    small = struct((ROWS, HALF), BF16)
    result = call(
        attention_body, scalars,
        (q_rows, q_oth, k_rows, k_oth, v_rows, v_oth, g_rows, g_oth, r_rows, lat_own, lat_oth, w_first, w_second),
        [own_spec] * 8
        + [pl.BlockSpec((SPAN, cols), lambda i, c, s: (1 - c[0], c[0] * steps + i)),
           lat_spec, lat_spec, whole((32, CH)), pl.BlockSpec((CH, cols), lambda i, c, s: (0, c[0] * steps + i))],
        [own_spec] * 4 + [send_spec] * 4,
        [big] * 4 + [small] * 4,
        grid=(steps,),
        scratch=[pltpu.VMEM((SEQ, cols), BF16)] * 8 + [pltpu.VMEM((SPAN, CH), BF16)],
    )
    sent = [swapped(value) for value in result[4:]]

    total = got[0].astype(F32)
    for j in range(1, 16):
        total = total + got[j].astype(F32)
    got = lax.all_gather(total.astype(BF16), "z")
    got, *sent = lax.optimization_barrier((got, *sent))
    near = pl.BlockSpec(memory_space=pltpu.VMEM)
    low, high = pl.pallas_call(
        depth_sum_body, in_specs=[near], out_specs=[near, near],
        out_shape=[pltpu.VMEM((8, 16, 128), BF16), pltpu.VMEM((9, 16, 128), BF16)],
    )(pltpu.with_memory_space_constraint(got, pltpu.VMEM))
    low, high = lax.all_gather(low, plane), lax.all_gather(high, plane)
    sum_second, sum_first = call(
        finish_body, (), (low, high),
        [pl.BlockSpec((4, 8, 16, 128), lambda i: (i, 0, 0, 0)), pl.BlockSpec((4, 9, 16, 128), lambda i: (i, 0, 0, 0))],
        [pl.BlockSpec((128, HALF), lambda i: (i, 0)), pl.BlockSpec((8, CH), lambda i: (i, 0))],
        [struct((CH, HALF), F32), struct((32, CH), F32)], grid=(4,),
    )

    parts = 2
    width = HALF // parts
    half_spec = pl.BlockSpec((ROWS, width), lambda i, c, s: (0, (1 - c[0]) * parts + i))
    outs = call(
        merge_body, scalars, (r_rows, lat_own, lat_oth, w_first, w_second, *sent, *result[:4]),
        [pl.BlockSpec((SPAN, width), lambda i, c, s: (1 - c[0], (1 - c[0]) * parts + i)), lat_spec, lat_spec,
         whole((32, CH)), pl.BlockSpec((CH, width), lambda i, c, s: (0, (1 - c[0]) * parts + i))]
        + [pl.BlockSpec((ROWS, width), lambda i, c, s: (0, i))] * 4 + [anywhere] * 4,
        [half_spec] * 4, [big] * 4, grid=(parts,), scratch=[pltpu.VMEM((SPAN, CH), BF16)],
        aliases={11 + i: i for i in range(4)},
    )
    return (*[value[None] for value in outs], sum_first, sum_second)


def solution(mesh):
    axes = Mesh(mesh.devices.reshape(8, 4, 4, 2), ("z", "y", "x", "ctx"))
    dp = ("z", "y", "x")
    rows = P(dp, "ctx", None)
    return jax.shard_map(
        local,
        mesh=axes,
        in_specs=(rows, rows, rows, rows, rows, P(dp, "ctx", None, None), P(dp, None), P(), P()),
        out_specs=(rows, rows, rows, rows, P(), P(None, "ctx")),
        check_vma=False,
    )
```

```python
import math

import jax
import jax.numpy as jnp
from jax import lax
from jax.experimental import pallas as pl
from jax.experimental.pallas import tpu as pltpu
from jax.sharding import Mesh
from jax.sharding import PartitionSpec as P

HEAD = 128
SPAN = 128
ROWS = 256
HALF = 1024
WIDTH = 2048
SEQ = 512
CH = 512
HEADS = 8
GROUP = 4
VMEM = 56 * 1024 * 1024

F32 = jnp.float32
BF16 = jnp.bfloat16


def dot(a, b, ca, cb):
    return lax.dot_general(a, b, (((ca,), (cb,)), ((), ())), preferred_element_type=F32)


def whole(shape):
    return pl.BlockSpec(shape, lambda *_: (0,) * len(shape))


def call(body, scalars, args, in_specs, out_specs, out_shape, grid=(1,), scratch=(), aliases=None):
    return pl.pallas_call(
        body,
        grid_spec=pltpu.PrefetchScalarGridSpec(
            num_scalar_prefetch=len(scalars),
            grid=grid,
            in_specs=in_specs,
            out_specs=out_specs,
            scratch_shapes=scratch,
        ),
        out_shape=out_shape,
        input_output_aliases=aliases or {},
        compiler_params=pltpu.CompilerParams(vmem_limit_bytes=VMEM),
    )(*scalars, *args)


def sigmoid(v):
    return 1.0 / (1.0 + jnp.exp(-v))


def eye(n):
    rows = lax.broadcasted_iota(jnp.int32, (n, n), 0)
    cols = lax.broadcasted_iota(jnp.int32, (n, n), 1)
    return (rows == cols).astype(F32).astype(BF16)


def pick(starts, lat_own, lat_oth):
    in_order = starts[0] == 0
    one, two = lat_own[...].astype(F32), lat_oth[...].astype(F32)
    return jnp.where(in_order, one, two).astype(BF16), jnp.where(in_order, two, one).astype(BF16)


def weight_body(ctx_ref, starts, lat_own, lat_oth, w1, w2_hbm, g_own, g_oth, out, w2, grads, sems):
    ctx = ctx_ref[0]
    own_rows = pl.ds(pl.multiple_of(ctx * SPAN, SPAN), SPAN)
    oth_rows = pl.ds(pl.multiple_of(SPAN - ctx * SPAN, SPAN), SPAN)
    copies = [
        pltpu.make_async_copy(g_own.at[own_rows, :], grads.at[0:SPAN, :], sems.at[0]),
        pltpu.make_async_copy(w2_hbm, w2, sems.at[1]),
    ]
    for copy in copies:
        copy.start()
    grads[SPAN:ROWS, :] = g_oth[oth_rows, :]
    patches = jnp.concatenate(pick(starts, lat_own, lat_oth), axis=1)
    pre = dot(w1[...], patches, 0, 0)
    sig = sigmoid(pre)
    hid_t = (pre * sig).astype(BF16)
    copies[0].wait()
    for n in range(4):
        half = grads[:, pl.ds(pl.multiple_of(ctx * HALF, HALF) + 256 * n, 256)]
        strip = dot(hid_t, half, 1, 0).astype(BF16)
        for j in range(16):
            for i in range(4):
                rows = 32 * j + 16 * (i // 2)
                out[j, 8 * (i // 2) + 2 * n + i % 2] = strip[rows : rows + 16, 128 * (i % 2) : 128 * (i % 2) + 128]
    copies[1].wait()
    back = dot(w2[...], grads[...], 1, 1)
    grad_pre = (back * sig * (1.0 + pre * (1.0 - sig))).astype(BF16)
    first = dot(patches, grad_pre, 1, 1)
    zeros = jnp.zeros((8, 128), F32)
    for j in range(16):
        tile = first[8 * (j // 4) : 8 * (j // 4) + 8, 128 * (j % 4) : 128 * (j % 4) + 128]
        out[j, 16] = jnp.concatenate([tile, zeros], axis=0).astype(BF16)


def plane_sum_body(got, out):
    total = got[0].astype(F32)
    for j in range(1, 16):
        total = total + got[j].astype(F32)
    total = total.astype(BF16)
    for z in range(8):
        out[z, 0:2] = total[2 * z : 2 * z + 2]
        out[z, 2] = total[16]


def depth_sum_body(got, main, first):
    total = got[0].astype(F32)
    for z in range(1, 8):
        total = total + got[z].astype(F32)
    total = total.astype(BF16)
    for z in range(8):
        main[z] = total[0:2]
    first[...] = total[2]


def join_body(main, first, out):
    for j in range(16):
        for z in range(8):
            out[j, 2 * z : 2 * z + 2] = main[z]
        out[j, 16] = first[...]


def finish_body(got, second, first, second_near, first_near, sems):
    copies = []
    for n in range(4):
        for j in range(4 * n, 4 * n + 4):
            for t in range(16):
                rows = 32 * j + 16 * (t // 8)
                cols = 128 * (t % 8)
                second_near[rows : rows + 16, cols : cols + 128] = got[j, t].astype(F32) * (1.0 / 128.0)
            cols = 128 * (j % 4)
            first_near[8 * n : 8 * n + 8, cols : cols + 128] = got[j, 16].astype(F32)[0:8] * (1.0 / 128.0)
        part = pl.ds(128 * n, 128)
        copies.append(pltpu.make_async_copy(second_near.at[part, :], second.at[part, :], sems.at[n]))
        copies[-1].start()
    copies.append(pltpu.make_async_copy(first_near, first, sems.at[4]))
    copies[-1].start()
    for copy in copies:
        copy.wait()


def chain(q, k, v, g, att, dq, dk, dv, cols, b, unit, shared):
    scale = HEAD ** -0.5
    power = scale * math.log2(math.e)
    seen = ROWS * (b + 1)
    rows = slice(ROWS * b, ROWS * b + ROWS)
    qb = q[rows, cols]
    gb = g[rows, cols]
    scores = dot(k[0:seen, cols], qb, 1, 1)
    dp = dot(v[0:seen, cols], gb, 1, 1)
    if b == 1:
        shared["k_t"] = dot(unit, k[:, cols], 1, 1).astype(BF16)
        shared["v_t"] = dot(unit, v[:, cols], 1, 1).astype(BF16)
    yield
    key_pos = lax.broadcasted_iota(jnp.int32, (ROWS, ROWS), 0)
    query_pos = lax.broadcasted_iota(jnp.int32, (ROWS, ROWS), 1)
    if b == 0:
        limit = jnp.where(query_pos < SPAN, SPAN - 1, query_pos)
    else:
        limit = jnp.where(query_pos < SPAN, query_pos, ROWS - 1)
    last = jnp.where(key_pos <= limit, scores[seen - ROWS : seen], -1e30)
    scores = last if b == 0 else jnp.concatenate([scores[0:ROWS], last], axis=0)
    top = jnp.max(scores, axis=0, keepdims=True)
    yield
    e = jnp.exp2((scores - top) * power)
    total = jnp.sum(e, axis=0, keepdims=True)
    yield
    p = e * (1.0 / total)
    pb = p.astype(BF16)
    u = p * dp
    out_dot = jnp.sum(u, axis=0, keepdims=True)
    yield
    ds = (u - p * out_dot).astype(BF16)
    att_t = dot(shared["v_t"][:, 0:seen], pb, 1, 0)
    new_v = dot(pb, gb, 1, 0)
    yield
    dq_t = dot(shared["k_t"][:, 0:seen], ds, 1, 0) * scale
    new_k = dot(ds, qb, 1, 0)
    att[rows, cols] = jnp.transpose(att_t).astype(BF16)
    yield
    dq[rows, cols] = jnp.transpose(dq_t).astype(BF16)
    if b == 1:
        shared["dk"] = new_k[0:ROWS]
        shared["dv"] = new_v[0:ROWS]
    else:
        new_k = new_k + shared["dk"]
        new_v = new_v + shared["dv"]
    dk[rows, cols] = (new_k[seen - ROWS : seen] * scale).astype(BF16)
    dv[rows, cols] = new_v[seen - ROWS : seen].astype(BF16)


def hidden_of(lat, w1):
    pre = dot(lat, w1, 0, 0)
    return (pre * sigmoid(pre)).astype(BF16)


def attention_body(ctx_ref, starts, q_own, q_oth, k_own, k_oth, v_own, v_oth, g_own, g_oth, text, lat_own, lat_oth, w1, w2,
                   lay_out, dq_out, dk_out, dv_out, att_send, dq_send, dk_send, dv_send,
                   q, k, v, g, att, dq, dk, dv, hid):
    ctx = ctx_ref[0]
    own = pl.multiple_of(ctx * ROWS, ROWS)
    oth = pl.multiple_of(ROWS - ctx * ROWS, ROWS)

    @pl.when(pl.program_id(0) == 0)
    def _():
        hid[...] = hidden_of(pick(starts, lat_own, lat_oth)[0], w1[...])

    for full, a, b in ((q, q_own, q_oth), (k, k_own, k_oth), (v, v_own, v_oth), (g, g_own, g_oth)):
        full[pl.ds(own, ROWS), :] = a[...]
        full[pl.ds(oth, ROWS), :] = b[...]
    unit = eye(HEAD)
    waiting = []
    for h in range(GROUP):
        cols = slice(HEAD * h, HEAD * h + HEAD)
        shared = {}
        for b in (1, 0):
            waiting.append(chain(q, k, v, g, att, dq, dk, dv, cols, b, unit, shared))
    running = []
    while waiting or running:
        if waiting:
            running.append(waiting.pop(0))
        running = [item for item in running if next(item, "end") != "end"]
    mine = pl.ds(own, ROWS)
    theirs = pl.ds(oth, ROWS)
    for full, keep, send in ((dq, dq_out, dq_send), (dk, dk_out, dk_send), (dv, dv_out, dv_send)):
        keep[...] = full[mine, :]
        send[...] = full[theirs, :]
    att_send[...] = att[theirs, :]
    add_residual(ctx, lay_out, att[mine, :], hid[...], w2[...], text[...])


def add_residual(ctx, lay_out, att, hid, w2, text):
    lay_out[...] = att
    image_rows = pl.ds(pl.multiple_of(ctx * SPAN, SPAN), SPAN)
    text_rows = pl.ds(pl.multiple_of(SPAN - ctx * SPAN, SPAN), SPAN)
    embedding = dot(hid, w2, 1, 0).astype(BF16).astype(F32)
    lay_out[image_rows, :] = (embedding + lay_out[image_rows, :].astype(F32)).astype(BF16)
    lay_out[text_rows, :] = (text.astype(F32) + lay_out[text_rows, :].astype(F32)).astype(BF16)


def merge_body(ctx_ref, starts, text, lat_own, lat_oth, w1, w2, att, dq, dk, dv, lay_in, dq_in, dk_in, dv_in,
               lay_out, dq_out, dk_out, dv_out, hid):
    @pl.when(pl.program_id(0) == 0)
    def _():
        hid[...] = hidden_of(pick(starts, lat_own, lat_oth)[0], w1[...])

    add_residual(ctx_ref[0], lay_out, att[...], hid[...], w2[...], text[...])
    dq_out[...] = dq[...]
    dk_out[...] = dk[...]
    dv_out[...] = dv[...]


def local(queries, keys, values, residual, grad_out, latents, image_starts, w_first, w_second):
    ctx = lax.axis_index("ctx").astype(jnp.int32)
    scalars = (ctx[None], image_starts.reshape(2))
    swap = [(0, 1), (1, 0)]

    def swapped(value):
        return lax.ppermute(value, "ctx", swap)

    q_rows, k_rows, v_rows, g_rows, r_rows = queries[0], keys[0], values[0], grad_out[0], residual[0]
    lat_own = latents[0, 0]
    lat_oth = swapped(lat_own)
    g_oth = swapped(g_rows)
    lat_oth, g_oth, *rows = lax.optimization_barrier((lat_oth, g_oth, q_rows, k_rows, v_rows))
    q_oth, k_oth, v_oth = [swapped(value) for value in rows]

    struct = jax.ShapeDtypeStruct
    anywhere = pl.BlockSpec(memory_space=pl.ANY)
    near = pl.BlockSpec(memory_space=pltpu.VMEM)

    def place_near(value):
        return pltpu.with_memory_space_constraint(value, pltpu.VMEM)

    def near_call(body, args, outs):
        return pl.pallas_call(
            body, in_specs=[near] * len(args), out_specs=[near] * len(outs),
            out_shape=[pltpu.VMEM(shape, BF16) for shape in outs],
        )(*[place_near(value) for value in args])

    lat_spec = whole((32, SPAN))
    payload, = call(
        weight_body, scalars, (lat_own, place_near(lat_oth), w_first, w_second, g_rows, place_near(g_oth)),
        [lat_spec, near, whole((32, CH)), anywhere, anywhere, near],
        [near], [pltpu.VMEM((16, 17, 16, 128), BF16)],
        scratch=[pltpu.VMEM((CH, WIDTH), BF16), pltpu.VMEM((ROWS, WIDTH), BF16), pltpu.SemaphoreType.DMA((2,))],
    )
    plane = ("y", "x")
    got = lax.all_to_all(payload, plane, 0, 0, tiled=False)

    cols = GROUP * HEAD
    steps = HEADS // GROUP
    own_spec = pl.BlockSpec((ROWS, cols), lambda i, c, s: (0, c[0] * steps + i))
    send_spec = pl.BlockSpec((ROWS, cols), lambda i, c, s: (0, i))
    big = struct((ROWS, WIDTH), BF16)
    small = struct((ROWS, HALF), BF16)
    result = call(
        attention_body, scalars,
        (q_rows, q_oth, k_rows, k_oth, v_rows, v_oth, g_rows, g_oth, r_rows, lat_own, lat_oth, w_first, w_second),
        [own_spec] * 8
        + [pl.BlockSpec((SPAN, cols), lambda i, c, s: (1 - c[0], c[0] * steps + i)),
           lat_spec, lat_spec, whole((32, CH)), pl.BlockSpec((CH, cols), lambda i, c, s: (0, c[0] * steps + i))],
        [own_spec] * 4 + [send_spec] * 4,
        [big] * 4 + [small] * 4,
        grid=(steps,),
        scratch=[pltpu.VMEM((SEQ, cols), BF16)] * 8 + [pltpu.VMEM((SPAN, CH), BF16)],
    )
    sent = [swapped(value) for value in result[4:]]

    part, = near_call(plane_sum_body, (got,), [(8, 3, 16, 128)])
    got = lax.all_to_all(part, "z", 0, 0, tiled=False)
    got, *sent = lax.optimization_barrier((got, *sent))
    main, first = near_call(depth_sum_body, (got,), [(8, 2, 16, 128), (16, 128)])
    main = lax.all_to_all(main, "z", 0, 0, tiled=False)
    whole_sums, = near_call(join_body, (main, first), [(16, 17, 16, 128)])
    got = lax.all_to_all(whole_sums, plane, 0, 0, tiled=False)
    sum_second, sum_first = pl.pallas_call(
        finish_body, in_specs=[near], out_specs=[anywhere, anywhere],
        out_shape=[struct((CH, HALF), F32), struct((32, CH), F32)],
        scratch_shapes=[pltpu.VMEM((CH, HALF), F32), pltpu.VMEM((32, CH), F32), pltpu.SemaphoreType.DMA((5,))],
        compiler_params=pltpu.CompilerParams(vmem_limit_bytes=VMEM),
    )(place_near(got))

    parts = 2
    width = HALF // parts
    half_spec = pl.BlockSpec((ROWS, width), lambda i, c, s: (0, (1 - c[0]) * parts + i))
    outs = call(
        merge_body, scalars, (r_rows, lat_own, lat_oth, w_first, w_second, *sent, *result[:4]),
        [pl.BlockSpec((SPAN, width), lambda i, c, s: (1 - c[0], (1 - c[0]) * parts + i)), lat_spec, lat_spec,
         whole((32, CH)), pl.BlockSpec((CH, width), lambda i, c, s: (0, (1 - c[0]) * parts + i))]
        + [pl.BlockSpec((ROWS, width), lambda i, c, s: (0, i))] * 4 + [anywhere] * 4,
        [half_spec] * 4, [big] * 4, grid=(parts,), scratch=[pltpu.VMEM((SPAN, CH), BF16)],
        aliases={11 + i: i for i in range(4)},
    )
    return (*[value[None] for value in outs], sum_first, sum_second)


def solution(mesh):
    axes = Mesh(mesh.devices.reshape(8, 4, 4, 2), ("z", "y", "x", "ctx"))
    dp = ("z", "y", "x")
    rows = P(dp, "ctx", None)
    return jax.shard_map(
        local,
        mesh=axes,
        in_specs=(rows, rows, rows, rows, rows, P(dp, "ctx", None, None), P(dp, None), P(), P()),
        out_specs=(rows, rows, rows, rows, P(), P(None, "ctx")),
        check_vma=False,
    )
```

```python
import math

import jax
import jax.numpy as jnp
from jax import lax
from jax.experimental import pallas as pl
from jax.experimental.pallas import tpu as pltpu
from jax.sharding import Mesh
from jax.sharding import PartitionSpec as P

HEAD = 128
SPAN = 128
ROWS = 256
HALF = 1024
WIDTH = 2048
SEQ = 512
CH = 512
HEADS = 8
GROUP = 4
VMEM = 56 * 1024 * 1024

F32 = jnp.float32
BF16 = jnp.bfloat16


def dot(a, b, ca, cb):
    return lax.dot_general(a, b, (((ca,), (cb,)), ((), ())), preferred_element_type=F32)


def whole(shape):
    return pl.BlockSpec(shape, lambda *_: (0,) * len(shape))


def call(body, scalars, args, in_specs, out_specs, out_shape, grid=(1,), scratch=(), aliases=None):
    return pl.pallas_call(
        body,
        grid_spec=pltpu.PrefetchScalarGridSpec(
            num_scalar_prefetch=len(scalars),
            grid=grid,
            in_specs=in_specs,
            out_specs=out_specs,
            scratch_shapes=scratch,
        ),
        out_shape=out_shape,
        input_output_aliases=aliases or {},
        compiler_params=pltpu.CompilerParams(vmem_limit_bytes=VMEM),
    )(*scalars, *args)


def sigmoid(v):
    return 1.0 / (1.0 + jnp.exp(-v))


def eye(n):
    rows = lax.broadcasted_iota(jnp.int32, (n, n), 0)
    cols = lax.broadcasted_iota(jnp.int32, (n, n), 1)
    return (rows == cols).astype(F32).astype(BF16)


def pick(starts, lat_own, lat_oth):
    in_order = starts[0] == 0
    one, two = lat_own[...].astype(F32), lat_oth[...].astype(F32)
    return jnp.where(in_order, one, two).astype(BF16), jnp.where(in_order, two, one).astype(BF16)


def weight_body(ctx_ref, starts, lat_hbm, lat_oth, w1_hbm, w2_hbm, g_own, g_oth, out, lat_own, w1, w2, grads, sems):
    ctx = ctx_ref[0]
    own_rows = pl.ds(pl.multiple_of(ctx * SPAN, SPAN), SPAN)
    oth_rows = pl.ds(pl.multiple_of(SPAN - ctx * SPAN, SPAN), SPAN)
    copies = [
        pltpu.make_async_copy(source, target, sems.at[i])
        for i, (source, target) in enumerate((
            (lat_hbm, lat_own), (w1_hbm, w1), (g_own.at[own_rows, :], grads.at[0:SPAN, :]), (w2_hbm, w2)))
    ]
    for copy in copies:
        copy.start()
    grads[SPAN:ROWS, :] = g_oth[oth_rows, :]
    copies[0].wait()
    copies[1].wait()
    patches = jnp.concatenate(pick(starts, lat_own, lat_oth), axis=1)
    pre = dot(w1[...], patches, 0, 0)
    sig = sigmoid(pre)
    hid_t = (pre * sig).astype(BF16)
    copies[2].wait()
    for n in range(4):
        half = grads[:, pl.ds(pl.multiple_of(ctx * HALF, HALF) + 256 * n, 256)]
        strip = dot(hid_t, half, 1, 0).astype(BF16)
        for j in range(16):
            for i in range(4):
                rows = 32 * j + 16 * (i // 2)
                out[j, 8 * (i // 2) + 2 * n + i % 2] = strip[rows : rows + 16, 128 * (i % 2) : 128 * (i % 2) + 128]
    copies[3].wait()
    back = dot(w2[...], grads[...], 1, 1)
    grad_pre = (back * sig * (1.0 + pre * (1.0 - sig))).astype(BF16)
    first = dot(patches, grad_pre, 1, 1)
    zeros = jnp.zeros((8, 128), F32)
    for j in range(16):
        tile = first[8 * (j // 4) : 8 * (j // 4) + 8, 128 * (j % 4) : 128 * (j % 4) + 128]
        out[j, 16] = jnp.concatenate([tile, zeros], axis=0).astype(BF16)


def plane_sum_body(got, out):
    total = got[0].astype(F32)
    for j in range(1, 16):
        total = total + got[j].astype(F32)
    total = total.astype(BF16)
    for z in range(8):
        out[z, 0:2] = total[2 * z : 2 * z + 2]
        out[z, 2] = total[16]


def depth_sum_body(got, main, first):
    total = got[0].astype(F32)
    for z in range(1, 8):
        total = total + got[z].astype(F32)
    total = total.astype(BF16)
    for z in range(8):
        main[z] = total[0:2]
    first[...] = total[2]


def join_body(main, first, out):
    for j in range(16):
        for z in range(8):
            out[j, 2 * z : 2 * z + 2] = main[z]
        out[j, 16] = first[...]


def finish_body(got, second, first, second_near, first_near, sems):
    copies = []
    for n in range(4):
        for j in range(4 * n, 4 * n + 4):
            for t in range(16):
                rows = 32 * j + 16 * (t // 8)
                cols = 128 * (t % 8)
                second_near[rows : rows + 16, cols : cols + 128] = got[j, t].astype(F32) * (1.0 / 128.0)
            cols = 128 * (j % 4)
            first_near[8 * n : 8 * n + 8, cols : cols + 128] = got[j, 16].astype(F32)[0:8] * (1.0 / 128.0)
        part = pl.ds(128 * n, 128)
        copies.append(pltpu.make_async_copy(second_near.at[part, :], second.at[part, :], sems.at[n]))
        copies[-1].start()
    copies.append(pltpu.make_async_copy(first_near, first, sems.at[4]))
    copies[-1].start()
    for copy in copies:
        copy.wait()


def chain(q, k, v, g, att, dq, dk, dv, cols, b, unit, shared):
    scale = HEAD ** -0.5
    power = scale * math.log2(math.e)
    seen = ROWS * (b + 1)
    rows = slice(ROWS * b, ROWS * b + ROWS)
    qb = q[rows, cols]
    gb = g[rows, cols]
    scores = dot(k[0:seen, cols], qb, 1, 1)
    dp = dot(v[0:seen, cols], gb, 1, 1)
    if b == 1:
        shared["k_t"] = dot(unit, k[:, cols], 1, 1).astype(BF16)
        shared["v_t"] = dot(unit, v[:, cols], 1, 1).astype(BF16)
    yield
    key_pos = lax.broadcasted_iota(jnp.int32, (ROWS, ROWS), 0)
    query_pos = lax.broadcasted_iota(jnp.int32, (ROWS, ROWS), 1)
    if b == 0:
        limit = jnp.where(query_pos < SPAN, SPAN - 1, query_pos)
    else:
        limit = jnp.where(query_pos < SPAN, query_pos, ROWS - 1)
    last = jnp.where(key_pos <= limit, scores[seen - ROWS : seen], -1e30)
    scores = last if b == 0 else jnp.concatenate([scores[0:ROWS], last], axis=0)
    top = jnp.max(scores, axis=0, keepdims=True)
    yield
    e = jnp.exp2((scores - top) * power)
    total = jnp.sum(e, axis=0, keepdims=True)
    yield
    p = e * (1.0 / total)
    pb = p.astype(BF16)
    u = p * dp
    out_dot = jnp.sum(u, axis=0, keepdims=True)
    yield
    ds = (u - p * out_dot).astype(BF16)
    att_t = dot(shared["v_t"][:, 0:seen], pb, 1, 0)
    new_v = dot(pb, gb, 1, 0)
    yield
    dq_t = dot(shared["k_t"][:, 0:seen], ds, 1, 0) * scale
    new_k = dot(ds, qb, 1, 0)
    att[rows, cols] = jnp.transpose(att_t).astype(BF16)
    yield
    dq[rows, cols] = jnp.transpose(dq_t).astype(BF16)
    if b == 1:
        shared["dk"] = new_k[0:ROWS]
        shared["dv"] = new_v[0:ROWS]
    else:
        new_k = new_k + shared["dk"]
        new_v = new_v + shared["dv"]
    dk[rows, cols] = (new_k[seen - ROWS : seen] * scale).astype(BF16)
    dv[rows, cols] = new_v[seen - ROWS : seen].astype(BF16)


def hidden_of(lat, w1):
    pre = dot(lat, w1, 0, 0)
    return (pre * sigmoid(pre)).astype(BF16)


def attention_body(ctx_ref, starts, q_own, q_oth, k_own, k_oth, v_own, v_oth, g_own, g_oth, text, lat_own, lat_oth, w1, w2,
                   lay_out, dq_out, dk_out, dv_out, att_send, dq_send, dk_send, dv_send,
                   q, k, v, g, att, dq, dk, dv, hid):
    ctx = ctx_ref[0]
    own = pl.multiple_of(ctx * ROWS, ROWS)
    oth = pl.multiple_of(ROWS - ctx * ROWS, ROWS)

    @pl.when(pl.program_id(0) == 0)
    def _():
        hid[...] = hidden_of(pick(starts, lat_own, lat_oth)[0], w1[...])

    for full, a, b in ((q, q_own, q_oth), (k, k_own, k_oth), (v, v_own, v_oth), (g, g_own, g_oth)):
        full[pl.ds(own, ROWS), :] = a[...]
        full[pl.ds(oth, ROWS), :] = b[...]
    unit = eye(HEAD)
    waiting = []
    for h in range(GROUP):
        cols = slice(HEAD * h, HEAD * h + HEAD)
        shared = {}
        for b in (1, 0):
            waiting.append(chain(q, k, v, g, att, dq, dk, dv, cols, b, unit, shared))
    running = []
    while waiting or running:
        if waiting:
            running.append(waiting.pop(0))
        running = [item for item in running if next(item, "end") != "end"]
    mine = pl.ds(own, ROWS)
    theirs = pl.ds(oth, ROWS)
    for full, keep, send in ((dq, dq_out, dq_send), (dk, dk_out, dk_send), (dv, dv_out, dv_send)):
        keep[...] = full[mine, :]
        send[...] = full[theirs, :]
    att_send[...] = att[theirs, :]
    add_residual(ctx, lay_out, att[mine, :], hid[...], w2[...], text[...])


def add_residual(ctx, lay_out, att, hid, w2, text):
    lay_out[...] = att
    image_rows = pl.ds(pl.multiple_of(ctx * SPAN, SPAN), SPAN)
    text_rows = pl.ds(pl.multiple_of(SPAN - ctx * SPAN, SPAN), SPAN)
    embedding = dot(hid, w2, 1, 0).astype(BF16).astype(F32)
    lay_out[image_rows, :] = (embedding + lay_out[image_rows, :].astype(F32)).astype(BF16)
    lay_out[text_rows, :] = (text.astype(F32) + lay_out[text_rows, :].astype(F32)).astype(BF16)


def place_body(ctx_ref, *refs):
    count = (len(refs) - 1) // 3
    got, out, sems = refs[:count], refs[2 * count : 3 * count], refs[-1]
    cols = pl.ds(pl.multiple_of(HALF - ctx_ref[0] * HALF, HALF), HALF)
    copies = [pltpu.make_async_copy(got[i], out[i].at[:, cols], sems.at[i]) for i in range(count)]
    for copy in copies:
        copy.start()
    for copy in copies:
        copy.wait()


def merge_body(ctx_ref, starts, text, lat_own, lat_oth, w1, w2, att, lay_in, lay_out, hid):
    @pl.when(pl.program_id(0) == 0)
    def _():
        hid[...] = hidden_of(pick(starts, lat_own, lat_oth)[0], w1[...])

    add_residual(ctx_ref[0], lay_out, att[...], hid[...], w2[...], text[...])


def local(queries, keys, values, residual, grad_out, latents, image_starts, w_first, w_second):
    ctx = lax.axis_index("ctx").astype(jnp.int32)
    scalars = (ctx[None], image_starts.reshape(2))
    swap = [(0, 1), (1, 0)]

    def swapped(value):
        return lax.ppermute(value, "ctx", swap)

    q_rows, k_rows, v_rows, g_rows, r_rows = queries[0], keys[0], values[0], grad_out[0], residual[0]
    lat_own = latents[0, 0]
    lat_oth = swapped(lat_own)
    g_oth = swapped(g_rows)
    lat_oth, g_oth, *rows = lax.optimization_barrier((lat_oth, g_oth, q_rows, k_rows, v_rows))
    q_oth, k_oth, v_oth = [swapped(value) for value in rows]

    struct = jax.ShapeDtypeStruct
    anywhere = pl.BlockSpec(memory_space=pl.ANY)
    near = pl.BlockSpec(memory_space=pltpu.VMEM)

    def place_near(value):
        return pltpu.with_memory_space_constraint(value, pltpu.VMEM)

    def near_call(body, args, outs):
        return pl.pallas_call(
            body, in_specs=[near] * len(args), out_specs=[near] * len(outs),
            out_shape=[pltpu.VMEM(shape, BF16) for shape in outs],
        )(*[place_near(value) for value in args])

    lat_spec = whole((32, SPAN))
    payload, = call(
        weight_body, scalars, (lat_own, place_near(lat_oth), w_first, w_second, g_rows, place_near(g_oth)),
        [anywhere, near, anywhere, anywhere, anywhere, near], [near], [pltpu.VMEM((16, 17, 16, 128), BF16)],
        scratch=[pltpu.VMEM((32, SPAN), BF16), pltpu.VMEM((32, CH), BF16), pltpu.VMEM((CH, WIDTH), BF16),
                 pltpu.VMEM((ROWS, WIDTH), BF16), pltpu.SemaphoreType.DMA((4,))],
    )
    plane = ("y", "x")
    got = lax.all_to_all(payload, plane, 0, 0, tiled=False)

    cols = GROUP * HEAD
    steps = HEADS // GROUP
    own_spec = pl.BlockSpec((ROWS, cols), lambda i, c, s: (0, c[0] * steps + i))
    send_spec = pl.BlockSpec((ROWS, cols), lambda i, c, s: (0, i))
    big = struct((ROWS, WIDTH), BF16)
    small = struct((ROWS, HALF), BF16)
    result = call(
        attention_body, scalars,
        (q_rows, q_oth, k_rows, k_oth, v_rows, v_oth, g_rows, g_oth, r_rows, lat_own, lat_oth, w_first, w_second),
        [own_spec] * 8
        + [pl.BlockSpec((SPAN, cols), lambda i, c, s: (1 - c[0], c[0] * steps + i)),
           lat_spec, lat_spec, whole((32, CH)), pl.BlockSpec((CH, cols), lambda i, c, s: (0, c[0] * steps + i))],
        [own_spec] * 4 + [send_spec] * 4,
        [big] * 4 + [small] * 4,
        grid=(steps,),
        scratch=[pltpu.VMEM((SEQ, cols), BF16)] * 8 + [pltpu.VMEM((SPAN, CH), BF16)],
    )
    lay, dq, dk, dv = result[:4]
    sent_att, sent_dq, sent_dk, sent_dv = [swapped(value) for value in result[4:]]

    def placed(got, into):
        count = len(got)
        return call(
            place_body, scalars[:1], (*got, *into), [anywhere] * (2 * count), [anywhere] * count, [big] * count,
            scratch=[pltpu.SemaphoreType.DMA((count,))], aliases={1 + count + i: i for i in range(count)},
        )

    part, = near_call(plane_sum_body, (got,), [(8, 3, 16, 128)])
    part, sent_dq, sent_dk = lax.optimization_barrier((part, sent_dq, sent_dk))
    got = lax.all_to_all(part, "z", 0, 0, tiled=False)
    dq, dk = placed((sent_dq, sent_dk), (dq, dk))
    got, dq, dk = lax.optimization_barrier((got, dq, dk))
    main, first = near_call(depth_sum_body, (got,), [(8, 2, 16, 128), (16, 128)])
    main, sent_dv = lax.optimization_barrier((main, sent_dv))
    main = lax.all_to_all(main, "z", 0, 0, tiled=False)
    dv, = placed((sent_dv,), (dv,))
    main, dv = lax.optimization_barrier((main, dv))
    whole_sums, = near_call(join_body, (main, first), [(16, 17, 16, 128)])
    whole_sums, sent_att = lax.optimization_barrier((whole_sums, sent_att))
    got = lax.all_to_all(whole_sums, plane, 0, 0, tiled=False)
    sum_second, sum_first = pl.pallas_call(
        finish_body, in_specs=[near], out_specs=[anywhere, anywhere],
        out_shape=[struct((CH, HALF), F32), struct((32, CH), F32)],
        scratch_shapes=[pltpu.VMEM((CH, HALF), F32), pltpu.VMEM((32, CH), F32), pltpu.SemaphoreType.DMA((5,))],
        compiler_params=pltpu.CompilerParams(vmem_limit_bytes=VMEM),
    )(place_near(got))

    parts = 2
    width = HALF // parts
    half_spec = pl.BlockSpec((ROWS, width), lambda i, c, s: (0, (1 - c[0]) * parts + i))
    lay = call(
        merge_body, scalars, (r_rows, lat_own, lat_oth, w_first, w_second, sent_att, lay),
        [pl.BlockSpec((SPAN, width), lambda i, c, s: (1 - c[0], (1 - c[0]) * parts + i)), lat_spec, lat_spec,
         whole((32, CH)), pl.BlockSpec((CH, width), lambda i, c, s: (0, (1 - c[0]) * parts + i)),
         pl.BlockSpec((ROWS, width), lambda i, c, s: (0, i)), anywhere],
        half_spec, big, grid=(parts,), scratch=[pltpu.VMEM((SPAN, CH), BF16)], aliases={8: 0},
    )
    outs = (lay, dq, dk, dv)
    return (*[value[None] for value in outs], sum_first, sum_second)


def solution(mesh):
    axes = Mesh(mesh.devices.reshape(8, 4, 4, 2), ("z", "y", "x", "ctx"))
    dp = ("z", "y", "x")
    rows = P(dp, "ctx", None)
    return jax.shard_map(
        local,
        mesh=axes,
        in_specs=(rows, rows, rows, rows, rows, P(dp, "ctx", None, None), P(dp, None), P(), P()),
        out_specs=(rows, rows, rows, rows, P(), P(None, "ctx")),
        check_vma=False,
    )
```

```python
import math

import jax
import jax.numpy as jnp
from jax import lax
from jax.experimental import pallas as pl
from jax.experimental.pallas import tpu as pltpu
from jax.sharding import Mesh
from jax.sharding import PartitionSpec as P

HEAD = 128
SPAN = 128
ROWS = 256
HALF = 1024
WIDTH = 2048
SEQ = 512
CH = 512
HEADS = 8
GROUP = 4
GROUPS = 32
VMEM = 56 * 1024 * 1024

F32 = jnp.float32
BF16 = jnp.bfloat16


def dot(a, b, ca, cb):
    return lax.dot_general(a, b, (((ca,), (cb,)), ((), ())), preferred_element_type=F32)


def whole(shape):
    return pl.BlockSpec(shape, lambda *_: (0,) * len(shape))


def call(body, scalars, args, in_specs, out_specs, out_shape, grid=(1,), scratch=(), aliases=None):
    return pl.pallas_call(
        body,
        grid_spec=pltpu.PrefetchScalarGridSpec(
            num_scalar_prefetch=len(scalars),
            grid=grid,
            in_specs=in_specs,
            out_specs=out_specs,
            scratch_shapes=scratch,
        ),
        out_shape=out_shape,
        input_output_aliases=aliases or {},
        compiler_params=pltpu.CompilerParams(vmem_limit_bytes=VMEM),
    )(*scalars, *args)


def sigmoid(v):
    return 1.0 / (1.0 + jnp.exp(-v))


def eye(n):
    rows = lax.broadcasted_iota(jnp.int32, (n, n), 0)
    cols = lax.broadcasted_iota(jnp.int32, (n, n), 1)
    return (rows == cols).astype(F32).astype(BF16)


def pick(starts, lat_own, lat_oth):
    in_order = starts[0] == 0
    one, two = lat_own[...].astype(F32), lat_oth[...].astype(F32)
    return jnp.where(in_order, one, two).astype(BF16), jnp.where(in_order, two, one).astype(BF16)


def weight_body(ctx_ref, starts, lat_hbm, lat_oth, w1_hbm, w2_hbm, g_own, g_oth, out, lat_own, w1, w2, grads, sems):
    ctx = ctx_ref[0]
    own_rows = pl.ds(pl.multiple_of(ctx * SPAN, SPAN), SPAN)
    oth_rows = pl.ds(pl.multiple_of(SPAN - ctx * SPAN, SPAN), SPAN)
    copies = [
        pltpu.make_async_copy(source, target, sems.at[i])
        for i, (source, target) in enumerate((
            (lat_hbm, lat_own), (w1_hbm, w1), (g_own.at[own_rows, :], grads.at[0:SPAN, :]), (w2_hbm, w2)))
    ]
    for copy in copies:
        copy.start()
    grads[SPAN:ROWS, :] = g_oth[oth_rows, :]
    copies[0].wait()
    copies[1].wait()
    patches = jnp.concatenate(pick(starts, lat_own, lat_oth), axis=1)
    pre = dot(w1[...], patches, 0, 0)
    sig = sigmoid(pre)
    hid_t = (pre * sig).astype(BF16)
    copies[2].wait()
    for n in range(4):
        half = grads[:, pl.ds(pl.multiple_of(ctx * HALF, HALF) + 256 * n, 256)]
        strip = dot(hid_t, half, 1, 0).astype(BF16)
        for j in range(GROUPS):
            for i in range(2):
                out[j, 2 * n + i] = strip[16 * j : 16 * j + 16, 128 * i : 128 * i + 128]
    copies[3].wait()
    back = dot(w2[...], grads[...], 1, 1)
    grad_pre = (back * sig * (1.0 + pre * (1.0 - sig))).astype(BF16)
    first = dot(patches, grad_pre, 1, 1)
    first = first.astype(BF16)
    for j in range(GROUPS):
        m = j // 4
        out[j, 8] = first[16 * (m // 4) : 16 * (m // 4) + 16, 128 * (m % 4) : 128 * (m % 4) + 128]


def group_sum_body(got, out):
    total = got[0].astype(F32)
    for j in range(1, GROUPS):
        total = total + got[j].astype(F32)
    out[...] = total.astype(BF16)


def pair_sum_body(one, two, out):
    out[...] = (one[...].astype(F32) + two[...].astype(F32)).astype(BF16)


def spread_sum_body(one, two, out):
    total = (one[...].astype(F32) + two[...].astype(F32)).astype(BF16)
    for j in range(GROUPS):
        out[j] = total


def finish_body(got, second, first, second_near, first_near, sems):
    copies = []
    for n in range(4):
        for j in range(8 * n, 8 * n + 8):
            for t in range(8):
                second_near[16 * j : 16 * j + 16, 128 * t : 128 * t + 128] = got[j, t].astype(F32) * (1.0 / 128.0)
        part = pl.ds(128 * n, 128)
        copies.append(pltpu.make_async_copy(second_near.at[part, :], second.at[part, :], sems.at[n]))
        copies[-1].start()
    for m in range(8):
        rows, cols = 16 * (m // 4), 128 * (m % 4)
        first_near[rows : rows + 16, cols : cols + 128] = got[4 * m, 8].astype(F32) * (1.0 / 128.0)
    copies.append(pltpu.make_async_copy(first_near, first, sems.at[4]))
    copies[-1].start()
    for copy in copies:
        copy.wait()


def chain(q, k, v, g, att, dq, dk, dv, cols, b, unit, shared):
    scale = HEAD ** -0.5
    power = scale * math.log2(math.e)
    seen = ROWS * (b + 1)
    rows = slice(ROWS * b, ROWS * b + ROWS)
    qb = q[rows, cols]
    gb = g[rows, cols]
    scores = dot(k[0:seen, cols], qb, 1, 1)
    dp = dot(v[0:seen, cols], gb, 1, 1)
    if b == 1:
        shared["k_t"] = dot(unit, k[:, cols], 1, 1).astype(BF16)
        shared["v_t"] = dot(unit, v[:, cols], 1, 1).astype(BF16)
    yield
    key_pos = lax.broadcasted_iota(jnp.int32, (ROWS, ROWS), 0)
    query_pos = lax.broadcasted_iota(jnp.int32, (ROWS, ROWS), 1)
    if b == 0:
        limit = jnp.where(query_pos < SPAN, SPAN - 1, query_pos)
    else:
        limit = jnp.where(query_pos < SPAN, query_pos, ROWS - 1)
    last = jnp.where(key_pos <= limit, scores[seen - ROWS : seen], -1e30)
    scores = last if b == 0 else jnp.concatenate([scores[0:ROWS], last], axis=0)
    top = jnp.max(scores, axis=0, keepdims=True)
    yield
    e = jnp.exp2((scores - top) * power)
    total = jnp.sum(e, axis=0, keepdims=True)
    yield
    p = e * (1.0 / total)
    pb = p.astype(BF16)
    u = p * dp
    out_dot = jnp.sum(u, axis=0, keepdims=True)
    yield
    ds = (u - p * out_dot).astype(BF16)
    att_t = dot(shared["v_t"][:, 0:seen], pb, 1, 0)
    new_v = dot(pb, gb, 1, 0)
    yield
    dq_t = dot(shared["k_t"][:, 0:seen], ds, 1, 0) * scale
    new_k = dot(ds, qb, 1, 0)
    att[rows, cols] = jnp.transpose(att_t).astype(BF16)
    yield
    dq[rows, cols] = jnp.transpose(dq_t).astype(BF16)
    if b == 1:
        shared["dk"] = new_k[0:ROWS]
        shared["dv"] = new_v[0:ROWS]
    else:
        new_k = new_k + shared["dk"]
        new_v = new_v + shared["dv"]
    dk[rows, cols] = (new_k[seen - ROWS : seen] * scale).astype(BF16)
    dv[rows, cols] = new_v[seen - ROWS : seen].astype(BF16)


def hidden_of(lat, w1):
    pre = dot(lat, w1, 0, 0)
    return (pre * sigmoid(pre)).astype(BF16)


def attention_body(ctx_ref, starts, q_own, q_oth, k_own, k_oth, v_own, v_oth, g_own, g_oth, text, lat_own, lat_oth, w1, w2,
                   lay_out, dq_out, dk_out, dv_out, att_send, dq_send, dk_send, dv_send,
                   q, k, v, g, att, dq, dk, dv, hid):
    ctx = ctx_ref[0]
    own = pl.multiple_of(ctx * ROWS, ROWS)
    oth = pl.multiple_of(ROWS - ctx * ROWS, ROWS)

    @pl.when(pl.program_id(0) == 0)
    def _():
        hid[...] = hidden_of(pick(starts, lat_own, lat_oth)[0], w1[...])

    step = pl.program_id(0)
    there = pl.ds(pl.multiple_of(ctx * HALF + step * GROUP * HEAD, GROUP * HEAD), GROUP * HEAD)
    for full, a, b in ((q, q_own, q_oth), (k, k_own, k_oth), (v, v_own, v_oth), (g, g_own, g_oth)):
        full[pl.ds(own, ROWS), :] = a[...]
        full[pl.ds(oth, ROWS), :] = b[:, there]
    unit = eye(HEAD)
    waiting = []
    for h in range(GROUP):
        cols = slice(HEAD * h, HEAD * h + HEAD)
        shared = {}
        for b in (1, 0):
            waiting.append(chain(q, k, v, g, att, dq, dk, dv, cols, b, unit, shared))
    running = []
    while waiting or running:
        if waiting:
            running.append(waiting.pop(0))
        running = [item for item in running if next(item, "end") != "end"]
    mine = pl.ds(own, ROWS)
    theirs = pl.ds(oth, ROWS)
    for full, keep, send in ((dq, dq_out, dq_send), (dk, dk_out, dk_send), (dv, dv_out, dv_send)):
        keep[...] = full[mine, :]
        send[...] = full[theirs, :]
    att_send[...] = att[theirs, :]
    add_residual(ctx, lay_out, att[mine, :], hid[...], w2[...], text[...])


def add_residual(ctx, lay_out, att, hid, w2, text):
    lay_out[...] = att
    image_rows = pl.ds(pl.multiple_of(ctx * SPAN, SPAN), SPAN)
    text_rows = pl.ds(pl.multiple_of(SPAN - ctx * SPAN, SPAN), SPAN)
    embedding = dot(hid, w2, 1, 0).astype(BF16).astype(F32)
    lay_out[image_rows, :] = (embedding + lay_out[image_rows, :].astype(F32)).astype(BF16)
    lay_out[text_rows, :] = (text.astype(F32) + lay_out[text_rows, :].astype(F32)).astype(BF16)


def place_body(ctx_ref, *refs):
    count = len(refs) // 3
    width = refs[-1].shape[1]
    cols = pl.ds(pl.multiple_of(pl.program_id(0) * width, width), width)
    for i in range(count):
        refs[2 * count + i][...] = refs[i][:, cols]


def merge_body(ctx_ref, starts, text, lat_own, lat_oth, w1, w2, att, lay_in, lay_out, hid):
    @pl.when(pl.program_id(0) == 0)
    def _():
        hid[...] = hidden_of(pick(starts, lat_own, lat_oth)[0], w1[...])

    width = lay_out.shape[1]
    cols = pl.ds(pl.multiple_of(pl.program_id(0) * width, width), width)
    add_residual(ctx_ref[0], lay_out, att[:, cols], hid[...], w2[...], text[...])


def local(queries, keys, values, residual, grad_out, latents, image_starts, w_first, w_second):
    ctx = lax.axis_index("ctx").astype(jnp.int32)
    scalars = (ctx[None], image_starts.reshape(2))
    swap = [(0, 1), (1, 0)]

    def swapped(value):
        return lax.ppermute(value, "ctx", swap)

    q_rows, k_rows, v_rows, g_rows, r_rows = queries[0], keys[0], values[0], grad_out[0], residual[0]
    lat_own = latents[0, 0]
    lat_oth = swapped(lat_own)
    g_oth = swapped(g_rows)
    lat_oth, g_oth, *rows = lax.optimization_barrier((lat_oth, g_oth, q_rows, k_rows, v_rows))
    q_oth, k_oth, v_oth = [swapped(value) for value in rows]

    struct = jax.ShapeDtypeStruct
    anywhere = pl.BlockSpec(memory_space=pl.ANY)
    near = pl.BlockSpec(memory_space=pltpu.VMEM)

    def place_near(value):
        return pltpu.with_memory_space_constraint(value, pltpu.VMEM)

    def near_call(body, args, outs):
        return pl.pallas_call(
            body, in_specs=[near] * len(args), out_specs=[near] * len(outs),
            out_shape=[pltpu.VMEM(shape, BF16) for shape in outs],
        )(*[place_near(value) for value in args])

    lat_spec = whole((32, SPAN))
    payload, = call(
        weight_body, scalars, (lat_own, place_near(lat_oth), w_first, w_second, g_rows, place_near(g_oth)),
        [anywhere, near, anywhere, anywhere, anywhere, near], [near], [pltpu.VMEM((GROUPS, 9, 16, 128), BF16)],
        scratch=[pltpu.VMEM((32, SPAN), BF16), pltpu.VMEM((32, CH), BF16), pltpu.VMEM((CH, WIDTH), BF16),
                 pltpu.VMEM((ROWS, WIDTH), BF16), pltpu.SemaphoreType.DMA((4,))],
    )
    block = ("zl", "y", "x")
    payload, v_oth = lax.optimization_barrier((payload, v_oth))
    q_oth, k_oth, v_oth, g_oth = [place_near(value) for value in (q_oth, k_oth, v_oth, g_oth)]
    got = lax.all_to_all(payload, block, 0, 0, tiled=False)

    cols = GROUP * HEAD
    steps = HEADS // GROUP
    own_spec = pl.BlockSpec((ROWS, cols), lambda i, c, s: (0, c[0] * steps + i))
    send_spec = pl.BlockSpec((ROWS, cols), lambda i, c, s: (0, i))
    big = struct((ROWS, WIDTH), BF16)
    small = struct((ROWS, HALF), BF16)
    result = call(
        attention_body, scalars,
        (q_rows, q_oth, k_rows, k_oth, v_rows, v_oth, g_rows, g_oth, r_rows, lat_own, lat_oth, w_first, w_second),
        [own_spec, near] * 4
        + [pl.BlockSpec((SPAN, cols), lambda i, c, s: (1 - c[0], c[0] * steps + i)),
           lat_spec, lat_spec, whole((32, CH)), pl.BlockSpec((CH, cols), lambda i, c, s: (0, c[0] * steps + i))],
        [own_spec] * 4 + [send_spec] * 4,
        [big] * 4 + [small] * 4,
        grid=(steps,),
        scratch=[pltpu.VMEM((SEQ, cols), BF16)] * 8 + [pltpu.VMEM((SPAN, CH), BF16)],
    )
    lay, dq, dk, dv = result[:4]
    sent_att, sent_dq, sent_dk, sent_dv = [swapped(value) for value in result[4:]]

    parts = 2
    width = HALF // parts
    half_spec = pl.BlockSpec((ROWS, width), lambda i, c, *_: (0, (1 - c[0]) * parts + i))

    def placed(got, into):
        count = len(got)
        return call(
            place_body, scalars[:1], (*map(place_near, got), *into), [near] * count + [anywhere] * count, [half_spec] * count,
            [big] * count, grid=(parts,), aliases={1 + count + i: i for i in range(count)},
        )

    def exchanged(value, turn):
        pairs = []
        for z in range(4):
            for core in range(2):
                other = (z + 2) % 4 if core == turn else z ^ 1
                pairs.append((2 * z + core, 2 * other + core))
        return lax.ppermute(value, ("zh", "ctx"), pairs)

    one, = near_call(group_sum_body, (got,), [(9, 16, 128)])
    one, sent_dq, sent_dk = lax.optimization_barrier((one, sent_dq, sent_dk))
    two = exchanged(one, 0)
    dq, dk = placed((sent_dq, sent_dk), (dq, dk))
    two, dq, dk = lax.optimization_barrier((two, dq, dk))
    one, = near_call(pair_sum_body, (one, two), [(9, 16, 128)])
    one, sent_dv = lax.optimization_barrier((one, sent_dv))
    two = exchanged(one, 1)
    dv, = placed((sent_dv,), (dv,))
    two, dv = lax.optimization_barrier((two, dv))
    sums, = near_call(spread_sum_body, (one, two), [(GROUPS, 9, 16, 128)])
    sums, sent_att = lax.optimization_barrier((sums, sent_att))
    got = lax.all_to_all(sums, block, 0, 0, tiled=False)
    sum_second, sum_first = pl.pallas_call(
        finish_body, in_specs=[near], out_specs=[anywhere, anywhere],
        out_shape=[struct((CH, HALF), F32), struct((32, CH), F32)],
        scratch_shapes=[pltpu.VMEM((CH, HALF), F32), pltpu.VMEM((32, CH), F32), pltpu.SemaphoreType.DMA((5,))],
        compiler_params=pltpu.CompilerParams(vmem_limit_bytes=VMEM),
    )(place_near(got))

    lay = call(
        merge_body, scalars, (r_rows, lat_own, lat_oth, w_first, w_second, place_near(sent_att), lay),
        [pl.BlockSpec((SPAN, width), lambda i, c, s: (1 - c[0], (1 - c[0]) * parts + i)), lat_spec, lat_spec,
         whole((32, CH)), pl.BlockSpec((CH, width), lambda i, c, s: (0, (1 - c[0]) * parts + i)),
         near, anywhere],
        half_spec, big, grid=(parts,), scratch=[pltpu.VMEM((SPAN, CH), BF16)], aliases={8: 0},
    )
    outs = (lay, dq, dk, dv)
    return (*[value[None] for value in outs], sum_first, sum_second)


def solution(mesh):
    axes = Mesh(mesh.devices.reshape(4, 2, 4, 4, 2), ("zh", "zl", "y", "x", "ctx"))
    dp = ("zh", "zl", "y", "x")
    rows = P(dp, "ctx", None)
    return jax.shard_map(
        local,
        mesh=axes,
        in_specs=(rows, rows, rows, rows, rows, P(dp, "ctx", None, None), P(dp, None), P(), P()),
        out_specs=(rows, rows, rows, rows, P(), P(None, "ctx")),
        check_vma=False,
    )
```

```python
import math

import jax
import jax.numpy as jnp
from jax import lax
from jax.experimental import pallas as pl
from jax.experimental.pallas import tpu as pltpu
from jax.sharding import Mesh
from jax.sharding import PartitionSpec as P

HEAD = 128
SPAN = 128
ROWS = 256
HALF = 1024
WIDTH = 2048
SEQ = 512
CH = 512
HEADS = 8
GROUP = 4
GROUPS = 32
VMEM = 56 * 1024 * 1024

F32 = jnp.float32
BF16 = jnp.bfloat16


def dot(a, b, ca, cb):
    return lax.dot_general(a, b, (((ca,), (cb,)), ((), ())), preferred_element_type=F32)


def whole(shape):
    return pl.BlockSpec(shape, lambda *_: (0,) * len(shape))


def call(body, scalars, args, in_specs, out_specs, out_shape, grid=(1,), scratch=(), aliases=None):
    return pl.pallas_call(
        body,
        grid_spec=pltpu.PrefetchScalarGridSpec(
            num_scalar_prefetch=len(scalars),
            grid=grid,
            in_specs=in_specs,
            out_specs=out_specs,
            scratch_shapes=scratch,
        ),
        out_shape=out_shape,
        input_output_aliases=aliases or {},
        compiler_params=pltpu.CompilerParams(vmem_limit_bytes=VMEM),
    )(*scalars, *args)


def sigmoid(v):
    return 1.0 / (1.0 + jnp.exp(-v))


def eye(n):
    rows = lax.broadcasted_iota(jnp.int32, (n, n), 0)
    cols = lax.broadcasted_iota(jnp.int32, (n, n), 1)
    return (rows == cols).astype(F32).astype(BF16)


def pick(starts, lat_own, lat_oth):
    in_order = starts[0] == 0
    one, two = lat_own[...].astype(F32), lat_oth[...].astype(F32)
    return jnp.where(in_order, one, two).astype(BF16), jnp.where(in_order, two, one).astype(BF16)


def weight_body(ctx_ref, starts, lat_hbm, lat_oth, w1_hbm, w2_hbm, g_own, g_oth, out, lat_own, w1, w2, grads, sems):
    ctx = ctx_ref[0]
    own_rows = pl.ds(pl.multiple_of(ctx * SPAN, SPAN), SPAN)
    oth_rows = pl.ds(pl.multiple_of(SPAN - ctx * SPAN, SPAN), SPAN)
    copies = [
        pltpu.make_async_copy(source, target, sems.at[i])
        for i, (source, target) in enumerate((
            (lat_hbm, lat_own), (w1_hbm, w1), (g_own.at[own_rows, :], grads.at[0:SPAN, :]), (w2_hbm, w2)))
    ]
    for copy in copies:
        copy.start()
    grads[SPAN:ROWS, :] = g_oth[oth_rows, :]
    copies[0].wait()
    copies[1].wait()
    patches = jnp.concatenate(pick(starts, lat_own, lat_oth), axis=1)
    pre = dot(w1[...], patches, 0, 0)
    sig = sigmoid(pre)
    hid_t = (pre * sig).astype(BF16)
    copies[2].wait()
    for n in range(4):
        half = grads[:, pl.ds(pl.multiple_of(ctx * HALF, HALF) + 256 * n, 256)]
        strip = dot(hid_t, half, 1, 0).astype(BF16)
        for j in range(GROUPS):
            for i in range(2):
                out[j // 8, j % 8, 2 * n + i] = strip[16 * j : 16 * j + 16, 128 * i : 128 * i + 128]
    copies[3].wait()
    back = dot(w2[...], grads[...], 1, 1)
    grad_pre = (back * sig * (1.0 + pre * (1.0 - sig))).astype(BF16)
    first = dot(patches, grad_pre, 1, 1)
    first = first.astype(BF16)
    for j in range(GROUPS):
        m = j // 4
        out[j // 8, j % 8, 8] = first[16 * (m // 4) : 16 * (m // 4) + 16, 128 * (m % 4) : 128 * (m % 4) + 128]


def group_sum_body(got, out):
    total = got[0].astype(F32)
    for j in range(1, got.shape[0]):
        total = total + got[j].astype(F32)
    out[...] = total.astype(BF16)


def pair_sum_body(one, two, out):
    out[...] = (one[...].astype(F32) + two[...].astype(F32)).astype(BF16)


def spread_sum_body(one, two, out):
    total = (one[...].astype(F32) + two[...].astype(F32)).astype(BF16)
    for j in range(out.shape[0]):
        out[j] = total


def spread_body(part, out):
    for j in range(out.shape[0]):
        out[j] = part[...]


def finish_body(got, second, first, second_near, first_near, sems):
    copies = []
    for n in range(4):
        for j in range(8 * n, 8 * n + 8):
            for t in range(8):
                second_near[16 * j : 16 * j + 16, 128 * t : 128 * t + 128] = got[j // 8, j % 8, t].astype(F32) * (1.0 / 128.0)
        part = pl.ds(128 * n, 128)
        copies.append(pltpu.make_async_copy(second_near.at[part, :], second.at[part, :], sems.at[n]))
        copies[-1].start()
    for m in range(8):
        rows, cols = 16 * (m // 4), 128 * (m % 4)
        first_near[rows : rows + 16, cols : cols + 128] = got[m // 2, 4 * (m % 2), 8].astype(F32) * (1.0 / 128.0)
    copies.append(pltpu.make_async_copy(first_near, first, sems.at[4]))
    copies[-1].start()
    for copy in copies:
        copy.wait()


def chain(q, k, v, g, att, dq, dk, dv, cols, b, unit, shared):
    scale = HEAD ** -0.5
    power = scale * math.log2(math.e)
    seen = ROWS * (b + 1)
    rows = slice(ROWS * b, ROWS * b + ROWS)
    qb = q[rows, cols]
    gb = g[rows, cols]
    scores = dot(k[0:seen, cols], qb, 1, 1)
    dp = dot(v[0:seen, cols], gb, 1, 1)
    if b == 1:
        shared["k_t"] = dot(unit, k[:, cols], 1, 1).astype(BF16)
        shared["v_t"] = dot(unit, v[:, cols], 1, 1).astype(BF16)
    yield
    key_pos = lax.broadcasted_iota(jnp.int32, (ROWS, ROWS), 0)
    query_pos = lax.broadcasted_iota(jnp.int32, (ROWS, ROWS), 1)
    if b == 0:
        limit = jnp.where(query_pos < SPAN, SPAN - 1, query_pos)
    else:
        limit = jnp.where(query_pos < SPAN, query_pos, ROWS - 1)
    last = jnp.where(key_pos <= limit, scores[seen - ROWS : seen], -1e30)
    scores = last if b == 0 else jnp.concatenate([scores[0:ROWS], last], axis=0)
    top = jnp.max(scores, axis=0, keepdims=True)
    yield
    e = jnp.exp2((scores - top) * power)
    total = jnp.sum(e, axis=0, keepdims=True)
    yield
    p = e * (1.0 / total)
    pb = p.astype(BF16)
    u = p * dp
    out_dot = jnp.sum(u, axis=0, keepdims=True)
    yield
    ds = (u - p * out_dot).astype(BF16)
    att_t = dot(shared["v_t"][:, 0:seen], pb, 1, 0)
    new_v = dot(pb, gb, 1, 0)
    yield
    dq_t = dot(shared["k_t"][:, 0:seen], ds, 1, 0) * scale
    new_k = dot(ds, qb, 1, 0)
    att[rows, cols] = jnp.transpose(att_t).astype(BF16)
    yield
    dq[rows, cols] = jnp.transpose(dq_t).astype(BF16)
    if b == 1:
        shared["dk"] = new_k[0:ROWS]
        shared["dv"] = new_v[0:ROWS]
    else:
        new_k = new_k + shared["dk"]
        new_v = new_v + shared["dv"]
    dk[rows, cols] = (new_k[seen - ROWS : seen] * scale).astype(BF16)
    dv[rows, cols] = new_v[seen - ROWS : seen].astype(BF16)


def near_groups():
    def chip(half, place):
        return place if half == 0 else 3 - place

    def device(zl, halves, places, core):
        return ((zl * 4 + chip(halves // 2, places // 2)) * 4 + chip(halves % 2, places % 2)) * 2 + core

    four = [[device(zl, h, p, 0) for p in range(4)] for zl in range(2) for h in range(4)]
    four += [[device(zl, h, p, 1) for h in range(4)] for zl in range(2) for p in range(4)]
    eight = [[device(zl, h, p, 0) for zl in range(2) for h in range(4)] for p in range(4)]
    eight += [[device(zl, h, p, 1) for zl in range(2) for p in range(4)] for h in range(4)]
    return four, eight


def hidden_of(lat, w1):
    pre = dot(lat, w1, 0, 0)
    return (pre * sigmoid(pre)).astype(BF16)


def attention_body(ctx_ref, starts, q_own, q_oth, k_own, k_oth, v_own, v_oth, g_own, g_oth, text, lat_own, lat_oth, w1, w2,
                   lay_out, dq_out, dk_out, dv_out, att_send, dq_send, dk_send, dv_send,
                   q, k, v, g, att, dq, dk, dv, hid):
    ctx = ctx_ref[0]
    own = pl.multiple_of(ctx * ROWS, ROWS)
    oth = pl.multiple_of(ROWS - ctx * ROWS, ROWS)

    @pl.when(pl.program_id(0) == 0)
    def _():
        hid[...] = hidden_of(pick(starts, lat_own, lat_oth)[0], w1[...])

    step = pl.program_id(0)
    there = pl.ds(pl.multiple_of(ctx * HALF + step * GROUP * HEAD, GROUP * HEAD), GROUP * HEAD)
    for full, a, b in ((q, q_own, q_oth), (k, k_own, k_oth), (v, v_own, v_oth), (g, g_own, g_oth)):
        full[pl.ds(own, ROWS), :] = a[...]
        full[pl.ds(oth, ROWS), :] = b[:, there]
    unit = eye(HEAD)
    waiting = []
    for h in range(GROUP):
        cols = slice(HEAD * h, HEAD * h + HEAD)
        shared = {}
        for b in (1, 0):
            waiting.append(chain(q, k, v, g, att, dq, dk, dv, cols, b, unit, shared))
    running = []
    while waiting or running:
        if waiting:
            running.append(waiting.pop(0))
        running = [item for item in running if next(item, "end") != "end"]
    mine = pl.ds(own, ROWS)
    theirs = pl.ds(oth, ROWS)
    for full, keep, send in ((dq, dq_out, dq_send), (dk, dk_out, dk_send), (dv, dv_out, dv_send)):
        keep[...] = full[mine, :]
        send[...] = full[theirs, :]
    att_send[...] = att[theirs, :]
    add_residual(ctx, lay_out, att[mine, :], hid[...], w2[...], text[...])


def add_residual(ctx, lay_out, att, hid, w2, text):
    lay_out[...] = att
    image_rows = pl.ds(pl.multiple_of(ctx * SPAN, SPAN), SPAN)
    text_rows = pl.ds(pl.multiple_of(SPAN - ctx * SPAN, SPAN), SPAN)
    embedding = dot(hid, w2, 1, 0).astype(BF16).astype(F32)
    lay_out[image_rows, :] = (embedding + lay_out[image_rows, :].astype(F32)).astype(BF16)
    lay_out[text_rows, :] = (text.astype(F32) + lay_out[text_rows, :].astype(F32)).astype(BF16)


def place_body(ctx_ref, *refs):
    count = len(refs) // 3
    width = refs[-1].shape[1]
    cols = pl.ds(pl.multiple_of(pl.program_id(0) * width, width), width)
    for i in range(count):
        refs[2 * count + i][...] = refs[i][:, cols]


def merge_body(ctx_ref, starts, text, lat_own, lat_oth, w1, w2, att, lay_in, lay_out, hid):
    @pl.when(pl.program_id(0) == 0)
    def _():
        hid[...] = hidden_of(pick(starts, lat_own, lat_oth)[0], w1[...])

    width = lay_out.shape[1]
    cols = pl.ds(pl.multiple_of(pl.program_id(0) * width, width), width)
    add_residual(ctx_ref[0], lay_out, att[:, cols], hid[...], w2[...], text[...])


def local(queries, keys, values, residual, grad_out, latents, image_starts, w_first, w_second):
    ctx = lax.axis_index("ctx").astype(jnp.int32)
    scalars = (ctx[None], image_starts.reshape(2))
    swap = [(0, 1), (1, 0)]

    def swapped(value):
        return lax.ppermute(value, "ctx", swap)

    q_rows, k_rows, v_rows, g_rows, r_rows = queries[0], keys[0], values[0], grad_out[0], residual[0]
    lat_own = latents[0, 0]
    lat_oth = swapped(lat_own)
    g_oth = swapped(g_rows)
    lat_oth, g_oth, *rows = lax.optimization_barrier((lat_oth, g_oth, q_rows, k_rows, v_rows))
    q_oth, k_oth, v_oth = [swapped(value) for value in rows]

    struct = jax.ShapeDtypeStruct
    anywhere = pl.BlockSpec(memory_space=pl.ANY)
    near = pl.BlockSpec(memory_space=pltpu.VMEM)

    def place_near(value):
        return pltpu.with_memory_space_constraint(value, pltpu.VMEM)

    def near_call(body, args, outs):
        return pl.pallas_call(
            body, in_specs=[near] * len(args), out_specs=[near] * len(outs),
            out_shape=[pltpu.VMEM(shape, BF16) for shape in outs],
        )(*[place_near(value) for value in args])

    lat_spec = whole((32, SPAN))
    payload, = call(
        weight_body, scalars, (lat_own, place_near(lat_oth), w_first, w_second, g_rows, place_near(g_oth)),
        [anywhere, near, anywhere, anywhere, anywhere, near], [near], [pltpu.VMEM((4, 8, 9, 16, 128), BF16)],
        scratch=[pltpu.VMEM((32, SPAN), BF16), pltpu.VMEM((32, CH), BF16), pltpu.VMEM((CH, WIDTH), BF16),
                 pltpu.VMEM((ROWS, WIDTH), BF16), pltpu.SemaphoreType.DMA((4,))],
    )
    four, eight = near_groups()

    def traded(value, groups):
        return lax.all_to_all(value, ("zl", "y", "x", "ctx"), 0, 0, axis_index_groups=groups, tiled=False)

    q_oth, k_oth, v_oth, g_oth = [place_near(value) for value in (q_oth, k_oth, v_oth, g_oth)]
    got = traded(payload, four)

    cols = GROUP * HEAD
    steps = HEADS // GROUP
    own_spec = pl.BlockSpec((ROWS, cols), lambda i, c, s: (0, c[0] * steps + i))
    send_spec = pl.BlockSpec((ROWS, cols), lambda i, c, s: (0, i))
    big = struct((ROWS, WIDTH), BF16)
    small = struct((ROWS, HALF), BF16)
    result = call(
        attention_body, scalars,
        (q_rows, q_oth, k_rows, k_oth, v_rows, v_oth, g_rows, g_oth, r_rows, lat_own, lat_oth, w_first, w_second),
        [own_spec, near] * 4
        + [pl.BlockSpec((SPAN, cols), lambda i, c, s: (1 - c[0], c[0] * steps + i)),
           lat_spec, lat_spec, whole((32, CH)), pl.BlockSpec((CH, cols), lambda i, c, s: (0, c[0] * steps + i))],
        [own_spec] * 4 + [send_spec] * 4,
        [big] * 4 + [small] * 4,
        grid=(steps,),
        scratch=[pltpu.VMEM((SEQ, cols), BF16)] * 8 + [pltpu.VMEM((SPAN, CH), BF16)],
    )
    got, *result = lax.optimization_barrier((got, *result))
    lay, dq, dk, dv = result[:4]
    sent_att, sent_dq, sent_dk, sent_dv = [swapped(value) for value in result[4:]]

    parts = 2
    width = HALF // parts
    half_spec = pl.BlockSpec((ROWS, width), lambda i, c, *_: (0, (1 - c[0]) * parts + i))

    def placed(after, got, into):
        count = len(got)
        return call(
            place_body, (after,), (*map(place_near, got), *into), [near] * count + [anywhere] * count,
            [half_spec] * count, [big] * count, grid=(parts,), aliases={1 + count + i: i for i in range(count)},
        )

    def exchanged(value, turn):
        pairs = []
        for z in range(4):
            for core in range(2):
                other = (z + 2) % 4 if core == turn else z ^ 1
                pairs.append((2 * z + core, 2 * other + core))
        return lax.ppermute(value, ("zh", "ctx"), pairs)

    part, = near_call(group_sum_body, (got,), [(8, 9, 16, 128)])
    one, = near_call(group_sum_body, (traded(part, eight),), [(9, 16, 128)])
    one, after = lax.optimization_barrier((one, scalars[0]))
    two = exchanged(one, 0)
    dq, dk = placed(after, (sent_dq, sent_dk), (dq, dk))
    two, dq, dk = lax.optimization_barrier((two, dq, dk))
    one, = near_call(pair_sum_body, (one, two), [(9, 16, 128)])
    two = exchanged(one, 1)
    part, = near_call(spread_sum_body, (one, two), [(8, 9, 16, 128)])
    part, after = lax.optimization_barrier((part, after))
    part = traded(part, eight)
    dv, = placed(after, (sent_dv,), (dv,))
    part, dv = lax.optimization_barrier((part, dv))
    sums, = near_call(spread_body, (part,), [(4, 8, 9, 16, 128)])
    sums, after = lax.optimization_barrier((sums, after))
    got = traded(sums, four)
    sum_second, sum_first = pl.pallas_call(
        finish_body, in_specs=[near], out_specs=[anywhere, anywhere],
        out_shape=[struct((CH, HALF), F32), struct((32, CH), F32)],
        scratch_shapes=[pltpu.VMEM((CH, HALF), F32), pltpu.VMEM((32, CH), F32), pltpu.SemaphoreType.DMA((5,))],
        compiler_params=pltpu.CompilerParams(vmem_limit_bytes=VMEM),
    )(place_near(got))

    lay = call(
        merge_body, (after, scalars[1]), (r_rows, lat_own, lat_oth, w_first, w_second, place_near(sent_att), lay),
        [pl.BlockSpec((SPAN, width), lambda i, c, s: (1 - c[0], (1 - c[0]) * parts + i)), lat_spec, lat_spec,
         whole((32, CH)), pl.BlockSpec((CH, width), lambda i, c, s: (0, (1 - c[0]) * parts + i)),
         near, anywhere],
        half_spec, big, grid=(parts,), scratch=[pltpu.VMEM((SPAN, CH), BF16)], aliases={8: 0},
    )
    outs = (lay, dq, dk, dv)
    return (*[value[None] for value in outs], sum_first, sum_second)


def solution(mesh):
    axes = Mesh(mesh.devices.reshape(4, 2, 4, 4, 2), ("zh", "zl", "y", "x", "ctx"))
    dp = ("zh", "zl", "y", "x")
    rows = P(dp, "ctx", None)
    return jax.shard_map(
        local,
        mesh=axes,
        in_specs=(rows, rows, rows, rows, rows, P(dp, "ctx", None, None), P(dp, None), P(), P()),
        out_specs=(rows, rows, rows, rows, P(), P(None, "ctx")),
        check_vma=False,
    )
```

```python
import math

import jax
import jax.numpy as jnp
from jax import lax
from jax.experimental import pallas as pl
from jax.experimental.pallas import tpu as pltpu
from jax.sharding import Mesh
from jax.sharding import PartitionSpec as P

HEAD = 128
SPAN = 128
ROWS = 256
HALF = 1024
WIDTH = 2048
SEQ = 512
CH = 512
HEADS = 8
GROUP = 4
GROUPS = 32
VMEM = 56 * 1024 * 1024

F32 = jnp.float32
BF16 = jnp.bfloat16


def dot(a, b, ca, cb):
    return lax.dot_general(a, b, (((ca,), (cb,)), ((), ())), preferred_element_type=F32)


def whole(shape):
    return pl.BlockSpec(shape, lambda *_: (0,) * len(shape))


def call(body, scalars, args, in_specs, out_specs, out_shape, grid=(1,), scratch=(), aliases=None, cost=None):
    return pl.pallas_call(
        body,
        grid_spec=pltpu.PrefetchScalarGridSpec(
            num_scalar_prefetch=len(scalars),
            grid=grid,
            in_specs=in_specs,
            out_specs=out_specs,
            scratch_shapes=scratch,
        ),
        out_shape=out_shape,
        input_output_aliases=aliases or {},
        cost_estimate=cost,
        compiler_params=pltpu.CompilerParams(vmem_limit_bytes=VMEM),
    )(*scalars, *args)


def sigmoid(v):
    return 1.0 / (1.0 + jnp.exp(-v))


def eye(n):
    rows = lax.broadcasted_iota(jnp.int32, (n, n), 0)
    cols = lax.broadcasted_iota(jnp.int32, (n, n), 1)
    return (rows == cols).astype(F32).astype(BF16)


def pick(starts, lat_own, lat_oth):
    in_order = starts[0] == 0
    one, two = lat_own[...].astype(F32), lat_oth[...].astype(F32)
    return jnp.where(in_order, one, two).astype(BF16), jnp.where(in_order, two, one).astype(BF16)


def weight_body(ctx_ref, starts, lat_hbm, lat_oth, w1_hbm, w2_hbm, g_own, g_oth, out, lat_own, w1, w2, grads, sems):
    ctx = ctx_ref[0]
    own_rows = pl.ds(pl.multiple_of(ctx * SPAN, SPAN), SPAN)
    oth_rows = pl.ds(pl.multiple_of(SPAN - ctx * SPAN, SPAN), SPAN)
    copies = [
        pltpu.make_async_copy(source, target, sems.at[i])
        for i, (source, target) in enumerate((
            (lat_hbm, lat_own), (w1_hbm, w1), (g_own.at[own_rows, :], grads.at[0:SPAN, :]), (w2_hbm, w2)))
    ]
    for copy in copies:
        copy.start()
    grads[SPAN:ROWS, :] = g_oth[oth_rows, :]
    copies[0].wait()
    copies[1].wait()
    patches = jnp.concatenate(pick(starts, lat_own, lat_oth), axis=1)
    pre = dot(w1[...], patches, 0, 0)
    sig = sigmoid(pre)
    hid_t = (pre * sig).astype(BF16)
    copies[2].wait()
    for n in range(4):
        half = grads[:, pl.ds(pl.multiple_of(ctx * HALF, HALF) + 256 * n, 256)]
        strip = dot(hid_t, half, 1, 0).astype(BF16)
        for j in range(GROUPS):
            for i in range(2):
                out[j, 2 * n + i] = strip[16 * j : 16 * j + 16, 128 * i : 128 * i + 128]
    copies[3].wait()
    back = dot(w2[...], grads[...], 1, 1)
    grad_pre = (back * sig * (1.0 + pre * (1.0 - sig))).astype(BF16)
    first = dot(patches, grad_pre, 1, 1)
    first = first.astype(BF16)
    for j in range(GROUPS):
        m = j // 4
        out[j, 8] = first[16 * (m // 4) : 16 * (m // 4) + 16, 128 * (m % 4) : 128 * (m % 4) + 128]


def group_sum_body(got, out):
    total = got[0].astype(F32)
    for j in range(1, GROUPS):
        total = total + got[j].astype(F32)
    out[...] = total.astype(BF16)


def pair_sum_body(one, two, out):
    out[...] = (one[...].astype(F32) + two[...].astype(F32)).astype(BF16)


def spread_sum_body(one, two, out):
    total = (one[...].astype(F32) + two[...].astype(F32)).astype(BF16)
    for j in range(GROUPS):
        out[j] = total


def finish_body(got, second, first, second_near, first_near, sems):
    copies = []
    for n in range(4):
        for j in range(8 * n, 8 * n + 8):
            for t in range(8):
                second_near[16 * j : 16 * j + 16, 128 * t : 128 * t + 128] = got[j, t].astype(F32) * (1.0 / 128.0)
        part = pl.ds(128 * n, 128)
        copies.append(pltpu.make_async_copy(second_near.at[part, :], second.at[part, :], sems.at[n]))
        copies[-1].start()
    for m in range(8):
        rows, cols = 16 * (m // 4), 128 * (m % 4)
        first_near[rows : rows + 16, cols : cols + 128] = got[4 * m, 8].astype(F32) * (1.0 / 128.0)
    copies.append(pltpu.make_async_copy(first_near, first, sems.at[4]))
    copies[-1].start()
    for copy in copies:
        copy.wait()


def chain(q, k, v, g, att, dq, dk, dv, cols, b, unit, shared):
    scale = HEAD ** -0.5
    power = scale * math.log2(math.e)
    seen = ROWS * (b + 1)
    rows = slice(ROWS * b, ROWS * b + ROWS)
    qb = q[rows, cols]
    gb = g[rows, cols]
    scores = dot(k[0:seen, cols], qb, 1, 1)
    dp = dot(v[0:seen, cols], gb, 1, 1)
    if b == 1:
        shared["k_t"] = dot(unit, k[:, cols], 1, 1).astype(BF16)
        shared["v_t"] = dot(unit, v[:, cols], 1, 1).astype(BF16)
    yield
    key_pos = lax.broadcasted_iota(jnp.int32, (ROWS, ROWS), 0)
    query_pos = lax.broadcasted_iota(jnp.int32, (ROWS, ROWS), 1)
    if b == 0:
        limit = jnp.where(query_pos < SPAN, SPAN - 1, query_pos)
    else:
        limit = jnp.where(query_pos < SPAN, query_pos, ROWS - 1)
    last = jnp.where(key_pos <= limit, scores[seen - ROWS : seen], -1e30)
    scores = last if b == 0 else jnp.concatenate([scores[0:ROWS], last], axis=0)
    top = jnp.max(scores, axis=0, keepdims=True)
    yield
    e = jnp.exp2((scores - top) * power)
    total = jnp.sum(e, axis=0, keepdims=True)
    yield
    p = e * (1.0 / total)
    pb = p.astype(BF16)
    u = p * dp
    out_dot = jnp.sum(u, axis=0, keepdims=True)
    yield
    ds = (u - p * out_dot).astype(BF16)
    att_t = dot(shared["v_t"][:, 0:seen], pb, 1, 0)
    new_v = dot(pb, gb, 1, 0)
    yield
    dq_t = dot(shared["k_t"][:, 0:seen], ds, 1, 0) * scale
    new_k = dot(ds, qb, 1, 0)
    att[rows, cols] = jnp.transpose(att_t).astype(BF16)
    yield
    dq[rows, cols] = jnp.transpose(dq_t).astype(BF16)
    if b == 1:
        shared["dk"] = new_k[0:ROWS]
        shared["dv"] = new_v[0:ROWS]
    else:
        new_k = new_k + shared["dk"]
        new_v = new_v + shared["dv"]
    dk[rows, cols] = (new_k[seen - ROWS : seen] * scale).astype(BF16)
    dv[rows, cols] = new_v[seen - ROWS : seen].astype(BF16)


def hidden_of(lat, w1):
    pre = dot(lat, w1, 0, 0)
    return (pre * sigmoid(pre)).astype(BF16)


def attention_body(ctx_ref, starts, q_own, q_oth, k_own, k_oth, v_own, v_oth, g_own, g_oth, text, lat_own, lat_oth, w1, w2,
                   lay_out, dq_out, dk_out, dv_out, att_send, dq_send, dk_send, dv_send,
                   q, k, v, g, att, dq, dk, dv, hid):
    ctx = ctx_ref[0]
    own = pl.multiple_of(ctx * ROWS, ROWS)
    oth = pl.multiple_of(ROWS - ctx * ROWS, ROWS)

    @pl.when(pl.program_id(0) == 0)
    def _():
        hid[...] = hidden_of(pick(starts, lat_own, lat_oth)[0], w1[...])

    step = pl.program_id(0)
    there = pl.ds(pl.multiple_of(ctx * HALF + step * GROUP * HEAD, GROUP * HEAD), GROUP * HEAD)
    for full, a, b in ((q, q_own, q_oth), (k, k_own, k_oth), (v, v_own, v_oth), (g, g_own, g_oth)):
        full[pl.ds(own, ROWS), :] = a[...]
        full[pl.ds(oth, ROWS), :] = b[:, there]
    unit = eye(HEAD)
    waiting = []
    for h in range(GROUP):
        cols = slice(HEAD * h, HEAD * h + HEAD)
        shared = {}
        for b in (1, 0):
            waiting.append(chain(q, k, v, g, att, dq, dk, dv, cols, b, unit, shared))
    running = []
    while waiting or running:
        if waiting:
            running.append(waiting.pop(0))
        running = [item for item in running if next(item, "end") != "end"]
    mine = pl.ds(own, ROWS)
    theirs = pl.ds(oth, ROWS)
    for full, keep, send in ((dq, dq_out, dq_send), (dk, dk_out, dk_send), (dv, dv_out, dv_send)):
        keep[...] = full[mine, :]
        send[...] = full[theirs, :]
    att_send[...] = att[theirs, :]
    add_residual(ctx, lay_out, att[mine, :], hid[...], w2[...], text[...])


def add_residual(ctx, lay_out, att, hid, w2, text):
    lay_out[...] = att
    image_rows = pl.ds(pl.multiple_of(ctx * SPAN, SPAN), SPAN)
    text_rows = pl.ds(pl.multiple_of(SPAN - ctx * SPAN, SPAN), SPAN)
    embedding = dot(hid, w2, 1, 0).astype(BF16).astype(F32)
    lay_out[image_rows, :] = (embedding + lay_out[image_rows, :].astype(F32)).astype(BF16)
    lay_out[text_rows, :] = (text.astype(F32) + lay_out[text_rows, :].astype(F32)).astype(BF16)


def place_body(ctx_ref, *refs):
    count = len(refs) // 3
    width = refs[-1].shape[1]
    cols = pl.ds(pl.multiple_of(pl.program_id(0) * width, width), width)
    for i in range(count):
        refs[2 * count + i][...] = refs[i][:, cols]


def merge_body(ctx_ref, starts, text, lat_own, lat_oth, w1, w2, att, lay_in, lay_out, hid):
    @pl.when(pl.program_id(0) == 0)
    def _():
        hid[...] = hidden_of(pick(starts, lat_own, lat_oth)[0], w1[...])

    width = lay_out.shape[1]
    cols = pl.ds(pl.multiple_of(pl.program_id(0) * width, width), width)
    add_residual(ctx_ref[0], lay_out, att[:, cols], hid[...], w2[...], text[...])


def local(queries, keys, values, residual, grad_out, latents, image_starts, w_first, w_second):
    ctx = lax.axis_index("ctx").astype(jnp.int32)
    scalars = (ctx[None], image_starts.reshape(2))
    swap = [(0, 1), (1, 0)]

    def swapped(value):
        return lax.ppermute(value, "ctx", swap)

    q_rows, k_rows, v_rows, g_rows, r_rows = queries[0], keys[0], values[0], grad_out[0], residual[0]
    lat_own = latents[0, 0]
    lat_oth = swapped(lat_own)
    g_oth = swapped(g_rows)
    lat_oth, g_oth, *rows = lax.optimization_barrier((lat_oth, g_oth, q_rows, k_rows, v_rows))
    q_oth, k_oth, v_oth = [swapped(value) for value in rows]

    struct = jax.ShapeDtypeStruct
    anywhere = pl.BlockSpec(memory_space=pl.ANY)
    near = pl.BlockSpec(memory_space=pltpu.VMEM)

    def place_near(value):
        return pltpu.with_memory_space_constraint(value, pltpu.VMEM)

    def near_call(body, args, outs):
        return pl.pallas_call(
            body, in_specs=[near] * len(args), out_specs=[near] * len(outs),
            out_shape=[pltpu.VMEM(shape, BF16) for shape in outs],
        )(*[place_near(value) for value in args])

    lat_spec = whole((32, SPAN))
    payload, = call(
        weight_body, scalars, (lat_own, place_near(lat_oth), w_first, w_second, g_rows, place_near(g_oth)),
        [anywhere, near, anywhere, anywhere, anywhere, near], [near], [pltpu.VMEM((GROUPS, 9, 16, 128), BF16)],
        scratch=[pltpu.VMEM((32, SPAN), BF16), pltpu.VMEM((32, CH), BF16), pltpu.VMEM((CH, WIDTH), BF16),
                 pltpu.VMEM((ROWS, WIDTH), BF16), pltpu.SemaphoreType.DMA((4,))],
    )
    block = ("zl", "y", "x")
    q_oth, k_oth, v_oth, g_oth = [place_near(value) for value in (q_oth, k_oth, v_oth, g_oth)]
    got = lax.all_to_all(payload, block, 0, 0, tiled=False)

    cols = GROUP * HEAD
    steps = HEADS // GROUP
    own_spec = pl.BlockSpec((ROWS, cols), lambda i, c, s: (0, c[0] * steps + i))
    send_spec = pl.BlockSpec((ROWS, cols), lambda i, c, s: (0, i))
    big = struct((ROWS, WIDTH), BF16)
    small = struct((ROWS, HALF), BF16)
    result = call(
        attention_body, scalars,
        (q_rows, q_oth, k_rows, k_oth, v_rows, v_oth, g_rows, g_oth, r_rows, lat_own, lat_oth, w_first, w_second),
        [own_spec, near] * 4
        + [pl.BlockSpec((SPAN, cols), lambda i, c, s: (1 - c[0], c[0] * steps + i)),
           lat_spec, lat_spec, whole((32, CH)), pl.BlockSpec((CH, cols), lambda i, c, s: (0, c[0] * steps + i))],
        [own_spec] * 4 + [send_spec] * 4,
        [big] * 4 + [small] * 4,
        grid=(steps,),
        scratch=[pltpu.VMEM((SEQ, cols), BF16)] * 8 + [pltpu.VMEM((SPAN, CH), BF16)],
        cost=pl.CostEstimate(flops=40_000_000_000, bytes_accessed=100_000_000, transcendentals=4_000_000),
    )
    lay, dq, dk, dv = result[:4]
    sent_att, sent_dq, sent_dk, sent_dv = [swapped(value) for value in result[4:]]

    parts = 2
    width = HALF // parts
    half_spec = pl.BlockSpec((ROWS, width), lambda i, c, *_: (0, (1 - c[0]) * parts + i))

    def placed(got, into):
        count = len(got)
        return call(
            place_body, scalars[:1], (*map(place_near, got), *into), [near] * count + [anywhere] * count, [half_spec] * count,
            [big] * count, grid=(parts,), aliases={1 + count + i: i for i in range(count)},
        )

    def exchanged(value, turn):
        pairs = []
        for z in range(4):
            for core in range(2):
                other = (z + 2) % 4 if core == turn else z ^ 1
                pairs.append((2 * z + core, 2 * other + core))
        return lax.ppermute(value, ("zh", "ctx"), pairs)

    one, = near_call(group_sum_body, (got,), [(9, 16, 128)])
    two = exchanged(one, 0)
    one, = near_call(pair_sum_body, (one, two), [(9, 16, 128)])
    one, sent_dq, sent_dk, sent_dv = lax.optimization_barrier((one, sent_dq, sent_dk, sent_dv))
    two = exchanged(one, 1)
    dq, dk, dv = placed((sent_dq, sent_dk, sent_dv), (dq, dk, dv))
    two, dq, dk, dv = lax.optimization_barrier((two, dq, dk, dv))
    sums, = near_call(spread_sum_body, (one, two), [(GROUPS, 9, 16, 128)])
    sums, sent_att = lax.optimization_barrier((sums, sent_att))
    got = lax.all_to_all(sums, block, 0, 0, tiled=False)
    sum_second, sum_first = pl.pallas_call(
        finish_body, in_specs=[near], out_specs=[anywhere, anywhere],
        out_shape=[struct((CH, HALF), F32), struct((32, CH), F32)],
        scratch_shapes=[pltpu.VMEM((CH, HALF), F32), pltpu.VMEM((32, CH), F32), pltpu.SemaphoreType.DMA((5,))],
        compiler_params=pltpu.CompilerParams(vmem_limit_bytes=VMEM),
    )(place_near(got))

    lay = call(
        merge_body, scalars, (r_rows, lat_own, lat_oth, w_first, w_second, place_near(sent_att), lay),
        [pl.BlockSpec((SPAN, width), lambda i, c, s: (1 - c[0], (1 - c[0]) * parts + i)), lat_spec, lat_spec,
         whole((32, CH)), pl.BlockSpec((CH, width), lambda i, c, s: (0, (1 - c[0]) * parts + i)),
         near, anywhere],
        half_spec, big, grid=(parts,), scratch=[pltpu.VMEM((SPAN, CH), BF16)], aliases={8: 0},
    )
    outs = (lay, dq, dk, dv)
    return (*[value[None] for value in outs], sum_first, sum_second)


def solution(mesh):
    axes = Mesh(mesh.devices.reshape(4, 2, 4, 4, 2), ("zh", "zl", "y", "x", "ctx"))
    dp = ("zh", "zl", "y", "x")
    rows = P(dp, "ctx", None)
    return jax.shard_map(
        local,
        mesh=axes,
        in_specs=(rows, rows, rows, rows, rows, P(dp, "ctx", None, None), P(dp, None), P(), P()),
        out_specs=(rows, rows, rows, rows, P(), P(None, "ctx")),
        check_vma=False,
    )
```

```python
import math

import jax
import jax.numpy as jnp
from jax import lax
from jax.experimental import pallas as pl
from jax.experimental.pallas import tpu as pltpu
from jax.sharding import Mesh
from jax.sharding import PartitionSpec as P

HEAD = 128
SPAN = 128
ROWS = 256
HALF = 1024
WIDTH = 2048
SEQ = 512
CH = 512
HEADS = 8
GROUP = 4
GROUPS = 32
VMEM = 56 * 1024 * 1024

F32 = jnp.float32
BF16 = jnp.bfloat16


def dot(a, b, ca, cb):
    return lax.dot_general(a, b, (((ca,), (cb,)), ((), ())), preferred_element_type=F32)


def whole(shape):
    return pl.BlockSpec(shape, lambda *_: (0,) * len(shape))


def call(body, scalars, args, in_specs, out_specs, out_shape, grid=(1,), scratch=(), aliases=None, cost=None):
    return pl.pallas_call(
        body,
        grid_spec=pltpu.PrefetchScalarGridSpec(
            num_scalar_prefetch=len(scalars),
            grid=grid,
            in_specs=in_specs,
            out_specs=out_specs,
            scratch_shapes=scratch,
        ),
        out_shape=out_shape,
        input_output_aliases=aliases or {},
        cost_estimate=cost,
        compiler_params=pltpu.CompilerParams(vmem_limit_bytes=VMEM),
    )(*scalars, *args)


def sigmoid(v):
    return 1.0 / (1.0 + jnp.exp(-v))


def eye(n):
    rows = lax.broadcasted_iota(jnp.int32, (n, n), 0)
    cols = lax.broadcasted_iota(jnp.int32, (n, n), 1)
    return (rows == cols).astype(F32).astype(BF16)


def pick(starts, lat_own, lat_oth):
    in_order = starts[0] == 0
    one, two = lat_own[...].astype(F32), lat_oth[...].astype(F32)
    return jnp.where(in_order, one, two).astype(BF16), jnp.where(in_order, two, one).astype(BF16)


def hidden_body(ctx_ref, starts, lat_hbm, lat_oth, w1_hbm, w2_hbm, g_own, patches, hid_t, gate, w2, grads, lat_own, w1, sems):
    own_rows = pl.ds(pl.multiple_of(ctx_ref[0] * SPAN, SPAN), SPAN)
    copies = [
        pltpu.make_async_copy(source, target, sems.at[i])
        for i, (source, target) in enumerate((
            (lat_hbm, lat_own), (w1_hbm, w1), (g_own.at[own_rows, :], grads), (w2_hbm, w2)))
    ]
    for copy in copies:
        copy.start()
    copies[0].wait()
    copies[1].wait()
    both = jnp.concatenate(pick(starts, lat_own, lat_oth), axis=1)
    pre = dot(w1[...], both, 0, 0)
    sig = sigmoid(pre)
    patches[...] = both
    hid_t[...] = (pre * sig).astype(BF16)
    gate[...] = sig * (1.0 + pre * (1.0 - sig))
    copies[2].wait()
    copies[3].wait()


def weight_body(ctx_ref, patches, hid_t, gate, w2, g_own, g_oth, out, grads, tiles, sems):
    ctx = ctx_ref[0]
    oth_rows = pl.ds(pl.multiple_of(SPAN - ctx * SPAN, SPAN), SPAN)
    grads[0:SPAN, :] = g_own[...]
    grads[SPAN:ROWS, :] = g_oth[oth_rows, :]
    for n in range(4):
        half = grads[:, pl.ds(pl.multiple_of(ctx * HALF, HALF) + 256 * n, 256)]
        strip = dot(hid_t[...], half, 1, 0).astype(BF16)
        for j in range(GROUPS):
            for i in range(2):
                tiles[j, 2 * n + i] = strip[16 * j : 16 * j + 16, 128 * i : 128 * i + 128]
    main, rest = pl.ds(0, 8), pl.ds(8, 1)
    copies = [pltpu.make_async_copy(tiles.at[:, part], out.at[:, part], sems.at[i]) for i, part in enumerate((main, rest))]
    copies[0].start()
    back = dot(w2[...], grads[...], 1, 1)
    grad_pre = (back * gate[...]).astype(BF16)
    first = dot(patches[...], grad_pre, 1, 1).astype(BF16)
    for j in range(GROUPS):
        m = j // 4
        tiles[j, 8] = first[16 * (m // 4) : 16 * (m // 4) + 16, 128 * (m % 4) : 128 * (m % 4) + 128]
    copies[1].start()
    copies[0].wait()
    copies[1].wait()


def group_sum_body(got, out):
    total = got[0].astype(F32)
    for j in range(1, GROUPS):
        total = total + got[j].astype(F32)
    out[...] = total.astype(BF16)


def spread_sum_body(one, next1, next2, next3, out):
    even = one[...].astype(F32) + next2[...].astype(F32)
    odd = next1[...].astype(F32) + next3[...].astype(F32)
    total = (even + odd).astype(BF16)
    for j in range(GROUPS):
        out[j] = total


def finish_body(got, second, first, second_near, first_near, sems):
    copies = []
    for n in range(4):
        for j in range(8 * n, 8 * n + 8):
            for t in range(8):
                second_near[16 * j : 16 * j + 16, 128 * t : 128 * t + 128] = got[j, t].astype(F32) * (1.0 / 128.0)
        part = pl.ds(128 * n, 128)
        copies.append(pltpu.make_async_copy(second_near.at[part, :], second.at[part, :], sems.at[n]))
        copies[-1].start()
    for m in range(8):
        rows, cols = 16 * (m // 4), 128 * (m % 4)
        first_near[rows : rows + 16, cols : cols + 128] = got[4 * m, 8].astype(F32) * (1.0 / 128.0)
    copies.append(pltpu.make_async_copy(first_near, first, sems.at[4]))
    copies[-1].start()
    for copy in copies:
        copy.wait()


def chain(q, k, v, g, att, dq, dk, dv, cols, b, unit, shared):
    scale = HEAD ** -0.5
    power = scale * math.log2(math.e)
    seen = ROWS * (b + 1)
    rows = slice(ROWS * b, ROWS * b + ROWS)
    qb = q[rows, cols]
    gb = g[rows, cols]
    scores = dot(k[0:seen, cols], qb, 1, 1)
    dp = dot(v[0:seen, cols], gb, 1, 1)
    if b == 1:
        shared["k_t"] = dot(unit, k[:, cols], 1, 1).astype(BF16)
        shared["v_t"] = dot(unit, v[:, cols], 1, 1).astype(BF16)
    yield
    key_pos = lax.broadcasted_iota(jnp.int32, (ROWS, ROWS), 0)
    query_pos = lax.broadcasted_iota(jnp.int32, (ROWS, ROWS), 1)
    if b == 0:
        limit = jnp.where(query_pos < SPAN, SPAN - 1, query_pos)
    else:
        limit = jnp.where(query_pos < SPAN, query_pos, ROWS - 1)
    last = jnp.where(key_pos <= limit, scores[seen - ROWS : seen], -1e30)
    scores = last if b == 0 else jnp.concatenate([scores[0:ROWS], last], axis=0)
    top = jnp.max(scores, axis=0, keepdims=True)
    yield
    e = jnp.exp2((scores - top) * power)
    total = jnp.sum(e, axis=0, keepdims=True)
    yield
    p = e * (1.0 / total)
    pb = p.astype(BF16)
    u = p * dp
    out_dot = jnp.sum(u, axis=0, keepdims=True)
    yield
    ds = (u - p * out_dot).astype(BF16)
    att_t = dot(shared["v_t"][:, 0:seen], pb, 1, 0)
    new_v = dot(pb, gb, 1, 0)
    yield
    dq_t = dot(shared["k_t"][:, 0:seen], ds, 1, 0) * scale
    new_k = dot(ds, qb, 1, 0)
    att[rows, cols] = jnp.transpose(att_t).astype(BF16)
    yield
    dq[rows, cols] = jnp.transpose(dq_t).astype(BF16)
    if b == 1:
        shared["dk"] = new_k[0:ROWS]
        shared["dv"] = new_v[0:ROWS]
    else:
        new_k = new_k + shared["dk"]
        new_v = new_v + shared["dv"]
    dk[rows, cols] = (new_k[seen - ROWS : seen] * scale).astype(BF16)
    dv[rows, cols] = new_v[seen - ROWS : seen].astype(BF16)


def hidden_of(lat, w1):
    pre = dot(lat, w1, 0, 0)
    return (pre * sigmoid(pre)).astype(BF16)


def attention_body(ctx_ref, starts, q_own, q_oth, k_own, k_oth, v_own, v_oth, g_own, g_oth, text, lat_own, lat_oth, w1, w2,
                   lay_out, dq_out, dk_out, dv_out, att_send, dq_send, dk_send, dv_send,
                   q, k, v, g, att, dq, dk, dv, hid):
    ctx = ctx_ref[0]
    own = pl.multiple_of(ctx * ROWS, ROWS)
    oth = pl.multiple_of(ROWS - ctx * ROWS, ROWS)

    @pl.when(pl.program_id(0) == 0)
    def _():
        hid[...] = hidden_of(pick(starts, lat_own, lat_oth)[0], w1[...])

    step = pl.program_id(0)
    there = pl.ds(pl.multiple_of(ctx * HALF + step * GROUP * HEAD, GROUP * HEAD), GROUP * HEAD)
    for full, a, b in ((q, q_own, q_oth), (k, k_own, k_oth), (v, v_own, v_oth), (g, g_own, g_oth)):
        full[pl.ds(own, ROWS), :] = a[...]
        full[pl.ds(oth, ROWS), :] = b[:, there]
    unit = eye(HEAD)
    waiting = []
    for h in range(GROUP):
        cols = slice(HEAD * h, HEAD * h + HEAD)
        shared = {}
        for b in (1, 0):
            waiting.append(chain(q, k, v, g, att, dq, dk, dv, cols, b, unit, shared))
    running = []
    while waiting or running:
        if waiting:
            running.append(waiting.pop(0))
        running = [item for item in running if next(item, "end") != "end"]
    mine = pl.ds(own, ROWS)
    theirs = pl.ds(oth, ROWS)
    for full, keep, send in ((dq, dq_out, dq_send), (dk, dk_out, dk_send), (dv, dv_out, dv_send)):
        keep[...] = full[mine, :]
        send[...] = full[theirs, :]
    att_send[...] = att[theirs, :]
    add_residual(ctx, lay_out, att[mine, :], hid[...], w2[...], text[...])


def add_residual(ctx, lay_out, att, hid, w2, text):
    lay_out[...] = att
    image_rows = pl.ds(pl.multiple_of(ctx * SPAN, SPAN), SPAN)
    text_rows = pl.ds(pl.multiple_of(SPAN - ctx * SPAN, SPAN), SPAN)
    embedding = dot(hid, w2, 1, 0).astype(BF16).astype(F32)
    lay_out[image_rows, :] = (embedding + lay_out[image_rows, :].astype(F32)).astype(BF16)
    lay_out[text_rows, :] = (text.astype(F32) + lay_out[text_rows, :].astype(F32)).astype(BF16)


def place_body(ctx_ref, *refs):
    count = len(refs) // 3
    width = refs[-1].shape[1]
    cols = pl.ds(pl.multiple_of(pl.program_id(0) * width, width), width)
    for i in range(count):
        refs[2 * count + i][...] = refs[i][:, cols]


def merge_body(ctx_ref, starts, text, lat_own, lat_oth, w1, w2, att, lay_in, lay_out, hid):
    @pl.when(pl.program_id(0) == 0)
    def _():
        hid[...] = hidden_of(pick(starts, lat_own, lat_oth)[0], w1[...])

    width = lay_out.shape[1]
    cols = pl.ds(pl.multiple_of(pl.program_id(0) * width, width), width)
    add_residual(ctx_ref[0], lay_out, att[:, cols], hid[...], w2[...], text[...])


def local(queries, keys, values, residual, grad_out, latents, image_starts, w_first, w_second):
    ctx = lax.axis_index("ctx").astype(jnp.int32)
    scalars = (ctx[None], image_starts.reshape(2))
    swap = [(0, 1), (1, 0)]

    def swapped(value):
        return lax.ppermute(value, "ctx", swap)

    q_rows, k_rows, v_rows, g_rows, r_rows = queries[0], keys[0], values[0], grad_out[0], residual[0]
    lat_own = latents[0, 0]
    lat_oth = swapped(lat_own)
    lat_oth, g_send = lax.optimization_barrier((lat_oth, g_rows))
    g_oth = swapped(g_send)

    struct = jax.ShapeDtypeStruct
    anywhere = pl.BlockSpec(memory_space=pl.ANY)
    near = pl.BlockSpec(memory_space=pltpu.VMEM)

    def place_near(value):
        return pltpu.with_memory_space_constraint(value, pltpu.VMEM)

    def near_call(body, args, outs):
        return pl.pallas_call(
            body, in_specs=[near] * len(args), out_specs=[near] * len(outs),
            out_shape=[pltpu.VMEM(shape, BF16) for shape in outs],
        )(*[place_near(value) for value in args])

    lat_spec = whole((32, SPAN))
    ready = call(
        hidden_body, scalars, (lat_own, place_near(lat_oth), w_first, w_second, g_rows),
        [anywhere, near, anywhere, anywhere, anywhere], [near] * 5,
        [pltpu.VMEM((32, ROWS), BF16), pltpu.VMEM((CH, ROWS), BF16), pltpu.VMEM((CH, ROWS), F32),
         pltpu.VMEM((CH, WIDTH), BF16), pltpu.VMEM((SPAN, WIDTH), BF16)],
        scratch=[pltpu.VMEM((32, SPAN), BF16), pltpu.VMEM((32, CH), BF16), pltpu.SemaphoreType.DMA((4,))],
        cost=pl.CostEstimate(flops=4_000_000_000, bytes_accessed=10_000_000, transcendentals=200_000),
    )
    g_oth, *rest = lax.optimization_barrier((g_oth, *ready, q_rows, k_rows, v_rows))
    ready, rows = rest[:5], rest[5:]
    q_oth, k_oth, v_oth = [swapped(value) for value in rows]
    payload = call(
        weight_body, scalars[:1], [place_near(value) for value in (*ready, g_oth)],
        [near] * 6, anywhere, struct((GROUPS, 9, 16, 128), BF16),
        scratch=[pltpu.VMEM((ROWS, WIDTH), BF16), pltpu.VMEM((GROUPS, 9, 16, 128), BF16), pltpu.SemaphoreType.DMA((2,))],
    )
    block = ("zl", "y", "x")
    q_oth, k_oth, v_oth, g_oth = [place_near(value) for value in (q_oth, k_oth, v_oth, g_oth)]
    got = lax.all_to_all(payload, block, 0, 0, tiled=False)

    cols = GROUP * HEAD
    steps = HEADS // GROUP
    own_spec = pl.BlockSpec((ROWS, cols), lambda i, c, s: (0, c[0] * steps + i))
    send_spec = pl.BlockSpec((ROWS, cols), lambda i, c, s: (0, i))
    big = struct((ROWS, WIDTH), BF16)
    small = struct((ROWS, HALF), BF16)
    result = call(
        attention_body, scalars,
        (q_rows, q_oth, k_rows, k_oth, v_rows, v_oth, g_rows, g_oth, r_rows, lat_own, lat_oth, w_first, w_second),
        [own_spec, near] * 4
        + [pl.BlockSpec((SPAN, cols), lambda i, c, s: (1 - c[0], c[0] * steps + i)),
           lat_spec, lat_spec, whole((32, CH)), pl.BlockSpec((CH, cols), lambda i, c, s: (0, c[0] * steps + i))],
        [own_spec] * 4 + [send_spec] * 4,
        [big] * 4 + [small] * 4,
        grid=(steps,),
        scratch=[pltpu.VMEM((SEQ, cols), BF16)] * 8 + [pltpu.VMEM((SPAN, CH), BF16)],
        cost=pl.CostEstimate(flops=40_000_000_000, bytes_accessed=100_000_000, transcendentals=4_000_000),
    )
    lay, dq, dk, dv = result[:4]
    sent_att, sent_dq, sent_dk, sent_dv = [swapped(value) for value in result[4:]]

    parts = 2
    width = HALF // parts
    half_spec = pl.BlockSpec((ROWS, width), lambda i, c, *_: (0, (1 - c[0]) * parts + i))

    def placed(after, got, into):
        count = len(got)
        return call(
            place_body, (after,), (*map(place_near, got), *into), [near] * count + [anywhere] * count, [half_spec] * count,
            [big] * count, grid=(parts,), aliases={1 + count + i: i for i in range(count)},
        )

    one, = near_call(group_sum_body, (got,), [(9, 16, 128)])
    one, after = lax.optimization_barrier((one, scalars[0]))
    others = [lax.ppermute(one, "zh", [(z, (z + s) % 4) for z in range(4)]) for s in (1, 2, 3)]
    dq, dk, dv = placed(after, (sent_dq, sent_dk, sent_dv), (dq, dk, dv))
    *others, dq, dk, dv = lax.optimization_barrier((*others, dq, dk, dv))
    sums, = near_call(spread_sum_body, (one, *others), [(GROUPS, 9, 16, 128)])
    sums, sent_att = lax.optimization_barrier((sums, sent_att))
    got = lax.all_to_all(sums, block, 0, 0, tiled=False)
    sum_second, sum_first = pl.pallas_call(
        finish_body, in_specs=[near], out_specs=[anywhere, anywhere],
        out_shape=[struct((CH, HALF), F32), struct((32, CH), F32)],
        scratch_shapes=[pltpu.VMEM((CH, HALF), F32), pltpu.VMEM((32, CH), F32), pltpu.SemaphoreType.DMA((5,))],
        compiler_params=pltpu.CompilerParams(vmem_limit_bytes=VMEM),
    )(place_near(got))

    lay = call(
        merge_body, scalars, (r_rows, lat_own, lat_oth, w_first, w_second, place_near(sent_att), lay),
        [pl.BlockSpec((SPAN, width), lambda i, c, s: (1 - c[0], (1 - c[0]) * parts + i)), lat_spec, lat_spec,
         whole((32, CH)), pl.BlockSpec((CH, width), lambda i, c, s: (0, (1 - c[0]) * parts + i)),
         near, anywhere],
        half_spec, big, grid=(parts,), scratch=[pltpu.VMEM((SPAN, CH), BF16)], aliases={8: 0},
    )
    outs = (lay, dq, dk, dv)
    return (*[value[None] for value in outs], sum_first, sum_second)


def solution(mesh):
    axes = Mesh(mesh.devices.reshape(4, 2, 4, 4, 2), ("zh", "zl", "y", "x", "ctx"))
    dp = ("zh", "zl", "y", "x")
    rows = P(dp, "ctx", None)
    return jax.shard_map(
        local,
        mesh=axes,
        in_specs=(rows, rows, rows, rows, rows, P(dp, "ctx", None, None), P(dp, None), P(), P()),
        out_specs=(rows, rows, rows, rows, P(), P(None, "ctx")),
        check_vma=False,
    )
```

```python
import math

import jax
import jax.numpy as jnp
from jax import lax
from jax.experimental import pallas as pl
from jax.experimental.pallas import tpu as pltpu
from jax.sharding import Mesh
from jax.sharding import PartitionSpec as P

HEAD = 128
SPAN = 128
ROWS = 256
HALF = 1024
WIDTH = 2048
SEQ = 512
CH = 512
HEADS = 8
GROUP = 4
GROUPS = 32
VMEM = 56 * 1024 * 1024

F32 = jnp.float32
BF16 = jnp.bfloat16


def dot(a, b, ca, cb):
    return lax.dot_general(a, b, (((ca,), (cb,)), ((), ())), preferred_element_type=F32)


def whole(shape):
    return pl.BlockSpec(shape, lambda *_: (0,) * len(shape))


def call(body, scalars, args, in_specs, out_specs, out_shape, grid=(1,), scratch=(), aliases=None, cost=None):
    return pl.pallas_call(
        body,
        grid_spec=pltpu.PrefetchScalarGridSpec(
            num_scalar_prefetch=len(scalars),
            grid=grid,
            in_specs=in_specs,
            out_specs=out_specs,
            scratch_shapes=scratch,
        ),
        out_shape=out_shape,
        input_output_aliases=aliases or {},
        cost_estimate=cost,
        compiler_params=pltpu.CompilerParams(vmem_limit_bytes=VMEM),
    )(*scalars, *args)


def sigmoid(v):
    return 1.0 / (1.0 + jnp.exp(-v))


def eye(n):
    rows = lax.broadcasted_iota(jnp.int32, (n, n), 0)
    cols = lax.broadcasted_iota(jnp.int32, (n, n), 1)
    return (rows == cols).astype(F32).astype(BF16)


def pick(starts, lat_own, lat_oth):
    in_order = starts[0] == 0
    one, two = lat_own[...].astype(F32), lat_oth[...].astype(F32)
    return jnp.where(in_order, one, two).astype(BF16), jnp.where(in_order, two, one).astype(BF16)


def hidden_and_gate(w1, lat):
    pre = dot(w1, lat, 0, 0)
    sig = sigmoid(pre)
    return (pre * sig).astype(BF16), sig * (1.0 + pre * (1.0 - sig))


def hidden_body(ctx_ref, lat_hbm, w1_hbm, w2_hbm, g_own, lat, w1, hid_t, gate, w2, grads, sems):
    own_rows = pl.ds(pl.multiple_of(ctx_ref[0] * SPAN, SPAN), SPAN)
    copies = [
        pltpu.make_async_copy(source, target, sems.at[i])
        for i, (source, target) in enumerate((
            (lat_hbm, lat), (w1_hbm, w1), (g_own.at[own_rows, :], grads), (w2_hbm, w2)))
    ]
    for copy in copies:
        copy.start()
    copies[0].wait()
    copies[1].wait()
    hid_t[...], gate[...] = hidden_and_gate(w1[...], lat[...])
    copies[2].wait()
    copies[3].wait()


def weight_body(ctx_ref, starts, lat_own, w1, hid_own, gate_own, w2, g_own, lat_oth, g_oth, out, grads, tiles, sems):
    ctx = ctx_ref[0]
    oth_rows = pl.ds(pl.multiple_of(SPAN - ctx * SPAN, SPAN), SPAN)
    place = pl.multiple_of(jnp.where(starts[0] == 0, 0, SPAN), SPAN)
    grads[pl.ds(place, SPAN), :] = g_own[...]
    grads[pl.ds(pl.multiple_of(SPAN - place, SPAN), SPAN), :] = g_oth[oth_rows, :]
    hid_oth, gate_oth = hidden_and_gate(w1[...], lat_oth[...])
    hid_t = jnp.concatenate([hid_own[...], hid_oth], axis=1)
    gate = jnp.concatenate([gate_own[...], gate_oth], axis=1)
    patches = jnp.concatenate([lat_own[...], lat_oth[...]], axis=1)
    for n in range(4):
        half = grads[:, pl.ds(pl.multiple_of(ctx * HALF, HALF) + 256 * n, 256)]
        strip = dot(hid_t, half, 1, 0).astype(BF16)
        for j in range(GROUPS):
            for i in range(2):
                tiles[j, 2 * n + i] = strip[16 * j : 16 * j + 16, 128 * i : 128 * i + 128]
    main, rest = pl.ds(0, 8), pl.ds(8, 1)
    copies = [pltpu.make_async_copy(tiles.at[:, part], out.at[:, part], sems.at[i]) for i, part in enumerate((main, rest))]
    copies[0].start()
    back = dot(w2[...], grads[...], 1, 1)
    grad_pre = (back * gate).astype(BF16)
    first = dot(patches, grad_pre, 1, 1).astype(BF16)
    for j in range(GROUPS):
        m = j // 4
        tiles[j, 8] = first[16 * (m // 4) : 16 * (m // 4) + 16, 128 * (m % 4) : 128 * (m % 4) + 128]
    copies[1].start()
    copies[0].wait()
    copies[1].wait()


def group_sum_body(got, out):
    total = got[0].astype(F32)
    for j in range(1, GROUPS):
        total = total + got[j].astype(F32)
    out[...] = total.astype(BF16)


def spread_sum_body(one, next1, next2, next3, out):
    even = one[...].astype(F32) + next2[...].astype(F32)
    odd = next1[...].astype(F32) + next3[...].astype(F32)
    total = (even + odd).astype(BF16)
    for j in range(GROUPS):
        out[j] = total


def finish_body(got, second, first, second_near, first_near, sems):
    copies = []
    for n in range(8):
        for j in range(4 * n, 4 * n + 4):
            for t in range(8):
                second_near[16 * j : 16 * j + 16, 128 * t : 128 * t + 128] = got[j, t].astype(F32) * (1.0 / 128.0)
        part = pl.ds(64 * n, 64)
        copies.append(pltpu.make_async_copy(second_near.at[part, :], second.at[part, :], sems.at[n]))
        copies[-1].start()
    for m in range(8):
        rows, cols = 16 * (m // 4), 128 * (m % 4)
        first_near[rows : rows + 16, cols : cols + 128] = got[4 * m, 8].astype(F32) * (1.0 / 128.0)
    copies.append(pltpu.make_async_copy(first_near, first, sems.at[8]))
    copies[-1].start()
    for copy in copies:
        copy.wait()


def chain(q, k, v, g, att, dq, dk, dv, cols, b, unit, shared):
    scale = HEAD ** -0.5
    power = scale * math.log2(math.e)
    seen = ROWS * (b + 1)
    rows = slice(ROWS * b, ROWS * b + ROWS)
    qb = q[rows, cols]
    gb = g[rows, cols]
    scores = dot(k[0:seen, cols], qb, 1, 1)
    dp = dot(v[0:seen, cols], gb, 1, 1)
    if b == 1:
        shared["k_t"] = dot(unit, k[:, cols], 1, 1).astype(BF16)
        shared["v_t"] = dot(unit, v[:, cols], 1, 1).astype(BF16)
    yield
    key_pos = lax.broadcasted_iota(jnp.int32, (ROWS, ROWS), 0)
    query_pos = lax.broadcasted_iota(jnp.int32, (ROWS, ROWS), 1)
    if b == 0:
        limit = jnp.where(query_pos < SPAN, SPAN - 1, query_pos)
    else:
        limit = jnp.where(query_pos < SPAN, query_pos, ROWS - 1)
    last = jnp.where(key_pos <= limit, scores[seen - ROWS : seen], -1e30)
    scores = last if b == 0 else jnp.concatenate([scores[0:ROWS], last], axis=0)
    top = jnp.max(scores, axis=0, keepdims=True)
    yield
    e = jnp.exp2((scores - top) * power)
    total = jnp.sum(e, axis=0, keepdims=True)
    yield
    p = e * (1.0 / total)
    pb = p.astype(BF16)
    u = p * dp
    out_dot = jnp.sum(u, axis=0, keepdims=True)
    yield
    ds = (u - p * out_dot).astype(BF16)
    att_t = dot(shared["v_t"][:, 0:seen], pb, 1, 0)
    new_v = dot(pb, gb, 1, 0)
    yield
    dq_t = dot(shared["k_t"][:, 0:seen], ds, 1, 0) * scale
    new_k = dot(ds, qb, 1, 0)
    att[rows, cols] = jnp.transpose(att_t).astype(BF16)
    yield
    dq[rows, cols] = jnp.transpose(dq_t).astype(BF16)
    if b == 1:
        shared["dk"] = new_k[0:ROWS]
        shared["dv"] = new_v[0:ROWS]
    else:
        new_k = new_k + shared["dk"]
        new_v = new_v + shared["dv"]
    dk[rows, cols] = (new_k[seen - ROWS : seen] * scale).astype(BF16)
    dv[rows, cols] = new_v[seen - ROWS : seen].astype(BF16)


def hidden_of(lat, w1):
    pre = dot(lat, w1, 0, 0)
    return (pre * sigmoid(pre)).astype(BF16)


def attention_body(ctx_ref, starts, q_own, q_oth, k_own, k_oth, v_own, v_oth, g_own, g_oth, text, lat_own, lat_oth, w1, w2,
                   lay_out, dq_out, dk_out, dv_out, att_send, dq_send, dk_send, dv_send,
                   q, k, v, g, att, dq, dk, dv, hid):
    ctx = ctx_ref[0]
    own = pl.multiple_of(ctx * ROWS, ROWS)
    oth = pl.multiple_of(ROWS - ctx * ROWS, ROWS)

    @pl.when(pl.program_id(0) == 0)
    def _():
        hid[...] = hidden_of(pick(starts, lat_own, lat_oth)[0], w1[...])

    step = pl.program_id(0)
    there = pl.ds(pl.multiple_of(ctx * HALF + step * GROUP * HEAD, GROUP * HEAD), GROUP * HEAD)
    for full, a, b in ((q, q_own, q_oth), (k, k_own, k_oth), (v, v_own, v_oth), (g, g_own, g_oth)):
        full[pl.ds(own, ROWS), :] = a[...]
        full[pl.ds(oth, ROWS), :] = b[:, there]
    unit = eye(HEAD)
    waiting = []
    for h in range(GROUP):
        cols = slice(HEAD * h, HEAD * h + HEAD)
        shared = {}
        for b in (1, 0):
            waiting.append(chain(q, k, v, g, att, dq, dk, dv, cols, b, unit, shared))
    running = []
    while waiting or running:
        if waiting:
            running.append(waiting.pop(0))
        running = [item for item in running if next(item, "end") != "end"]
    mine = pl.ds(own, ROWS)
    theirs = pl.ds(oth, ROWS)
    for full, keep, send in ((dq, dq_out, dq_send), (dk, dk_out, dk_send), (dv, dv_out, dv_send)):
        keep[...] = full[mine, :]
        send[...] = full[theirs, :]
    att_send[...] = att[theirs, :]
    add_residual(ctx, lay_out, att[mine, :], hid[...], w2[...], text[...])


def add_residual(ctx, lay_out, att, hid, w2, text):
    lay_out[...] = att
    image_rows = pl.ds(pl.multiple_of(ctx * SPAN, SPAN), SPAN)
    text_rows = pl.ds(pl.multiple_of(SPAN - ctx * SPAN, SPAN), SPAN)
    embedding = dot(hid, w2, 1, 0).astype(BF16).astype(F32)
    lay_out[image_rows, :] = (embedding + lay_out[image_rows, :].astype(F32)).astype(BF16)
    lay_out[text_rows, :] = (text.astype(F32) + lay_out[text_rows, :].astype(F32)).astype(BF16)


def place_body(ctx_ref, *refs):
    count = len(refs) // 3
    width = refs[-1].shape[1]
    cols = pl.ds(pl.multiple_of(pl.program_id(0) * width, width), width)
    for i in range(count):
        refs[2 * count + i][...] = refs[i][:, cols]


def merge_body(ctx_ref, starts, text, lat_own, lat_oth, w1, w2, att, lay_in, lay_out, hid):
    @pl.when(pl.program_id(0) == 0)
    def _():
        hid[...] = hidden_of(pick(starts, lat_own, lat_oth)[0], w1[...])

    width = lay_out.shape[1]
    cols = pl.ds(pl.multiple_of(pl.program_id(0) * width, width), width)
    add_residual(ctx_ref[0], lay_out, att[:, cols], hid[...], w2[...], text[...])


def local(queries, keys, values, residual, grad_out, latents, image_starts, w_first, w_second):
    ctx = lax.axis_index("ctx").astype(jnp.int32)
    scalars = (ctx[None], image_starts.reshape(2))
    swap = [(0, 1), (1, 0)]

    def swapped(value):
        return lax.ppermute(value, "ctx", swap)

    q_rows, k_rows, v_rows, g_rows, r_rows = queries[0], keys[0], values[0], grad_out[0], residual[0]
    lat_own = latents[0, 0]
    lat_oth = swapped(lat_own)
    g_oth = swapped(g_rows)

    struct = jax.ShapeDtypeStruct
    anywhere = pl.BlockSpec(memory_space=pl.ANY)
    near = pl.BlockSpec(memory_space=pltpu.VMEM)

    def place_near(value):
        return pltpu.with_memory_space_constraint(value, pltpu.VMEM)

    def near_call(body, args, outs):
        return pl.pallas_call(
            body, in_specs=[near] * len(args), out_specs=[near] * len(outs),
            out_shape=[pltpu.VMEM(shape, BF16) for shape in outs],
        )(*[place_near(value) for value in args])

    lat_spec = whole((32, SPAN))
    ready = call(
        hidden_body, scalars[:1], (lat_own, w_first, w_second, g_rows), [anywhere] * 4, [near] * 6,
        [pltpu.VMEM((32, SPAN), BF16), pltpu.VMEM((32, CH), BF16), pltpu.VMEM((CH, SPAN), BF16), pltpu.VMEM((CH, SPAN), F32),
         pltpu.VMEM((CH, WIDTH), BF16), pltpu.VMEM((SPAN, WIDTH), BF16)],
        scratch=[pltpu.SemaphoreType.DMA((4,))],
        cost=pl.CostEstimate(flops=4_000_000_000, bytes_accessed=10_000_000, transcendentals=200_000),
    )
    lat_oth, g_oth, *rest = lax.optimization_barrier((lat_oth, g_oth, *ready, q_rows, k_rows, v_rows))
    ready, rows = rest[:6], rest[6:]
    q_oth, k_oth, v_oth = [swapped(value) for value in rows]
    payload = call(
        weight_body, scalars, [place_near(value) for value in (*ready, lat_oth, g_oth)],
        [near] * 8, anywhere, struct((GROUPS, 9, 16, 128), BF16),
        scratch=[pltpu.VMEM((ROWS, WIDTH), BF16), pltpu.VMEM((GROUPS, 9, 16, 128), BF16), pltpu.SemaphoreType.DMA((2,))],
    )
    block = ("zl", "y", "x")
    q_oth, k_oth, v_oth, g_oth = [place_near(value) for value in (q_oth, k_oth, v_oth, g_oth)]
    got = lax.all_to_all(payload, block, 0, 0, tiled=False)

    cols = GROUP * HEAD
    steps = HEADS // GROUP
    own_spec = pl.BlockSpec((ROWS, cols), lambda i, c, s: (0, c[0] * steps + i))
    send_spec = pl.BlockSpec((ROWS, cols), lambda i, c, s: (0, i))
    big = struct((ROWS, WIDTH), BF16)
    small = struct((ROWS, HALF), BF16)
    result = call(
        attention_body, scalars,
        (q_rows, q_oth, k_rows, k_oth, v_rows, v_oth, g_rows, g_oth, r_rows, lat_own, lat_oth, w_first, w_second),
        [own_spec, near] * 4
        + [pl.BlockSpec((SPAN, cols), lambda i, c, s: (1 - c[0], c[0] * steps + i)),
           lat_spec, lat_spec, whole((32, CH)), pl.BlockSpec((CH, cols), lambda i, c, s: (0, c[0] * steps + i))],
        [own_spec] * 4 + [send_spec] * 4,
        [big] * 4 + [small] * 4,
        grid=(steps,),
        scratch=[pltpu.VMEM((SEQ, cols), BF16)] * 8 + [pltpu.VMEM((SPAN, CH), BF16)],
        cost=pl.CostEstimate(flops=40_000_000_000, bytes_accessed=100_000_000, transcendentals=4_000_000),
    )
    lay, dq, dk, dv = result[:4]
    sent_att, sent_dq, sent_dk, sent_dv = [swapped(value) for value in result[4:]]

    parts = 2
    width = HALF // parts
    half_spec = pl.BlockSpec((ROWS, width), lambda i, c, *_: (0, (1 - c[0]) * parts + i))

    def placed(after, got, into):
        count = len(got)
        return call(
            place_body, (after,), (*map(place_near, got), *into), [near] * count + [anywhere] * count, [half_spec] * count,
            [big] * count, grid=(parts,), aliases={1 + count + i: i for i in range(count)},
        )

    one, = near_call(group_sum_body, (got,), [(9, 16, 128)])
    one, after = lax.optimization_barrier((one, scalars[0]))
    others = [lax.ppermute(one, "zh", [(z, (z + s) % 4) for z in range(4)]) for s in (1, 2, 3)]
    dq, dk, dv = placed(after, (sent_dq, sent_dk, sent_dv), (dq, dk, dv))
    *others, dq, dk, dv = lax.optimization_barrier((*others, dq, dk, dv))
    sums, = near_call(spread_sum_body, (one, *others), [(GROUPS, 9, 16, 128)])
    sums, sent_att = lax.optimization_barrier((sums, sent_att))
    got = lax.all_to_all(sums, block, 0, 0, tiled=False)
    sum_second, sum_first = pl.pallas_call(
        finish_body, in_specs=[near], out_specs=[anywhere, anywhere],
        out_shape=[struct((CH, HALF), F32), struct((32, CH), F32)],
        scratch_shapes=[pltpu.VMEM((CH, HALF), F32), pltpu.VMEM((32, CH), F32), pltpu.SemaphoreType.DMA((9,))],
        compiler_params=pltpu.CompilerParams(vmem_limit_bytes=VMEM),
    )(place_near(got))

    lay = call(
        merge_body, scalars, (r_rows, lat_own, lat_oth, w_first, w_second, place_near(sent_att), lay),
        [pl.BlockSpec((SPAN, width), lambda i, c, s: (1 - c[0], (1 - c[0]) * parts + i)), lat_spec, lat_spec,
         whole((32, CH)), pl.BlockSpec((CH, width), lambda i, c, s: (0, (1 - c[0]) * parts + i)),
         near, anywhere],
        half_spec, big, grid=(parts,), scratch=[pltpu.VMEM((SPAN, CH), BF16)], aliases={8: 0},
    )
    outs = (lay, dq, dk, dv)
    return (*[value[None] for value in outs], sum_first, sum_second)


def solution(mesh):
    axes = Mesh(mesh.devices.reshape(4, 2, 4, 4, 2), ("zh", "zl", "y", "x", "ctx"))
    dp = ("zh", "zl", "y", "x")
    rows = P(dp, "ctx", None)
    return jax.shard_map(
        local,
        mesh=axes,
        in_specs=(rows, rows, rows, rows, rows, P(dp, "ctx", None, None), P(dp, None), P(), P()),
        out_specs=(rows, rows, rows, rows, P(), P(None, "ctx")),
        check_vma=False,
    )
```

```python
import math

import jax
import jax.numpy as jnp
from jax import lax
from jax.experimental import pallas as pl
from jax.experimental.pallas import tpu as pltpu
from jax.sharding import Mesh
from jax.sharding import PartitionSpec as P

HEAD = 128
SPAN = 128
ROWS = 256
HALF = 1024
WIDTH = 2048
SEQ = 512
CH = 512
HEADS = 8
GROUP = 4
GROUPS = 32
VMEM = 56 * 1024 * 1024

F32 = jnp.float32
BF16 = jnp.bfloat16


def dot(a, b, ca, cb):
    return lax.dot_general(a, b, (((ca,), (cb,)), ((), ())), preferred_element_type=F32)


def whole(shape):
    return pl.BlockSpec(shape, lambda *_: (0,) * len(shape))


def call(body, scalars, args, in_specs, out_specs, out_shape, grid=(1,), scratch=(), aliases=None, cost=None):
    return pl.pallas_call(
        body,
        grid_spec=pltpu.PrefetchScalarGridSpec(
            num_scalar_prefetch=len(scalars),
            grid=grid,
            in_specs=in_specs,
            out_specs=out_specs,
            scratch_shapes=scratch,
        ),
        out_shape=out_shape,
        input_output_aliases=aliases or {},
        cost_estimate=cost,
        compiler_params=pltpu.CompilerParams(vmem_limit_bytes=VMEM),
    )(*scalars, *args)


def sigmoid(v):
    return 1.0 / (1.0 + jnp.exp(-v))


def eye(n):
    rows = lax.broadcasted_iota(jnp.int32, (n, n), 0)
    cols = lax.broadcasted_iota(jnp.int32, (n, n), 1)
    return (rows == cols).astype(F32).astype(BF16)


def pick(starts, lat_own, lat_oth):
    in_order = starts[0] == 0
    one, two = lat_own[...].astype(F32), lat_oth[...].astype(F32)
    return jnp.where(in_order, one, two).astype(BF16), jnp.where(in_order, two, one).astype(BF16)


def hidden_and_gate(w1, lat):
    pre = dot(w1, lat, 0, 0)
    sig = sigmoid(pre)
    return (pre * sig).astype(BF16), sig * (1.0 + pre * (1.0 - sig))


def hidden_body(ctx_ref, lat_hbm, w1_hbm, w2_hbm, g_own, lat, w1, hid_t, gate, w2, grads, sems):
    own_rows = pl.ds(pl.multiple_of(ctx_ref[0] * SPAN, SPAN), SPAN)
    copies = [
        pltpu.make_async_copy(source, target, sems.at[i])
        for i, (source, target) in enumerate((
            (lat_hbm, lat), (w1_hbm, w1), (g_own.at[own_rows, :], grads), (w2_hbm, w2)))
    ]
    for copy in copies:
        copy.start()
    copies[0].wait()
    copies[1].wait()
    hid_t[...], gate[...] = hidden_and_gate(w1[...], lat[...])
    copies[2].wait()
    copies[3].wait()


def weight_body(ctx_ref, starts, lat_own, w1, hid_own, gate_own, w2, g_own, lat_oth, g_oth, out, grads, tiles, sems):
    ctx = ctx_ref[0]
    oth_rows = pl.ds(pl.multiple_of(SPAN - ctx * SPAN, SPAN), SPAN)
    place = pl.multiple_of(jnp.where(starts[0] == 0, 0, SPAN), SPAN)
    grads[pl.ds(place, SPAN), :] = g_own[...]
    grads[pl.ds(pl.multiple_of(SPAN - place, SPAN), SPAN), :] = g_oth[oth_rows, :]
    hid_oth, gate_oth = hidden_and_gate(w1[...], lat_oth[...])
    hid_t = jnp.concatenate([hid_own[...], hid_oth], axis=1)
    gate = jnp.concatenate([gate_own[...], gate_oth], axis=1)
    patches = jnp.concatenate([lat_own[...], lat_oth[...]], axis=1)
    for n in range(4):
        half = grads[:, pl.ds(pl.multiple_of(ctx * HALF, HALF) + 256 * n, 256)]
        strip = dot(hid_t, half, 1, 0).astype(BF16)
        for j in range(GROUPS):
            for i in range(2):
                tiles[j, 2 * n + i] = strip[16 * j : 16 * j + 16, 128 * i : 128 * i + 128]
    main, rest = pl.ds(0, 8), pl.ds(8, 1)
    copies = [pltpu.make_async_copy(tiles.at[:, part], out.at[:, part], sems.at[i]) for i, part in enumerate((main, rest))]
    copies[0].start()
    back = dot(w2[...], grads[...], 1, 1)
    grad_pre = (back * gate).astype(BF16)
    first = dot(patches, grad_pre, 1, 1).astype(BF16)
    for j in range(GROUPS):
        m = j // 4
        tiles[j, 8] = first[16 * (m // 4) : 16 * (m // 4) + 16, 128 * (m % 4) : 128 * (m % 4) + 128]
    copies[1].start()
    copies[0].wait()
    copies[1].wait()


def group_sum_body(got, out):
    total = got[0].astype(F32)
    for j in range(1, GROUPS):
        total = total + got[j].astype(F32)
    out[...] = total.astype(BF16)


def spread_sum_body(one, next1, next2, next3, out):
    even = one[...].astype(F32) + next2[...].astype(F32)
    odd = next1[...].astype(F32) + next3[...].astype(F32)
    total = (even + odd).astype(BF16)
    for j in range(GROUPS):
        out[j] = total


def finish_body(got, second, first, second_near, first_near, sems):
    copies = []
    for n in range(8):
        for j in range(4 * n, 4 * n + 4):
            for t in range(8):
                second_near[16 * j : 16 * j + 16, 128 * t : 128 * t + 128] = got[j, t].astype(F32) * (1.0 / 128.0)
        part = pl.ds(64 * n, 64)
        copies.append(pltpu.make_async_copy(second_near.at[part, :], second.at[part, :], sems.at[n]))
        copies[-1].start()
    for m in range(8):
        rows, cols = 16 * (m // 4), 128 * (m % 4)
        first_near[rows : rows + 16, cols : cols + 128] = got[4 * m, 8].astype(F32) * (1.0 / 128.0)
    copies.append(pltpu.make_async_copy(first_near, first, sems.at[8]))
    copies[-1].start()
    for copy in copies:
        copy.wait()


def chain(q, k, v, g, att, dq, dk, dv, cols, b, unit, shared):
    scale = HEAD ** -0.5
    power = scale * math.log2(math.e)
    seen = ROWS * (b + 1)
    rows = slice(ROWS * b, ROWS * b + ROWS)
    qb = q[rows, cols]
    gb = g[rows, cols]
    scores = dot(k[0:seen, cols], qb, 1, 1)
    dp = dot(v[0:seen, cols], gb, 1, 1)
    if b == 1:
        shared["k_t"] = dot(unit, k[:, cols], 1, 1).astype(BF16)
        shared["v_t"] = dot(unit, v[:, cols], 1, 1).astype(BF16)
    yield
    key_pos = lax.broadcasted_iota(jnp.int32, (ROWS, ROWS), 0)
    query_pos = lax.broadcasted_iota(jnp.int32, (ROWS, ROWS), 1)
    if b == 0:
        limit = jnp.where(query_pos < SPAN, SPAN - 1, query_pos)
    else:
        limit = jnp.where(query_pos < SPAN, query_pos, ROWS - 1)
    last = jnp.where(key_pos <= limit, scores[seen - ROWS : seen], -1e30)
    scores = last if b == 0 else jnp.concatenate([scores[0:ROWS], last], axis=0)
    top = jnp.max(scores, axis=0, keepdims=True)
    yield
    e = jnp.exp2((scores - top) * power)
    total = jnp.sum(e, axis=0, keepdims=True)
    yield
    p = e * (1.0 / total)
    pb = p.astype(BF16)
    u = p * dp
    out_dot = jnp.sum(u, axis=0, keepdims=True)
    yield
    ds = (u - p * out_dot).astype(BF16)
    att_t = dot(shared["v_t"][:, 0:seen], pb, 1, 0)
    new_v = dot(pb, gb, 1, 0)
    yield
    dq_t = dot(shared["k_t"][:, 0:seen], ds, 1, 0) * scale
    new_k = dot(ds, qb, 1, 0)
    att[rows, cols] = jnp.transpose(att_t).astype(BF16)
    yield
    dq[rows, cols] = jnp.transpose(dq_t).astype(BF16)
    if b == 1:
        shared["dk"] = new_k[0:ROWS]
        shared["dv"] = new_v[0:ROWS]
    else:
        new_k = new_k + shared["dk"]
        new_v = new_v + shared["dv"]
    dk[rows, cols] = (new_k[seen - ROWS : seen] * scale).astype(BF16)
    dv[rows, cols] = new_v[seen - ROWS : seen].astype(BF16)


def hidden_of(lat, w1):
    pre = dot(lat, w1, 0, 0)
    return (pre * sigmoid(pre)).astype(BF16)


def attention_body(ctx_ref, starts, q_own, q_oth, k_own, k_oth, v_own, v_oth, g_own, g_oth, text, lat_own, lat_oth, w1, w2,
                   lay_out, dq_out, dk_out, dv_out, att_send, dq_send, dk_send, dv_send,
                   q, k, v, g, att, dq, dk, dv, hid):
    ctx = ctx_ref[0]
    own = pl.multiple_of(ctx * ROWS, ROWS)
    oth = pl.multiple_of(ROWS - ctx * ROWS, ROWS)

    @pl.when(pl.program_id(0) == 0)
    def _():
        hid[...] = hidden_of(pick(starts, lat_own, lat_oth)[0], w1[...])

    step = pl.program_id(0)
    there = pl.ds(pl.multiple_of(ctx * HALF + step * GROUP * HEAD, GROUP * HEAD), GROUP * HEAD)
    for full, a, b in ((q, q_own, q_oth), (k, k_own, k_oth), (v, v_own, v_oth), (g, g_own, g_oth)):
        full[pl.ds(own, ROWS), :] = a[...]
        full[pl.ds(oth, ROWS), :] = b[:, there]
    unit = eye(HEAD)
    waiting = []
    for h in range(GROUP):
        cols = slice(HEAD * h, HEAD * h + HEAD)
        shared = {}
        for b in (1, 0):
            waiting.append(chain(q, k, v, g, att, dq, dk, dv, cols, b, unit, shared))
    running = []
    while waiting or running:
        if waiting:
            running.append(waiting.pop(0))
        running = [item for item in running if next(item, "end") != "end"]
    mine = pl.ds(own, ROWS)
    theirs = pl.ds(oth, ROWS)
    for full, keep, send in ((dq, dq_out, dq_send), (dk, dk_out, dk_send), (dv, dv_out, dv_send)):
        keep[...] = full[mine, :]
        send[...] = full[theirs, :]
    att_send[...] = att[theirs, :]
    add_residual(ctx, lay_out, att[mine, :], hid[...], w2[...], text[...])


def add_residual(ctx, lay_out, att, hid, w2, text):
    lay_out[...] = att
    image_rows = pl.ds(pl.multiple_of(ctx * SPAN, SPAN), SPAN)
    text_rows = pl.ds(pl.multiple_of(SPAN - ctx * SPAN, SPAN), SPAN)
    embedding = dot(hid, w2, 1, 0).astype(BF16).astype(F32)
    lay_out[image_rows, :] = (embedding + lay_out[image_rows, :].astype(F32)).astype(BF16)
    lay_out[text_rows, :] = (text.astype(F32) + lay_out[text_rows, :].astype(F32)).astype(BF16)


def place_body(ctx_ref, *refs):
    count = len(refs) // 3
    width = refs[-1].shape[1]
    cols = pl.ds(pl.multiple_of(pl.program_id(0) * width, width), width)
    for i in range(count):
        refs[2 * count + i][...] = refs[i][:, cols]


def merge_body(ctx_ref, starts, text, lat_own, lat_oth, w1, w2, att, lay_in, lay_out, hid):
    @pl.when(pl.program_id(0) == 0)
    def _():
        hid[...] = hidden_of(pick(starts, lat_own, lat_oth)[0], w1[...])

    width = lay_out.shape[1]
    cols = pl.ds(pl.multiple_of(pl.program_id(0) * width, width), width)
    add_residual(ctx_ref[0], lay_out, att[:, cols], hid[...], w2[...], text[...])


def local(queries, keys, values, residual, grad_out, latents, image_starts, w_first, w_second):
    ctx = lax.axis_index("ctx").astype(jnp.int32)
    scalars = (ctx[None], image_starts.reshape(2))
    swap = [(0, 1), (1, 0)]

    def swapped(value):
        return lax.ppermute(value, "ctx", swap)

    q_rows, k_rows, v_rows, g_rows, r_rows = queries[0], keys[0], values[0], grad_out[0], residual[0]
    lat_own = latents[0, 0]
    lat_oth = swapped(lat_own)
    g_oth = swapped(g_rows)

    struct = jax.ShapeDtypeStruct
    anywhere = pl.BlockSpec(memory_space=pl.ANY)
    near = pl.BlockSpec(memory_space=pltpu.VMEM)

    def place_near(value):
        return pltpu.with_memory_space_constraint(value, pltpu.VMEM)

    def near_call(body, args, outs):
        return pl.pallas_call(
            body, in_specs=[near] * len(args), out_specs=[near] * len(outs),
            out_shape=[pltpu.VMEM(shape, BF16) for shape in outs],
        )(*[place_near(value) for value in args])

    lat_spec = whole((32, SPAN))
    ready = call(
        hidden_body, scalars[:1], (lat_own, w_first, w_second, g_rows), [anywhere] * 4, [near] * 6,
        [pltpu.VMEM((32, SPAN), BF16), pltpu.VMEM((32, CH), BF16), pltpu.VMEM((CH, SPAN), BF16), pltpu.VMEM((CH, SPAN), F32),
         pltpu.VMEM((CH, WIDTH), BF16), pltpu.VMEM((SPAN, WIDTH), BF16)],
        scratch=[pltpu.SemaphoreType.DMA((4,))],
        cost=pl.CostEstimate(flops=4_000_000_000, bytes_accessed=10_000_000, transcendentals=200_000),
    )
    lat_oth, g_oth, *rest = lax.optimization_barrier((lat_oth, g_oth, *ready, q_rows, k_rows, v_rows))
    ready, rows = rest[:6], rest[6:]
    q_oth, k_oth, v_oth = [swapped(value) for value in rows]
    payload = call(
        weight_body, scalars, [place_near(value) for value in (*ready, lat_oth, g_oth)],
        [near] * 8, anywhere, struct((GROUPS, 9, 16, 128), BF16),
        scratch=[pltpu.VMEM((ROWS, WIDTH), BF16), pltpu.VMEM((GROUPS, 9, 16, 128), BF16), pltpu.SemaphoreType.DMA((2,))],
    )
    block = ("zl", "y", "x")
    q_oth, k_oth, v_oth, g_oth = [place_near(value) for value in (q_oth, k_oth, v_oth, g_oth)]
    got = lax.all_to_all(payload, block, 0, 0, tiled=False)

    cols = GROUP * HEAD
    steps = HEADS // GROUP
    own_spec = pl.BlockSpec((ROWS, cols), lambda i, c, s: (0, c[0] * steps + i))
    send_spec = pl.BlockSpec((ROWS, cols), lambda i, c, s: (0, i))
    big = struct((ROWS, WIDTH), BF16)
    small = struct((ROWS, HALF), BF16)
    result = call(
        attention_body, scalars,
        (q_rows, q_oth, k_rows, k_oth, v_rows, v_oth, g_rows, g_oth, r_rows, lat_own, lat_oth, w_first, w_second),
        [own_spec, near] * 4
        + [pl.BlockSpec((SPAN, cols), lambda i, c, s: (1 - c[0], c[0] * steps + i)),
           lat_spec, lat_spec, whole((32, CH)), pl.BlockSpec((CH, cols), lambda i, c, s: (0, c[0] * steps + i))],
        [own_spec] * 4 + [send_spec] * 4,
        [big] * 4 + [small] * 4,
        grid=(steps,),
        scratch=[pltpu.VMEM((SEQ, cols), BF16)] * 8 + [pltpu.VMEM((SPAN, CH), BF16)],
        cost=pl.CostEstimate(flops=40_000_000_000, bytes_accessed=100_000_000, transcendentals=4_000_000),
    )
    lay, dq, dk, dv = result[:4]
    sent_att, sent_dq, sent_dk, sent_dv = [swapped(value) for value in result[4:]]

    parts = 2
    width = HALF // parts
    half_spec = pl.BlockSpec((ROWS, width), lambda i, c, *_: (0, (1 - c[0]) * parts + i))

    def placed(after, got, into):
        count = len(got)
        return call(
            place_body, (after,), (*map(place_near, got), *into), [near] * count + [anywhere] * count, [half_spec] * count,
            [big] * count, grid=(parts,), aliases={1 + count + i: i for i in range(count)},
        )

    one, = near_call(group_sum_body, (got,), [(9, 16, 128)])
    one, sent_dq, sent_dk = lax.optimization_barrier((one, sent_dq, sent_dk))
    others = [lax.ppermute(one, "zh", [(z, z ^ s) for z in range(4)]) for s in (1, 2, 3)]
    sums, = near_call(spread_sum_body, (one, *others), [(GROUPS, 9, 16, 128)])
    sums, sent_att, sent_dq, sent_dk, sent_dv, after = lax.optimization_barrier(
        (sums, sent_att, sent_dq, sent_dk, sent_dv, scalars[0]))
    got = lax.all_to_all(sums, block, 0, 0, tiled=False)
    dq, dk, dv = placed(after, (sent_dq, sent_dk, sent_dv), (dq, dk, dv))
    sum_second, sum_first = pl.pallas_call(
        finish_body, in_specs=[near], out_specs=[anywhere, anywhere],
        out_shape=[struct((CH, HALF), F32), struct((32, CH), F32)],
        scratch_shapes=[pltpu.VMEM((CH, HALF), F32), pltpu.VMEM((32, CH), F32), pltpu.SemaphoreType.DMA((9,))],
        compiler_params=pltpu.CompilerParams(vmem_limit_bytes=VMEM),
    )(place_near(got))

    lay = call(
        merge_body, scalars, (r_rows, lat_own, lat_oth, w_first, w_second, place_near(sent_att), lay),
        [pl.BlockSpec((SPAN, width), lambda i, c, s: (1 - c[0], (1 - c[0]) * parts + i)), lat_spec, lat_spec,
         whole((32, CH)), pl.BlockSpec((CH, width), lambda i, c, s: (0, (1 - c[0]) * parts + i)),
         near, anywhere],
        half_spec, big, grid=(parts,), scratch=[pltpu.VMEM((SPAN, CH), BF16)], aliases={8: 0},
    )
    outs = (lay, dq, dk, dv)
    return (*[value[None] for value in outs], sum_first, sum_second)


def solution(mesh):
    axes = Mesh(mesh.devices.reshape(4, 2, 4, 4, 2), ("zh", "zl", "y", "x", "ctx"))
    dp = ("zh", "zl", "y", "x")
    rows = P(dp, "ctx", None)
    return jax.shard_map(
        local,
        mesh=axes,
        in_specs=(rows, rows, rows, rows, rows, P(dp, "ctx", None, None), P(dp, None), P(), P()),
        out_specs=(rows, rows, rows, rows, P(), P(None, "ctx")),
        check_vma=False,
    )
```

```python
import math

import jax
import jax.numpy as jnp
from jax import lax
from jax.experimental import pallas as pl
from jax.experimental.pallas import tpu as pltpu
from jax.sharding import Mesh
from jax.sharding import PartitionSpec as P

HEAD = 128
SPAN = 128
ROWS = 256
HALF = 1024
WIDTH = 2048
SEQ = 512
CH = 512
HEADS = 8
GROUP = 4
GROUPS = 32
VMEM = 56 * 1024 * 1024

F32 = jnp.float32
BF16 = jnp.bfloat16


def dot(a, b, ca, cb):
    return lax.dot_general(a, b, (((ca,), (cb,)), ((), ())), preferred_element_type=F32)


def whole(shape):
    return pl.BlockSpec(shape, lambda *_: (0,) * len(shape))


def call(body, scalars, args, in_specs, out_specs, out_shape, grid=(1,), scratch=(), aliases=None, cost=None):
    return pl.pallas_call(
        body,
        grid_spec=pltpu.PrefetchScalarGridSpec(
            num_scalar_prefetch=len(scalars),
            grid=grid,
            in_specs=in_specs,
            out_specs=out_specs,
            scratch_shapes=scratch,
        ),
        out_shape=out_shape,
        input_output_aliases=aliases or {},
        cost_estimate=cost,
        compiler_params=pltpu.CompilerParams(vmem_limit_bytes=VMEM),
    )(*scalars, *args)


def sigmoid(v):
    return 1.0 / (1.0 + jnp.exp(-v))


def eye(n):
    rows = lax.broadcasted_iota(jnp.int32, (n, n), 0)
    cols = lax.broadcasted_iota(jnp.int32, (n, n), 1)
    return (rows == cols).astype(F32).astype(BF16)


def pick(starts, lat_own, lat_oth):
    in_order = starts[0] == 0
    one, two = lat_own[...].astype(F32), lat_oth[...].astype(F32)
    return jnp.where(in_order, one, two).astype(BF16), jnp.where(in_order, two, one).astype(BF16)


def hidden_and_gate(w1, lat):
    pre = dot(w1, lat, 0, 0)
    sig = sigmoid(pre)
    return (pre * sig).astype(BF16), sig * (1.0 + pre * (1.0 - sig))


def hidden_body(ctx_ref, lat_hbm, w1_hbm, w2_hbm, g_own, lat, w1, hid_t, gate, w2, grads, sems):
    own_rows = pl.ds(pl.multiple_of(ctx_ref[0] * SPAN, SPAN), SPAN)
    copies = [
        pltpu.make_async_copy(source, target, sems.at[i])
        for i, (source, target) in enumerate((
            (lat_hbm, lat), (w1_hbm, w1), (g_own.at[own_rows, :], grads), (w2_hbm, w2)))
    ]
    for copy in copies:
        copy.start()
    copies[0].wait()
    copies[1].wait()
    hid_t[...], gate[...] = hidden_and_gate(w1[...], lat[...])
    copies[2].wait()
    copies[3].wait()


def weight_body(ctx_ref, starts, lat_own, w1, hid_own, gate_own, w2, g_own, lat_oth, g_oth, out, grads, tiles, sems):
    ctx = ctx_ref[0]
    oth_rows = pl.ds(pl.multiple_of(SPAN - ctx * SPAN, SPAN), SPAN)
    place = pl.multiple_of(jnp.where(starts[0] == 0, 0, SPAN), SPAN)
    grads[pl.ds(place, SPAN), :] = g_own[...]
    grads[pl.ds(pl.multiple_of(SPAN - place, SPAN), SPAN), :] = g_oth[oth_rows, :]
    hid_oth, gate_oth = hidden_and_gate(w1[...], lat_oth[...])
    hid_t = jnp.concatenate([hid_own[...], hid_oth], axis=1)
    gate = jnp.concatenate([gate_own[...], gate_oth], axis=1)
    patches = jnp.concatenate([lat_own[...], lat_oth[...]], axis=1)
    for n in range(4):
        half = grads[:, pl.ds(pl.multiple_of(ctx * HALF, HALF) + 256 * n, 256)]
        strip = dot(hid_t, half, 1, 0).astype(BF16)
        for j in range(GROUPS):
            for i in range(2):
                tiles[j, 2 * n + i] = strip[16 * j : 16 * j + 16, 128 * i : 128 * i + 128]
    main, rest = pl.ds(0, 8), pl.ds(8, 1)
    copies = [pltpu.make_async_copy(tiles.at[:, part], out.at[:, part], sems.at[i]) for i, part in enumerate((main, rest))]
    copies[0].start()
    back = dot(w2[...], grads[...], 1, 1)
    grad_pre = (back * gate).astype(BF16)
    first = dot(patches, grad_pre, 1, 1).astype(BF16)
    for j in range(GROUPS):
        m = j // 4
        tiles[j, 8] = first[16 * (m // 4) : 16 * (m // 4) + 16, 128 * (m % 4) : 128 * (m % 4) + 128]
    copies[1].start()
    copies[0].wait()
    copies[1].wait()


def group_sum_body(got, out):
    total = got[0].astype(F32)
    for j in range(1, GROUPS):
        total = total + got[j].astype(F32)
    out[...] = total.astype(BF16)


def spread_sum_body(one, next1, next2, next3, out, total, sems):
    even = one[...].astype(F32) + next2[...].astype(F32)
    odd = next1[...].astype(F32) + next3[...].astype(F32)
    total[...] = (even + odd).astype(BF16)
    copies = [pltpu.make_async_copy(total, out.at[j], sems.at[j]) for j in range(GROUPS)]
    for copy in copies:
        copy.start()
    for copy in copies:
        copy.wait()


def finish_body(got, second, first, second_near, first_near, sems):
    copies = []
    for n in range(8):
        for j in range(4 * n, 4 * n + 4):
            for t in range(8):
                second_near[16 * j : 16 * j + 16, 128 * t : 128 * t + 128] = got[j, t].astype(F32) * (1.0 / 128.0)
        part = pl.ds(64 * n, 64)
        copies.append(pltpu.make_async_copy(second_near.at[part, :], second.at[part, :], sems.at[n]))
        copies[-1].start()
    for m in range(8):
        rows, cols = 16 * (m // 4), 128 * (m % 4)
        first_near[rows : rows + 16, cols : cols + 128] = got[4 * m, 8].astype(F32) * (1.0 / 128.0)
    copies.append(pltpu.make_async_copy(first_near, first, sems.at[8]))
    copies[-1].start()
    for copy in copies:
        copy.wait()


def chain(q, k, v, g, att, dq, dk, dv, cols, b, unit, shared):
    scale = HEAD ** -0.5
    power = scale * math.log2(math.e)
    seen = ROWS * (b + 1)
    rows = slice(ROWS * b, ROWS * b + ROWS)
    qb = q[rows, cols]
    gb = g[rows, cols]
    scores = dot(k[0:seen, cols], qb, 1, 1)
    dp = dot(v[0:seen, cols], gb, 1, 1)
    if b == 1:
        shared["k_t"] = dot(unit, k[:, cols], 1, 1).astype(BF16)
        shared["v_t"] = dot(unit, v[:, cols], 1, 1).astype(BF16)
    yield
    key_pos = lax.broadcasted_iota(jnp.int32, (ROWS, ROWS), 0)
    query_pos = lax.broadcasted_iota(jnp.int32, (ROWS, ROWS), 1)
    if b == 0:
        limit = jnp.where(query_pos < SPAN, SPAN - 1, query_pos)
    else:
        limit = jnp.where(query_pos < SPAN, query_pos, ROWS - 1)
    last = jnp.where(key_pos <= limit, scores[seen - ROWS : seen], -1e30)
    scores = last if b == 0 else jnp.concatenate([scores[0:ROWS], last], axis=0)
    top = jnp.max(scores, axis=0, keepdims=True)
    yield
    e = jnp.exp2((scores - top) * power)
    total = jnp.sum(e, axis=0, keepdims=True)
    yield
    p = e * (1.0 / total)
    pb = p.astype(BF16)
    u = p * dp
    out_dot = jnp.sum(u, axis=0, keepdims=True)
    yield
    ds = (u - p * out_dot).astype(BF16)
    att_t = dot(shared["v_t"][:, 0:seen], pb, 1, 0)
    new_v = dot(pb, gb, 1, 0)
    yield
    dq_t = dot(shared["k_t"][:, 0:seen], ds, 1, 0) * scale
    new_k = dot(ds, qb, 1, 0)
    att[rows, cols] = jnp.transpose(att_t).astype(BF16)
    yield
    dq[rows, cols] = jnp.transpose(dq_t).astype(BF16)
    if b == 1:
        shared["dk"] = new_k[0:ROWS]
        shared["dv"] = new_v[0:ROWS]
    else:
        new_k = new_k + shared["dk"]
        new_v = new_v + shared["dv"]
    dk[rows, cols] = (new_k[seen - ROWS : seen] * scale).astype(BF16)
    dv[rows, cols] = new_v[seen - ROWS : seen].astype(BF16)


def hidden_of(lat, w1):
    pre = dot(lat, w1, 0, 0)
    return (pre * sigmoid(pre)).astype(BF16)


def attention_body(ctx_ref, starts, q_own, q_oth, k_own, k_oth, v_own, v_oth, g_own, g_oth, text, lat_own, lat_oth, w1, w2,
                   lay_out, dq_out, dk_out, dv_out, att_send, dq_send, dk_send, dv_send,
                   q, k, v, g, att, dq, dk, dv, hid):
    ctx = ctx_ref[0]
    own = pl.multiple_of(ctx * ROWS, ROWS)
    oth = pl.multiple_of(ROWS - ctx * ROWS, ROWS)

    @pl.when(pl.program_id(0) == 0)
    def _():
        hid[...] = hidden_of(pick(starts, lat_own, lat_oth)[0], w1[...])

    step = pl.program_id(0)
    there = pl.ds(pl.multiple_of(ctx * HALF + step * GROUP * HEAD, GROUP * HEAD), GROUP * HEAD)
    for full, a, b in ((q, q_own, q_oth), (k, k_own, k_oth), (v, v_own, v_oth), (g, g_own, g_oth)):
        full[pl.ds(own, ROWS), :] = a[...]
        full[pl.ds(oth, ROWS), :] = b[:, there]
    unit = eye(HEAD)
    waiting = []
    for h in range(GROUP):
        cols = slice(HEAD * h, HEAD * h + HEAD)
        shared = {}
        for b in (1, 0):
            waiting.append(chain(q, k, v, g, att, dq, dk, dv, cols, b, unit, shared))
    running = []
    while waiting or running:
        if waiting:
            running.append(waiting.pop(0))
        running = [item for item in running if next(item, "end") != "end"]
    mine = pl.ds(own, ROWS)
    theirs = pl.ds(oth, ROWS)
    for full, keep, send in ((dq, dq_out, dq_send), (dk, dk_out, dk_send), (dv, dv_out, dv_send)):
        keep[...] = full[mine, :]
        send[...] = full[theirs, :]
    att_send[...] = att[theirs, :]
    add_residual(ctx, lay_out, att[mine, :], hid[...], w2[...], text[...])


def add_residual(ctx, lay_out, att, hid, w2, text):
    lay_out[...] = att
    image_rows = pl.ds(pl.multiple_of(ctx * SPAN, SPAN), SPAN)
    text_rows = pl.ds(pl.multiple_of(SPAN - ctx * SPAN, SPAN), SPAN)
    embedding = dot(hid, w2, 1, 0).astype(BF16).astype(F32)
    lay_out[image_rows, :] = (embedding + lay_out[image_rows, :].astype(F32)).astype(BF16)
    lay_out[text_rows, :] = (text.astype(F32) + lay_out[text_rows, :].astype(F32)).astype(BF16)


def place_body(ctx_ref, *refs):
    count = len(refs) // 3
    width = refs[-1].shape[1]
    cols = pl.ds(pl.multiple_of(pl.program_id(0) * width, width), width)
    for i in range(count):
        refs[2 * count + i][...] = refs[i][:, cols]


def merge_body(ctx_ref, starts, text, lat_own, lat_oth, w1, w2, att, lay_in, lay_out, hid):
    @pl.when(pl.program_id(0) == 0)
    def _():
        hid[...] = hidden_of(pick(starts, lat_own, lat_oth)[0], w1[...])

    width = lay_out.shape[1]
    cols = pl.ds(pl.multiple_of(pl.program_id(0) * width, width), width)
    add_residual(ctx_ref[0], lay_out, att[:, cols], hid[...], w2[...], text[...])


def local(queries, keys, values, residual, grad_out, latents, image_starts, w_first, w_second):
    ctx = lax.axis_index("ctx").astype(jnp.int32)
    scalars = (ctx[None], image_starts.reshape(2))
    swap = [(0, 1), (1, 0)]

    def swapped(value):
        return lax.ppermute(value, "ctx", swap)

    q_rows, k_rows, v_rows, g_rows, r_rows = queries[0], keys[0], values[0], grad_out[0], residual[0]
    lat_own = latents[0, 0]
    lat_oth = swapped(lat_own)
    g_oth = swapped(g_rows)

    struct = jax.ShapeDtypeStruct
    anywhere = pl.BlockSpec(memory_space=pl.ANY)
    near = pl.BlockSpec(memory_space=pltpu.VMEM)

    def place_near(value):
        return pltpu.with_memory_space_constraint(value, pltpu.VMEM)

    def near_call(body, args, outs):
        return pl.pallas_call(
            body, in_specs=[near] * len(args), out_specs=[near] * len(outs),
            out_shape=[pltpu.VMEM(shape, BF16) for shape in outs],
        )(*[place_near(value) for value in args])

    lat_spec = whole((32, SPAN))
    ready = call(
        hidden_body, scalars[:1], (lat_own, w_first, w_second, g_rows), [anywhere] * 4, [near] * 6,
        [pltpu.VMEM((32, SPAN), BF16), pltpu.VMEM((32, CH), BF16), pltpu.VMEM((CH, SPAN), BF16), pltpu.VMEM((CH, SPAN), F32),
         pltpu.VMEM((CH, WIDTH), BF16), pltpu.VMEM((SPAN, WIDTH), BF16)],
        scratch=[pltpu.SemaphoreType.DMA((4,))],
        cost=pl.CostEstimate(flops=4_000_000_000, bytes_accessed=10_000_000, transcendentals=200_000),
    )
    lat_oth, g_oth, *rest = lax.optimization_barrier((lat_oth, g_oth, *ready, q_rows, k_rows, v_rows))
    ready, rows = rest[:6], rest[6:]
    q_oth, k_oth, v_oth = [swapped(value) for value in rows]
    payload = call(
        weight_body, scalars, [place_near(value) for value in (*ready, lat_oth, g_oth)],
        [near] * 8, anywhere, struct((GROUPS, 9, 16, 128), BF16),
        scratch=[pltpu.VMEM((ROWS, WIDTH), BF16), pltpu.VMEM((GROUPS, 9, 16, 128), BF16), pltpu.SemaphoreType.DMA((2,))],
    )
    block = ("zl", "y", "x")
    q_oth, k_oth, v_oth, g_oth = [place_near(value) for value in (q_oth, k_oth, v_oth, g_oth)]
    got = lax.all_to_all(payload, block, 0, 0, tiled=False)

    cols = GROUP * HEAD
    steps = HEADS // GROUP
    own_spec = pl.BlockSpec((ROWS, cols), lambda i, c, s: (0, c[0] * steps + i))
    send_spec = pl.BlockSpec((ROWS, cols), lambda i, c, s: (0, i))
    big = struct((ROWS, WIDTH), BF16)
    small = struct((ROWS, HALF), BF16)
    result = call(
        attention_body, scalars,
        (q_rows, q_oth, k_rows, k_oth, v_rows, v_oth, g_rows, g_oth, r_rows, lat_own, lat_oth, w_first, w_second),
        [own_spec, near] * 4
        + [pl.BlockSpec((SPAN, cols), lambda i, c, s: (1 - c[0], c[0] * steps + i)),
           lat_spec, lat_spec, whole((32, CH)), pl.BlockSpec((CH, cols), lambda i, c, s: (0, c[0] * steps + i))],
        [own_spec] * 4 + [send_spec] * 4,
        [big] * 4 + [small] * 4,
        grid=(steps,),
        scratch=[pltpu.VMEM((SEQ, cols), BF16)] * 8 + [pltpu.VMEM((SPAN, CH), BF16)],
        cost=pl.CostEstimate(flops=40_000_000_000, bytes_accessed=100_000_000, transcendentals=4_000_000),
    )
    lay, dq, dk, dv = result[:4]
    sent_att, sent_dq, sent_dk, sent_dv = [swapped(value) for value in result[4:]]

    parts = 2
    width = HALF // parts
    half_spec = pl.BlockSpec((ROWS, width), lambda i, c, *_: (0, (1 - c[0]) * parts + i))

    def placed(after, got, into):
        count = len(got)
        return call(
            place_body, (after,), (*map(place_near, got), *into), [near] * count + [anywhere] * count, [half_spec] * count,
            [big] * count, grid=(parts,), aliases={1 + count + i: i for i in range(count)},
        )

    one, = near_call(group_sum_body, (got,), [(9, 16, 128)])
    one, after = lax.optimization_barrier((one, scalars[0]))
    others = [lax.ppermute(one, "zh", [(z, (z + s) % 4) for z in range(4)]) for s in (1, 2, 3)]
    dq, dk, dv = placed(after, (sent_dq, sent_dk, sent_dv), (dq, dk, dv))
    *others, dq, dk, dv = lax.optimization_barrier((*others, dq, dk, dv))
    sums = pl.pallas_call(
        spread_sum_body, in_specs=[near] * 4, out_specs=anywhere, out_shape=struct((GROUPS, 9, 16, 128), BF16),
        scratch_shapes=[pltpu.VMEM((9, 16, 128), BF16), pltpu.SemaphoreType.DMA((GROUPS,))],
    )(*[place_near(value) for value in (one, *others)])
    sums, sent_att = lax.optimization_barrier((sums, sent_att))
    got = lax.all_to_all(sums, block, 0, 0, tiled=False)
    sum_second, sum_first = pl.pallas_call(
        finish_body, in_specs=[near], out_specs=[anywhere, anywhere],
        out_shape=[struct((CH, HALF), F32), struct((32, CH), F32)],
        scratch_shapes=[pltpu.VMEM((CH, HALF), F32), pltpu.VMEM((32, CH), F32), pltpu.SemaphoreType.DMA((9,))],
        compiler_params=pltpu.CompilerParams(vmem_limit_bytes=VMEM),
    )(place_near(got))

    lay = call(
        merge_body, scalars, (r_rows, lat_own, lat_oth, w_first, w_second, place_near(sent_att), lay),
        [pl.BlockSpec((SPAN, width), lambda i, c, s: (1 - c[0], (1 - c[0]) * parts + i)), lat_spec, lat_spec,
         whole((32, CH)), pl.BlockSpec((CH, width), lambda i, c, s: (0, (1 - c[0]) * parts + i)),
         near, anywhere],
        half_spec, big, grid=(parts,), scratch=[pltpu.VMEM((SPAN, CH), BF16)], aliases={8: 0},
    )
    outs = (lay, dq, dk, dv)
    return (*[value[None] for value in outs], sum_first, sum_second)


def solution(mesh):
    axes = Mesh(mesh.devices.reshape(4, 2, 4, 4, 2), ("zh", "zl", "y", "x", "ctx"))
    dp = ("zh", "zl", "y", "x")
    rows = P(dp, "ctx", None)
    return jax.shard_map(
        local,
        mesh=axes,
        in_specs=(rows, rows, rows, rows, rows, P(dp, "ctx", None, None), P(dp, None), P(), P()),
        out_specs=(rows, rows, rows, rows, P(), P(None, "ctx")),
        check_vma=False,
    )
```
